32 devices in a mesh: seq: 8 (over z, x), batch: 4 (over y, core).
Axes of the slice: x: 2, y: 2, z: 4, core: 2. Of those that a mesh axis runs over, the one named last changes fastest.
Arguments:
- inputs: bfloat16 [4, 1024, 768], P('batch', 'seq'), may hold values from -6 to 6
- cotangent: bfloat16 [4, 1024, 768], P('batch', 'seq'), may hold values from -6 to 6
- doc_lengths: int32 [4, 9], P('batch'), may hold values from 1 to 896, as said below
- gain_one: float32 [768], replicated, may hold values from 0.5 to 1.5
- shift_one: float32 [768], replicated, may hold values from -2 to 2
- qkv_weight: bfloat16 [768, 2304], replicated, may hold values from -0.21875 to 0.21875
- qkv_bias: float32 [2304], replicated, may hold values from -2 to 2
- proj_weight: bfloat16 [768, 768], replicated, may hold values from -6 to 6
- proj_bias: float32 [768], replicated, may hold values from -2 to 2
- gain_two: float32 [768], replicated, may hold values from 0.5 to 1.5
- shift_two: float32 [768], replicated, may hold values from -2 to 2
- up_weight: bfloat16 [768, 3072], replicated, may hold values from -0.21875 to 0.21875
- up_bias: float32 [3072], replicated, may hold values from -2 to 2
- down_weight: bfloat16 [3072, 768], replicated, may hold values from -0.109375 to 0.109375
- down_bias: float32 [768], replicated, may hold values from -2 to 2
Outputs:
- layer_out: bfloat16 [4, 1024, 768], P('batch', 'seq')
- input_grad: bfloat16 [4, 1024, 768], P('batch', 'seq')
- grad_gain_one: float32 [768], replicated
- grad_shift_one: float32 [768], replicated
- grad_qkv_weight: float32 [768, 2304], replicated
- grad_qkv_bias: float32 [2304], replicated
- grad_proj_weight: float32 [768, 768], replicated
- grad_proj_bias: float32 [768], replicated
- grad_gain_two: float32 [768], replicated
- grad_shift_two: float32 [768], replicated
- grad_up_weight: float32 [768, 3072], replicated
- grad_up_bias: float32 [3072], replicated
- grad_down_weight: float32 [3072, 768], replicated
- grad_down_bias: float32 [768], replicated
The draws below stay inside these ranges and needn't reach their ends.
Inputs may be any that keep to these rules, and one draw needn't show every extreme that they name: `doc_lengths`: each row lists in order the lengths of the 9 documents packed into one stream: 8 short ones that hold 128 tokens together, and one of exactly 896 tokens with at least one short document before it and one after it.
All inputs are finite; a program needn't handle non-finite values.
Results may differ from the reference program's by a relative error of at most 0.018.
Values may be sent and summed in bfloat16 or wider, within the bound.
A program may use at most 256 MiB of HBM per device.

```python
import math
import jax
import jax.numpy as jnp
from jax import lax

HEADS = 12
HD = 64
FF = 3072
TOK_DEV = 128
SMALL_DOCS = 8
D = 768
STREAMS = 4
STREAM = 1024
DOCS = 9


def one_stream(key):
    first_key, second_key = jax.random.split(key, 2)
    places = jnp.arange(1, TOK_DEV, dtype=jnp.int32)
    scores = jax.random.randint(first_key, (TOK_DEV - 1,), 0, 1 << 20, dtype=jnp.int32)
    ranked = scores * TOK_DEV + places
    picked = lax.top_k(ranked, SMALL_DOCS - 1)[1]
    cuts = jnp.sort(places[picked])
    bounds = jnp.concatenate([jnp.zeros((1,), jnp.int32), cuts, jnp.full((1,), TOK_DEV, jnp.int32)])
    small = (bounds[1:] - bounds[:-1]).astype(jnp.int32)
    before_count = jax.random.randint(second_key, (), 1, SMALL_DOCS, dtype=jnp.int32)
    slots = jnp.arange(DOCS, dtype=jnp.int32)
    early = small[jnp.minimum(slots, SMALL_DOCS - 1)]
    late = small[jnp.clip(slots - 1, 0, SMALL_DOCS - 1)]
    big = jnp.full((DOCS,), STREAM - TOK_DEV, jnp.int32)
    return jnp.where(slots < before_count, early, jnp.where(slots == before_count, big, late)).astype(jnp.int32)


def draw_doc_lengths(key, part):
    stream_keys = jax.random.split(jax.random.fold_in(key, 17), STREAMS)
    return jax.vmap(one_stream)(stream_keys)


def steps_of(rng, dims, shards, smallest, top_value):
    factor_of = 1.0
    for position, shards_of in shards:
        heights = jax.random.uniform(jax.random.fold_in(jax.random.fold_in(rng, 6), position), (shards_of,), jnp.float32, smallest / len(shards), top_value / len(shards))
        factor_of = factor_of * jnp.repeat(jnp.exp(heights), dims[position] // shards_of).reshape((-1,) + (1,) * (len(dims) - 1 - position))
    return factor_of


def scatter_about(own_key, extent, scale, most, shards=(), kind=jnp.bfloat16):
    entries = scale * jax.random.normal(own_key, extent, jnp.float32)
    if shards:
        entries = entries * steps_of(own_key, extent, shards, -0.22, 0.18)
    return jnp.clip(entries, -most, most).astype(kind)


def setup_inputs(seed: int = 0) -> dict:
    streams_of = jax.random.split(jax.random.key(seed), 16)
    return {
        "inputs": scatter_about(streams_of[0], (STREAMS, STREAM, D), 1.0, 6.0, ((0, 4), (1, 8))),
        "cotangent": scatter_about(streams_of[1], (STREAMS, STREAM, D), 1.0, 6.0, ((0, 4), (1, 8))),
        "doc_lengths": draw_doc_lengths(jax.random.fold_in(streams_of[15], 71), 0),
        "gain_one": jnp.clip(1.0 + 0.1 * jax.random.normal(streams_of[3], (D,), jnp.float32), 0.5, 1.5),
        "shift_one": scatter_about(streams_of[4], (D,), 0.3, 2.0, (), jnp.float32),
        "qkv_weight": scatter_about(streams_of[5], (D, 3 * D), D ** -0.5, 0.21875),
        "qkv_bias": scatter_about(streams_of[6], (3 * D,), 0.3, 2.0, (), jnp.float32),
        "proj_weight": scatter_about(streams_of[7], (D, D), 1 ** -0.5, 6.0),
        "proj_bias": scatter_about(streams_of[8], (D,), 0.3, 2.0, (), jnp.float32),
        "gain_two": jnp.clip(1.0 + 0.1 * jax.random.normal(streams_of[9], (D,), jnp.float32), 0.5, 1.5),
        "shift_two": scatter_about(streams_of[10], (D,), 0.3, 2.0, (), jnp.float32),
        "up_weight": scatter_about(streams_of[11], (D, FF), D ** -0.5, 0.21875),
        "up_bias": scatter_about(streams_of[12], (FF,), 0.3, 2.0, (), jnp.float32),
        "down_weight": scatter_about(streams_of[13], (FF, D), FF ** -0.5, 0.109375),
        "down_bias": scatter_about(streams_of[14], (D,), 0.3, 2.0, (), jnp.float32),
    }


precise = lax.Precision.HIGHEST

@jax.custom_vjp
def low(v):
    return lax.optimization_barrier(v.astype(jnp.bfloat16)).astype(jnp.float32)

@jax.custom_vjp
def low_back(v):
    return v

def low_keep(v):
    return (low(v), None)

def low_pass(kept, grad):
    return (grad,)

def back_keep(v):
    return (v, None)

def back_low(kept, grad):
    return (low(grad),)
low.defvjp(low_keep, low_pass)
low_back.defvjp(back_keep, back_low)

def layer_norm(rows, gain, shift):
    center = rows - lax.optimization_barrier(jnp.mean(rows, axis=-1, keepdims=True))
    spread = lax.optimization_barrier(jnp.mean(center * center, axis=-1, keepdims=True))
    return center * lax.rsqrt(spread + 1e-05) * gain + shift

def gelu_tanh(value):
    return jax.nn.gelu(value, approximate=True)

def document_ids(doc_lengths, length):
    ends = jnp.cumsum(doc_lengths, axis=-1).astype(jnp.int32)
    places = jnp.arange(length, dtype=jnp.int32)
    return lax.optimization_barrier(jnp.sum((ends[:, None, :] <= places[None, :, None]).astype(jnp.int32), axis=-1)).astype(jnp.int32)

def attend(queries, keys, values, docids):
    streams, length, width = queries.shape
    blocks = length // TOK_DEV
    scale = 1.0 / math.sqrt(HD)
    key_places = jnp.arange(length, dtype=jnp.int32)

    def one_block(index):
        stream = (index // blocks).astype(jnp.int32)
        start = (index % blocks * TOK_DEV).astype(jnp.int32)
        zero = jnp.zeros((), jnp.int32)
        q_blk = lax.dynamic_slice(queries, (stream, start, zero), (1, TOK_DEV, width))[0].reshape(TOK_DEV, HEADS, HD)
        k_all = lax.dynamic_slice(keys, (stream, zero, zero), (1, length, width))[0].reshape(length, HEADS, HD)
        v_all = lax.dynamic_slice(values, (stream, zero, zero), (1, length, width))[0].reshape(length, HEADS, HD)
        q_doc = lax.dynamic_slice(docids, (stream, start), (1, TOK_DEV))[0]
        k_doc = lax.dynamic_slice(docids, (stream, zero), (1, length))[0]
        q_places = start + jnp.arange(TOK_DEV, dtype=jnp.int32)
        allowed = (q_doc[:, None] == k_doc[None, :]) & (key_places[None, :] <= q_places[:, None])
        raw = low_back(jnp.einsum('qhd,khd->hqk', q_blk, k_all, precision=precise))
        scores = jnp.where(allowed[None], raw * scale, 0.0)
        top = lax.optimization_barrier(jnp.max(jnp.where(allowed[None], jnp.abs(scores), -1e+30), axis=2, keepdims=True))
        plus = jnp.where(allowed[None], jnp.exp(scores - top), 0.0)
        minus = jnp.where(allowed[None], jnp.exp(-scores - top), 0.0)
        total = lax.optimization_barrier(jnp.sum(plus + minus, axis=2, keepdims=True))
        weights = low((plus - minus) / total)
        out = jnp.einsum('hqk,khd->qhd', weights, v_all, precision=precise)
        return out.reshape(TOK_DEV, width)
    outs = lax.map(jax.checkpoint(one_block), jnp.arange(streams * blocks, dtype=jnp.int32))
    return outs.reshape(streams, length, width)

def forward(inputs, gain_one, shift_one, qkv_weight, qkv_bias, proj_weight, proj_bias, gain_two, shift_two, up_weight, up_bias, down_weight, down_bias, docids):
    width = inputs.shape[-1]
    norm_one = low(layer_norm(inputs, gain_one, shift_one))
    mixed = jnp.einsum('bsd,de->bse', norm_one, qkv_weight, precision=precise) + qkv_bias
    mixed = low(low_back(mixed))
    attn32 = attend(mixed[..., :width], mixed[..., width:2 * width], mixed[..., 2 * width:], docids)
    attn = low(low_back(attn32))
    branch = low_back(jnp.einsum('bsd,de->bse', attn, proj_weight, precision=precise) + proj_bias)
    resid = inputs + branch
    norm_two = low(layer_norm(resid, gain_two, shift_two))
    hidden = low_back(jnp.einsum('bsd,df->bsf', norm_two, up_weight, precision=precise) + up_bias)
    active = low(gelu_tanh(hidden))
    return resid + jnp.einsum('bsf,fd->bsd', active, down_weight, precision=precise) + down_bias

def reference(inputs, cotangent, doc_lengths, gain_one, shift_one, qkv_weight, qkv_bias, proj_weight, proj_bias, gain_two, shift_two, up_weight, up_bias, down_weight, down_bias):
    docids = document_ids(doc_lengths, inputs.shape[1])

    def run(x_in, g_one, s_one, w_qkv, b_qkv, w_proj, b_proj, g_two, s_two, w_up, b_up, w_down, b_down):
        return forward(x_in, g_one, s_one, w_qkv, b_qkv, w_proj, b_proj, g_two, s_two, w_up, b_up, w_down, b_down, docids)
    result, pull = jax.vjp(run, inputs.astype(jnp.float32), gain_one.astype(jnp.float32), shift_one.astype(jnp.float32), qkv_weight.astype(jnp.float32), qkv_bias.astype(jnp.float32), proj_weight.astype(jnp.float32), proj_bias.astype(jnp.float32), gain_two.astype(jnp.float32), shift_two.astype(jnp.float32), up_weight.astype(jnp.float32), up_bias.astype(jnp.float32), down_weight.astype(jnp.float32), down_bias.astype(jnp.float32))
    grads = pull(cotangent.astype(jnp.float32))
    return (result.astype(jnp.bfloat16), grads[0].astype(jnp.bfloat16), grads[1], grads[2], grads[3], grads[4], grads[5], grads[6], grads[7], grads[8], grads[9], grads[10], grads[11], grads[12])
```

```python
import functools
import math

import jax
import jax.numpy as jnp
from jax import lax
from jax.experimental import pallas as pl
from jax.experimental.pallas import tpu as pltpu
from jax.sharding import PartitionSpec as P

HEADS = 12
HD = 64


norm_eps = 1e-05
masked_low = -1e30


MESH_ID = pl.DeviceIdType.MESH
TILE = 16


def running_sum(lengths):
    places = jnp.arange(lengths.shape[0], dtype=jnp.int32)
    return jnp.sum(jnp.where(places[None, :] <= places[:, None], lengths[None, :], 0), axis=1)


class Place:
    def __init__(self):
        self.seq = lax.axis_index("seq")
        self.batch = lax.axis_index("batch")

    def bit(self, axis):
        name, k = axis
        return ((self.seq if name == "seq" else self.batch) // (1 << k)) % 2

    def partner(self, axis):
        name, k = axis
        step = (1 << k) * (1 - 2 * self.bit(axis))
        if name == "seq":
            return (self.seq + step, self.batch)
        return (self.seq, self.batch + step)


CORE = ("batch", 0)
ACROSS = ("batch", 1)


def seq_axes(peers):
    return [("seq", k) for k in range((peers - 1).bit_length())]


def axis_orders(peers):
    bits = seq_axes(peers)
    return [[bits[0], ACROSS] + bits[1:], [ACROSS] + bits, bits[1:] + [bits[0], ACROSS]]


def parts_of(rows, stages):
    found = []
    for _ in range(stages):
        halve = (rows // 2) % TILE == 0
        rows = rows // 2 if halve else rows
        found.append((rows, halve))
    return found


class Sems:
    def __init__(self, send, recv):
        self.send, self.recv, self.count = send, recv, 0

    def take(self):
        k = self.count
        self.count += 1
        return self.send.at[k], self.recv.at[k]


def rows_at(start, size):
    return pl.ds(pl.multiple_of(start, TILE), size)


def add_rows(into, one, at, other, other_at, rows):
    step = 32 if rows % 32 == 0 else TILE

    def body(i, carry):
        here = rows_at(at + i * step, step)
        there = rows_at(other_at + i * step, step)
        both = one[here].astype(jnp.float32) + other[there].astype(jnp.float32)
        into[here] = both.astype(into.dtype)
        return carry

    lax.fori_loop(0, rows // step, body, 0)


def sum_item(place, sems, buf, at, rows, order, inbox, used, total):
    low, plan = at, []
    for k, (axis, (part, halve)) in enumerate(zip(order, parts_of(rows, len(order)))):
        bit = place.bit(axis)
        keep, give = (low + bit * part, low + (1 - bit) * part) if halve else (low, low)
        copy = pltpu.make_async_remote_copy(
            buf.at[rows_at(give, part)],
            inbox.at[rows_at(used, part)],
            *sems.take(),
            device_id=place.partner(axis),
            device_id_type=MESH_ID,
        )
        copy.start()
        yield
        copy.wait()
        add_rows(total if k == len(order) - 1 else buf, buf, keep, inbox, used, part)
        plan.append((axis, keep, part, halve))
        used += part
        low = keep
    for axis, keep, part, halve in reversed(plan):
        if halve:
            here = rows_at(keep, part)
            copy = pltpu.make_async_remote_copy(
                total.at[here],
                total.at[here],
                *sems.take(),
                device_id=place.partner(axis),
                device_id_type=MESH_ID,
            )
            copy.start()
            yield
            copy.wait()


def take_turns(tasks, enter):
    live, waiting = [], list(tasks)
    while live or waiting:
        live, waiting = live + waiting[:enter], waiting[enter:]
        still = []
        for task in live:
            try:
                next(task)
                still.append(task)
            except StopIteration:
                pass
        live = still


def sum_kernel(items, orders, small_axes, grads, small, out, small_out, buf, inbox, near, small_in, ssem, rsem, lsem):
    place = Place()
    sems = Sems(ssem, rsem)
    barrier = pltpu.get_barrier_semaphore()
    for axis in small_axes:
        pl.semaphore_signal(barrier, inc=1, device_id=place.partner(axis), device_id_type=MESH_ID)
    pl.semaphore_wait(barrier, len(small_axes))
    half = buf.shape[0]
    core = place.bit(CORE)
    small_out[...] = small[...]

    def small_task():
        for k, axis in enumerate(small_axes):
            copy = pltpu.make_async_remote_copy(
                small_out,
                small_in.at[k],
                *sems.take(),
                device_id=place.partner(axis),
                device_id_type=MESH_ID,
            )
            copy.start()
            yield
            copy.wait()
            small_out[...] += small_in[k]

    def item_task(k, at, rows, order, used):
        mine = pltpu.make_async_copy(
            grads.at[rows_at(core * half + at, rows)], buf.at[rows_at(at, rows)], lsem.at[2 * k]
        )
        other = pltpu.make_async_remote_copy(
            grads.at[rows_at((1 - core) * half + at, rows)],
            near.at[rows_at(at, rows)],
            *sems.take(),
            device_id=place.partner(CORE),
            device_id_type=MESH_ID,
        )
        mine.start()
        other.start()
        yield
        mine.wait()
        other.wait()
        add_rows(buf, buf, at, near, at, rows)
        yield from sum_item(place, sems, buf, at, rows, order, inbox, used, near)
        there = out.at[rows_at(core * half + at, rows)]
        keep = pltpu.make_async_copy(near.at[rows_at(at, rows)], there, lsem.at[2 * k + 1])
        give = pltpu.make_async_remote_copy(
            near.at[rows_at(at, rows)],
            there,
            *sems.take(),
            device_id=place.partner(CORE),
            device_id_type=MESH_ID,
        )
        keep.start()
        give.start()
        yield
        keep.wait()
        give.wait()

    tasks, at, used = [], 0, 0
    for k, (rows, kind) in enumerate(items):
        tasks.append(item_task(k, at, rows, orders[kind], used))
        at += rows
        used += sum(part for part, _ in parts_of(rows, len(orders[kind])))
    take_turns(tasks[:3] + [small_task()] + tasks[3:], 3)


def sum_over_devices(grads, small, peers):
    half = grads.shape[0] // 2
    width = grads.shape[1]
    orders = axis_orders(peers)
    small_axes = [CORE, ACROSS] + seq_axes(peers)
    unit = 256
    items = [(unit, k % 3) for k in range(half // unit)]
    counts = [parts_of(rows, len(orders[kind])) for rows, kind in items]
    used = sum(part for count in counts for part, _ in count)
    copies = sum(3 + 2 * len(count) for count in counts) + len(small_axes)
    return pl.pallas_call(
        functools.partial(sum_kernel, items, orders, small_axes),
        out_shape=(
            jax.ShapeDtypeStruct(grads.shape, jnp.bfloat16),
            jax.ShapeDtypeStruct(small.shape, jnp.float32),
        ),
        in_specs=[pl.BlockSpec(memory_space=pl.ANY), pl.BlockSpec(memory_space=pltpu.VMEM)],
        out_specs=(pl.BlockSpec(memory_space=pl.ANY), pl.BlockSpec(memory_space=pltpu.VMEM)),
        scratch_shapes=[
            pltpu.VMEM((half, width), jnp.bfloat16),
            pltpu.VMEM((used, width), jnp.bfloat16),
            pltpu.VMEM((half, width), jnp.bfloat16),
            pltpu.VMEM((len(small_axes),) + small.shape, jnp.float32),
            pltpu.SemaphoreType.DMA((copies,)),
            pltpu.SemaphoreType.DMA((copies,)),
            pltpu.SemaphoreType.DMA((2 * len(items),)),
        ],
        compiler_params=pltpu.CompilerParams(
            collective_id=1, has_side_effects=True, vmem_limit_bytes=56 * 2**20
        ),
    )(grads, small)


def from_behind(shard, axis, by):
    peers = lax.axis_size(axis)
    pairs = [(i, i + by) for i in range(peers) if 0 <= i + by < peers]
    return lax.ppermute(shard, axis, pairs)


def shifted(block, axis, distance):
    devices = range(lax.axis_size(axis))
    route = [((i - distance) % len(devices), i) for i in devices]
    return lax.ppermute(block, axis, route)


def layer_norm(rows, gain, shift):
    center = rows - jnp.mean(rows, axis=-1, keepdims=True)
    spread = jnp.mean(center * center, axis=-1, keepdims=True)
    return center * lax.rsqrt(spread + norm_eps) * gain + shift


def gelu_tanh(value):
    return jax.nn.gelu(value, approximate=True)


def doc_of(ends, first, count):
    places = first + jnp.arange(count, dtype=jnp.int32)
    return jnp.sum((ends[None, :] <= places[:, None]).astype(jnp.int32), axis=1)


def scores_of(q_heads, k_heads, allowed):
    raw = jnp.einsum("qhd,khd->hqk", q_heads, k_heads, preferred_element_type=jnp.float32)
    return jnp.where(allowed[None], raw * (1.0 / math.sqrt(q_heads.shape[2])), 0.0)


def forward_part(state, q_heads, k_heads, v_heads, allowed):
    running, total, accum = state
    scores = scores_of(q_heads, k_heads, allowed)
    top = jnp.max(jnp.where(allowed[None], jnp.abs(scores), masked_low), axis=2)
    newer = jnp.maximum(running, top)
    plus = jnp.where(allowed[None], jnp.exp(scores - newer[:, :, None]), 0.0)
    minus = jnp.where(allowed[None], jnp.exp(-scores - newer[:, :, None]), 0.0)
    keep = jnp.exp(running - newer)
    total = total * keep + jnp.sum(plus + minus, axis=2)
    weights = (plus - minus).astype(jnp.bfloat16)
    accum = accum * keep[:, :, None] + jnp.einsum(
        "hqk,khd->hqd", weights, v_heads, preferred_element_type=jnp.float32
    )
    return (newer, total, accum)


def backward_part(q_heads, k_heads, v_heads, grad_out, log_total, delta, allowed):
    scale = 1.0 / math.sqrt(q_heads.shape[2])
    scores = scores_of(q_heads, k_heads, allowed)
    plus = jnp.where(allowed[None], jnp.exp(scores - log_total[:, :, None]), 0.0)
    minus = jnp.where(allowed[None], jnp.exp(-scores - log_total[:, :, None]), 0.0)
    signed = plus - minus
    along = jnp.einsum("qhd,khd->hqk", grad_out, v_heads, preferred_element_type=jnp.float32)
    dscore = (((plus + minus) * along - signed * delta[:, :, None]) * scale).astype(jnp.bfloat16)
    weights = signed.astype(jnp.bfloat16)
    grad_q = jnp.einsum("hqk,khd->qhd", dscore, k_heads, preferred_element_type=jnp.float32)
    grad_k = jnp.einsum("hqk,qhd->khd", dscore, q_heads, preferred_element_type=jnp.float32)
    grad_v = jnp.einsum("hqk,qhd->khd", weights, grad_out, preferred_element_type=jnp.float32)
    return (grad_q, grad_k, grad_v)


def forward_step(state, q_heads, k_heads, v_heads, allowed):
    return forward_part(state, q_heads, k_heads, v_heads, allowed)


def backward_step(q_heads, k_heads, v_heads, grad_out, log_total, delta, allowed):
    return backward_part(q_heads, k_heads, v_heads, grad_out, log_total, delta, allowed)


def per_device(
    inputs,
    cotangent,
    doc_lengths,
    gain_one,
    shift_one,
    qkv_weight,
    qkv_bias,
    proj_weight,
    proj_bias,
    gain_two,
    shift_two,
    up_weight,
    up_bias,
    down_weight,
    down_bias,
):
    rows = inputs.shape[1]
    width = inputs.shape[2]
    index = lax.axis_index("seq")
    count = lax.axis_size("seq")
    ends = running_sum(doc_lengths[0])
    q_place = index * rows + jnp.arange(rows, dtype=jnp.int32)
    q_doc = doc_of(ends, index * rows, rows)

    def heads(flat):
        return flat.reshape(flat.shape[0], HEADS, HD)

    x_rows = inputs[0].astype(jnp.float32)
    norm_one = layer_norm(x_rows, gain_one, shift_one).astype(jnp.bfloat16)
    mixed = (jnp.dot(norm_one, qkv_weight, preferred_element_type=jnp.float32) + qkv_bias).astype(
        jnp.bfloat16
    )
    q_flat = mixed[:, :width]
    k_flat = mixed[:, width : 2 * width]
    v_flat = mixed[:, 2 * width :]
    q_heads = heads(q_flat)

    def allowed_for(first, extent):
        k_place = first + jnp.arange(extent, dtype=jnp.int32)
        k_doc = doc_of(ends, first, extent)
        return (q_doc[:, None] == k_doc[None, :]) & (k_place[None, :] <= q_place[:, None])

    start_state = (
        jnp.full((HEADS, rows), masked_low, jnp.float32),
        jnp.zeros((HEADS, rows), jnp.float32),
        jnp.zeros((HEADS, rows, HD), jnp.float32),
    )
    state = start_state
    k_all = lax.all_gather(k_flat, "seq", axis=0, tiled=True)
    v_all = lax.all_gather(v_flat, "seq", axis=0, tiled=True)
    fold_extent = k_all.shape[0]
    number = fold_extent // rows

    def one(inner, block):
        offset = block * rows
        k_blk = lax.dynamic_slice_in_dim(k_all, offset, rows, 0)
        v_blk = lax.dynamic_slice_in_dim(v_all, offset, rows, 0)
        allowed = allowed_for(offset, rows)
        return (forward_step(inner, q_heads, heads(k_blk), heads(v_blk), allowed), None)

    state, unused = lax.scan(one, state, jnp.arange(number, dtype=jnp.int32))
    running, total, accum = state
    attn_heads = accum / total[:, :, None]
    attn32 = jnp.transpose(attn_heads, (1, 0, 2)).reshape(rows, width)
    attn = attn32.astype(jnp.bfloat16)
    resid = x_rows + jnp.dot(attn, proj_weight, preferred_element_type=jnp.float32) + proj_bias
    norm_two = layer_norm(resid, gain_two, shift_two).astype(jnp.bfloat16)
    hidden = jnp.dot(norm_two, up_weight, preferred_element_type=jnp.float32) + up_bias
    active = gelu_tanh(hidden).astype(jnp.bfloat16)
    result = resid + jnp.dot(active, down_weight, preferred_element_type=jnp.float32) + down_bias
    layer_out = result.astype(jnp.bfloat16)[None]
    grad_rows = cotangent[0]
    grad_down_weight = jnp.einsum(
        "tf,td->fd", active, grad_rows, preferred_element_type=jnp.float32
    )
    grad_down_bias = jnp.sum(grad_rows.astype(jnp.float32), axis=0)
    grad_active = jnp.dot(grad_rows, down_weight.T, preferred_element_type=jnp.float32)
    gelu_back = jax.vjp(gelu_tanh, hidden)[1]
    grad_hidden = gelu_back(grad_active)[0].astype(jnp.bfloat16)
    grad_up_weight = jnp.einsum(
        "td,tf->df", norm_two, grad_hidden, preferred_element_type=jnp.float32
    )
    grad_up_bias = jnp.sum(grad_hidden.astype(jnp.float32), axis=0)
    grad_norm_two = jnp.dot(grad_hidden, up_weight.T, preferred_element_type=jnp.float32)
    norm_two_back = jax.vjp(layer_norm, resid, gain_two, shift_two)[1]
    resid_part, grad_gain_two, grad_shift_two = norm_two_back(grad_norm_two)
    grad_resid = grad_rows.astype(jnp.float32) + resid_part
    grad_branch = grad_resid.astype(jnp.bfloat16)
    grad_proj_weight = jnp.einsum(
        "td,te->de", attn, grad_branch, preferred_element_type=jnp.float32
    )
    grad_proj_bias = jnp.sum(grad_branch.astype(jnp.float32), axis=0)
    grad_attn = jnp.dot(grad_branch, proj_weight.T, preferred_element_type=jnp.float32).astype(
        jnp.bfloat16
    )
    grad_out = heads(grad_attn)
    log_total = running + jnp.log(total)
    delta = jnp.einsum("qhd,hqd->hq", grad_out.astype(jnp.float32), attn_heads)

    def circle_step(step, carry):
        k_held, v_held, acc_k, acc_v, grad_q = carry
        source = jnp.remainder(index - step, count)
        allowed = allowed_for(source * rows, rows)
        part = backward_step(
            q_heads, heads(k_held), heads(v_held), grad_out, log_total, delta, allowed
        )
        grad_q = grad_q + part[0]
        acc_k = acc_k + part[1].reshape(rows, width)
        acc_v = acc_v + part[2].reshape(rows, width)
        k_held, v_held = from_behind((k_held, v_held), "seq", 1)
        acc_k, acc_v = (
            shifted(acc_k.astype(jnp.bfloat16), "seq", 1).astype(acc_k.dtype),
            shifted(acc_v.astype(jnp.bfloat16), "seq", 1).astype(acc_v.dtype),
        )
        return (k_held, v_held, acc_k, acc_v, grad_q)

    circle_start = (
        k_flat,
        v_flat,
        jnp.zeros((rows, width), jnp.float32),
        jnp.zeros((rows, width), jnp.float32),
        jnp.zeros((rows, HEADS, HD), jnp.float32),
    )
    unused_k, unused_v, grad_k, grad_v, grad_q = lax.fori_loop(0, count, circle_step, circle_start)
    grad_mixed = jnp.concatenate(
        [
            grad_q.reshape(rows, width).astype(jnp.bfloat16),
            grad_k.astype(jnp.bfloat16),
            grad_v.astype(jnp.bfloat16),
        ],
        axis=1,
    )
    grad_qkv_weight = jnp.einsum(
        "td,te->de", norm_one, grad_mixed, preferred_element_type=jnp.float32
    )
    grad_qkv_bias = jnp.sum(grad_mixed.astype(jnp.float32), axis=0)
    grad_norm_one = jnp.dot(grad_mixed, qkv_weight.T, preferred_element_type=jnp.float32)
    norm_one_back = jax.vjp(layer_norm, x_rows, gain_one, shift_one)[1]
    input_part, grad_gain_one, grad_shift_one = norm_one_back(grad_norm_one)
    input_grad = (grad_resid + input_part).astype(jnp.bfloat16)[None]
    members = (
        grad_gain_one,
        grad_shift_one,
        grad_qkv_weight,
        grad_qkv_bias,
        grad_proj_weight,
        grad_proj_bias,
        grad_gain_two,
        grad_shift_two,
        grad_up_weight,
        grad_up_bias,
        grad_down_weight,
        grad_down_bias,
    )
    large = [2, 4, 8, 10]
    blocks = []
    for k in large:
        member = members[k].astype(jnp.bfloat16)
        for r in range(member.shape[0] // width):
            for c in range(member.shape[1] // width):
                blocks.append(member[r * width : (r + 1) * width, c * width : (c + 1) * width])
    stacked = jnp.stack(blocks).reshape(len(blocks), 2, width // 2, width)
    grads = jnp.transpose(stacked, (1, 0, 2, 3)).reshape(-1, width)
    rest = [k for k in range(len(members)) if k not in large]
    flat = jnp.concatenate([members[k] for k in rest])
    small_rows = -(-flat.size // (8 * width)) * 8
    small = jnp.pad(flat, (0, small_rows * width - flat.size)).reshape(small_rows, width)
    grads, small = sum_over_devices(grads, small, count)
    flat = small.reshape(-1)
    blocks = jnp.transpose(grads.reshape(2, len(blocks), width // 2, width), (1, 0, 2, 3))
    blocks = blocks.reshape(-1, width, width)
    outputs = [None] * len(members)
    at = 0
    for k in large:
        tall, wide = (extent // width for extent in members[k].shape)
        rows_of = []
        for r in range(tall):
            rows_of.append(jnp.concatenate([blocks[at + r * wide + c] for c in range(wide)], axis=1))
        outputs[k] = jnp.concatenate(rows_of, axis=0).astype(jnp.float32)
        at += tall * wide
    offset = 0
    for k in rest:
        extent = members[k].size
        outputs[k] = flat[offset : offset + extent]
        offset = offset + extent
    return (
        layer_out,
        input_grad,
        outputs[0],
        outputs[1],
        outputs[2],
        outputs[3],
        outputs[4],
        outputs[5],
        outputs[6],
        outputs[7],
        outputs[8],
        outputs[9],
        outputs[10],
        outputs[11],
    )


def solution(mesh):
    in_specs = (
        P("batch", "seq", None),
        P("batch", "seq", None),
        P("batch", None),
        P(),
        P(),
        P(),
        P(),
        P(),
        P(),
        P(),
        P(),
        P(),
        P(),
        P(),
        P(),
    )
    out_specs = (
        P("batch", "seq", None),
        P("batch", "seq", None),
        P(),
        P(),
        P(),
        P(),
        P(),
        P(),
        P(),
        P(),
        P(),
        P(),
        P(),
        P(),
    )
    return jax.shard_map(
        per_device, mesh=mesh, in_specs=in_specs, out_specs=out_specs, check_vma=False
    )
```

```python
import functools
import math

import jax
import jax.numpy as jnp
from jax import lax
from jax.experimental import pallas as pl
from jax.experimental.pallas import tpu as pltpu
from jax.sharding import PartitionSpec as P

HEADS = 12
HD = 64


norm_eps = 1e-05
masked_low = -1e30


MESH_ID = pl.DeviceIdType.MESH
TILE = 16
LANES = 128
FF_TILE = 768
ITEM = 256
KINDS = "012"
GROUPS = 5
PACE = 8


def running_sum(lengths):
    places = jnp.arange(lengths.shape[0], dtype=jnp.int32)
    return jnp.sum(jnp.where(places[None, :] <= places[:, None], lengths[None, :], 0), axis=1)


class Place:
    def __init__(self):
        self.seq = lax.axis_index("seq")
        self.batch = lax.axis_index("batch")

    def bit(self, axis):
        name, k = axis
        return ((self.seq if name == "seq" else self.batch) // (1 << k)) % 2

    def partner(self, axis):
        name, k = axis
        step = (1 << k) * (1 - 2 * self.bit(axis))
        if name == "seq":
            return (self.seq + step, self.batch)
        return (self.seq, self.batch + step)


CORE = ("batch", 0)
ACROSS = ("batch", 1)


def seq_axes(peers):
    return [("seq", k) for k in range((peers - 1).bit_length())]


def axis_orders(peers):
    bits = seq_axes(peers)
    return [[bits[0], ACROSS] + bits[1:], [ACROSS] + bits, bits[1:] + [bits[0], ACROSS]]


def parts_of(rows, stages):
    found = []
    for _ in range(stages):
        halve = (rows // 2) % TILE == 0
        rows = rows // 2 if halve else rows
        found.append((rows, halve))
    return found


class Sems:
    def __init__(self, send, recv):
        self.send, self.recv, self.count = send, recv, 0

    def take(self):
        k = self.count
        self.count += 1
        return self.send.at[k], self.recv.at[k]


def rows_at(start, size):
    return pl.ds(pl.multiple_of(start, TILE), size)


def add_rows(into, one, at, other, other_at, rows):
    step = 32 if rows % 32 == 0 else TILE

    def body(i, carry):
        here = rows_at(at + i * step, step)
        there = rows_at(other_at + i * step, step)
        both = one[here].astype(jnp.float32) + other[there].astype(jnp.float32)
        into[here] = both.astype(into.dtype)
        return carry

    lax.fori_loop(0, rows // step, body, 0)


def sum_item(place, sems, buf, at, rows, order, inbox, used, total):
    low, plan = at, []
    for k, (axis, (part, halve)) in enumerate(zip(order, parts_of(rows, len(order)))):
        bit = place.bit(axis)
        keep, give = (low + bit * part, low + (1 - bit) * part) if halve else (low, low)
        copy = pltpu.make_async_remote_copy(
            buf.at[rows_at(give, part)],
            inbox.at[rows_at(used, part)],
            *sems.take(),
            device_id=place.partner(axis),
            device_id_type=MESH_ID,
        )
        copy.start()
        yield
        copy.wait()
        add_rows(total if k == len(order) - 1 else buf, buf, keep, inbox, used, part)
        plan.append((axis, keep, part, halve))
        used += part
        low = keep
    for axis, keep, part, halve in reversed(plan):
        if halve:
            here = rows_at(keep, part)
            copy = pltpu.make_async_remote_copy(
                total.at[here],
                total.at[here],
                *sems.take(),
                device_id=place.partner(axis),
                device_id_type=MESH_ID,
            )
            copy.start()
            yield
            copy.wait()


def dot(a, b, dims=((1,), (0,))):
    return lax.dot_general(a, b, (dims, ((), ())), preferred_element_type=jnp.float32)


NT = ((1,), (1,))
TN = ((0,), (0,))


def norm_parts(rows):
    center = rows - jnp.mean(rows, axis=-1, keepdims=True)
    spread = jnp.mean(center * center, axis=-1, keepdims=True)
    inverse = lax.rsqrt(spread + norm_eps)
    return center * inverse, inverse


def norm_back(grad, unit, inverse, gain):
    scaled = grad * gain
    along = jnp.mean(scaled * unit, axis=-1, keepdims=True)
    return inverse * (scaled - jnp.mean(scaled, axis=-1, keepdims=True) - unit * along)


def doc_ids(ends, places):
    found = jnp.zeros(places.shape, jnp.int32)
    for k in range(ends.shape[0]):
        found += (ends[k] <= places).astype(jnp.int32)
    return found


def places_down(first, rows):
    return first + lax.broadcasted_iota(jnp.int32, (rows, 1), 0)


def places_along(first, rows):
    return first + lax.broadcasted_iota(jnp.int32, (1, rows), 1)


def mask_of(ends, q_places, k_places):
    allowed = (doc_ids(ends, q_places) == doc_ids(ends, k_places)) & (k_places <= q_places)
    return jnp.where(allowed, 0.0, masked_low)


def first_half():
    return lax.broadcasted_iota(jnp.int32, (1, LANES), 1) < HD


def both_heads(pair):
    left = first_half()
    none = jnp.zeros_like(pair)
    return jnp.concatenate([jnp.where(left, pair, none), jnp.where(left, none, pair)], axis=0)


def own_columns(stacked):
    rows = stacked.shape[0] // 2
    return jnp.where(first_half(), stacked[:rows], stacked[rows:])


def lanes(p):
    return pl.ds(p * LANES, LANES)


def forward_kernel(
    nz, n_ends, x_ref, e_ref, ends, gain_one, shift_one, qkv_bias, proj_bias, gain_two, shift_two, up_bias, down_bias,
    qkv_hbm, proj_hbm, up_hbm, down_hbm,
    layer_out, n1_all, q_out, attn_out, da_out, do_out, n2_out, g_out, du_out, dx_out, stats_out, small_out,
    x_all, qkv_w, proj_w, up_w, down_w, kv, mask, top, total, acc, two_q, res_acc, dh_acc,
    up_send, up_recv, down_send, down_recv, side_send, side_recv, w_sem,
):
    rows, width = x_ref.shape
    pair = 2 * rows
    seq = lax.axis_index("seq")
    batch = lax.axis_index("batch")
    z = seq // 2
    x = seq % 2
    loads = [
        pltpu.make_async_copy(hbm, vmem, w_sem.at[k])
        for k, (hbm, vmem) in enumerate(
            [(qkv_hbm, qkv_w), (proj_hbm, proj_w), (up_hbm, up_w), (down_hbm, down_w)]
        )
    ]
    loads[0].start()
    barrier = pltpu.get_barrier_semaphore()
    has_up = z + 1 < nz
    has_down = z > 0
    above = (seq + 2, batch)
    below = (seq - 2, batch)
    beside = (seq + 1 - 2 * x, batch)

    @pl.when(has_up)
    def _():
        pl.semaphore_signal(barrier, inc=1, device_id=above, device_id_type=MESH_ID)

    @pl.when(has_down)
    def _():
        pl.semaphore_signal(barrier, inc=1, device_id=below, device_id_type=MESH_ID)

    pl.semaphore_signal(barrier, inc=1, device_id=beside, device_id_type=MESH_ID)
    pl.semaphore_wait(barrier, 1 + has_up.astype(jnp.int32) + has_down.astype(jnp.int32))
    for load in loads[1:]:
        load.start()

    def block(level, side):
        return x_all.at[rows_at((2 * level + side) * rows, rows)]

    def send(source, level, to, send_sem, recv_sem):
        return pltpu.make_async_remote_copy(
            source, block(level, x), send_sem.at[level], recv_sem.at[level], device_id=to, device_id_type=MESH_ID
        )

    def up_copy(source, level):
        return send(source, level, above, up_send, up_recv)

    def down_copy(source, level):
        return send(source, level, below, down_send, down_recv)

    def side_copy(source, level):
        return send(source, level, beside, side_send, side_recv)

    def wait_side(level):
        pltpu.make_async_remote_copy(
            x_ref, block(level, 1 - x), side_send.at[level], side_recv.at[level], device_id=beside, device_id_type=MESH_ID
        ).wait_recv()

    @pl.when(has_up)
    def _():
        up_copy(x_ref, z).start()

    side_copy(x_ref, z).start()

    @pl.when(has_down)
    def _():
        down_copy(x_ref, z).start()

    x_all[rows_at(seq * rows, rows)] = x_ref[...]
    x32 = x_ref[...].astype(jnp.float32)
    unit_one, _ = norm_parts(x32)
    mine = (unit_one * gain_one[...] + shift_one[...]).astype(jnp.bfloat16)
    top[...] = jnp.full(top.shape, masked_low, jnp.float32)
    total[...] = jnp.zeros(total.shape, jnp.float32)
    acc[...] = jnp.zeros(acc.shape, jnp.float32)
    loads[0].wait()
    q = (dot(mine, qkv_w[:, :width]) + qkv_bias[:, :width]).astype(jnp.bfloat16)
    q = q * jnp.asarray(1.0 / math.sqrt(HD), jnp.bfloat16)
    q_out[...] = q
    for p in range(HEADS // 2):
        two_q[p] = both_heads(q[:, p * LANES : (p + 1) * LANES])

    def pass_on(d):
        @pl.when(z >= d)
        def _():
            level = z - d
            up_copy(x_ref, level).wait_recv()

            @pl.when(has_up)
            def _():
                up_copy(block(level, x), level).start()

            side_copy(block(level, x), level).start()

        @pl.when(z + d < nz)
        def _():
            level = z + d
            down_copy(x_ref, level).wait_recv()

            @pl.when(has_down)
            def _():
                down_copy(block(level, x), level).start()

            side_copy(block(level, x), level).start()

    def normalize(level):
        here = rows_at(level * pair, pair)
        unit, _ = norm_parts(x_all[here].astype(jnp.float32))
        n1 = (unit * gain_one[...] + shift_one[...]).astype(jnp.bfloat16)
        n1_all[here] = n1
        return n1

    def attend(level):
        wait_side(level)
        n1 = normalize(level)
        kv[...] = (dot(n1, qkv_w[:, width:]) + qkv_bias[:, width:]).astype(jnp.bfloat16)
        one = mask_of(ends, places_down(seq * rows, rows), places_along(level * pair, pair))
        mask[:rows] = one
        mask[rows:] = one
        for p in range(HEADS // 2):
            k_pair = kv[:, p * LANES : (p + 1) * LANES]
            v_pair = kv[:, width + p * LANES : width + (p + 1) * LANES]
            s = dot(two_q[p], k_pair, NT)
            low = mask[...]
            before = top[p][:, :1]
            newer = jnp.maximum(before, jnp.max(jnp.abs(s) + low, axis=1, keepdims=True))
            low = low - newer
            plus = jnp.exp(low + s)
            minus = jnp.exp(low - s)
            keep = jnp.exp(before - newer)
            total[p] = total[p] * keep + jnp.sum(plus + minus, axis=1, keepdims=True)
            top[p] = jnp.broadcast_to(newer, (pair, LANES))
            out = own_columns(dot((plus - minus).astype(jnp.bfloat16), v_pair))
            keep = own_columns(jnp.broadcast_to(keep, (pair, LANES)))
            here = slice(p * LANES, (p + 1) * LANES)
            acc[:, here] = acc[:, here] * keep + out

    def level_step(d, carry):
        @pl.when(d + 1 < nz)
        def _():
            pass_on(d + 1)

        @pl.when(z >= d)
        def _():
            attend(z - d)

        @pl.when((d > 0) & (z + d < nz))
        def _():
            wait_side(z + d)
            normalize(z + d)

        return carry

    lax.fori_loop(0, nz, level_step, 0)

    column = lax.broadcasted_iota(jnp.int32, (1, LANES), 1)
    log_total = jnp.zeros((rows, LANES), jnp.float32)
    for p in range(HEADS // 2):
        here = slice(p * LANES, (p + 1) * LANES)
        acc[:, here] = acc[:, here] / own_columns(total[p])
        lse = top[p] + jnp.log(total[p])
        log_total = jnp.where(column == 2 * p, lse[:rows], log_total)
        log_total = jnp.where(column == 2 * p + 1, lse[rows:], log_total)
    attn = acc[...].astype(jnp.bfloat16)
    attn_out[...] = attn
    loads[1].wait()
    resid = x32 + dot(attn, proj_w[...]) + proj_bias[...]
    unit, inverse = norm_parts(resid)
    n2 = (unit * gain_two[...] + shift_two[...]).astype(jnp.bfloat16)
    n2_out[...] = n2
    res_acc[...] = resid + down_bias[...]
    dh_acc[...] = jnp.zeros(dh_acc.shape, jnp.float32)
    loads[2].wait()
    loads[3].wait()
    slope = math.sqrt(2.0 / math.pi)

    def ff_step(t, carry):
        here = pl.ds(pl.multiple_of(t * FF_TILE, FF_TILE), FF_TILE)
        u = dot(n2_out[...], up_w[:, here]) + up_bias[:, here]
        square = u * u
        bend = jnp.tanh(slope * (u + 0.044715 * (square * u)))
        half = 0.5 * (1.0 + bend)
        g = (u * half).astype(jnp.bfloat16)
        slant = half + (0.5 * u) * (1.0 - bend * bend) * (slope * (1.0 + 3.0 * 0.044715 * square))
        g_out[:, here] = g
        res_acc[...] += dot(g, down_w[here])
        du32 = dot(e_ref[...], down_w[here], NT) * slant
        du = du32.astype(jnp.bfloat16)
        du_out[:, here] = du
        small_out[pl.ds(4 + t, 1)] = jnp.sum(du.astype(jnp.float32), axis=0, keepdims=True)
        dh_acc[...] += dot(du, up_w[:, here], NT)
        return carry

    lax.fori_loop(0, up_w.shape[1] // FF_TILE, ff_step, 0)
    layer_out[...] = res_acc[...].astype(jnp.bfloat16)
    dh = dh_acc[...]
    grad_rows = e_ref[...].astype(jnp.float32)
    dx = grad_rows + norm_back(dh, unit, inverse, gain_two[...])
    dx_out[...] = dx
    da = dx.astype(jnp.bfloat16)
    da_out[...] = da
    do = dot(da, proj_w[...], NT).astype(jnp.bfloat16)
    do_out[...] = do
    product = do.astype(jnp.float32) * acc[...]
    delta = jnp.zeros((rows, LANES), jnp.float32)
    left = first_half()
    for p in range(HEADS // 2):
        here = product[:, p * LANES : (p + 1) * LANES]
        one = jnp.sum(jnp.where(left, here, 0.0), axis=1, keepdims=True)
        two = jnp.sum(jnp.where(left, 0.0, here), axis=1, keepdims=True)
        delta = jnp.where(column == 2 * p, one, delta)
        delta = jnp.where(column == 2 * p + 1, two, delta)
    stats_out[0] = log_total
    stats_out[1] = delta
    small_out[0:1] = jnp.sum(dh * unit, axis=0, keepdims=True)
    small_out[1:2] = jnp.sum(dh, axis=0, keepdims=True)
    small_out[2:3] = jnp.sum(grad_rows, axis=0, keepdims=True)
    small_out[3:4] = jnp.sum(da.astype(jnp.float32), axis=0, keepdims=True)

    side_copy(x_ref, z).wait_send()

    @pl.when(has_up)
    def _():
        up_copy(x_ref, z).wait_send()

    @pl.when(has_down)
    def _():
        down_copy(x_ref, z).wait_send()

    def sent(d, carry):
        @pl.when(z >= d)
        def _():
            side_copy(x_ref, z - d).wait_send()

            @pl.when(has_up)
            def _():
                up_copy(x_ref, z - d).wait_send()

        @pl.when(z + d < nz)
        def _():
            side_copy(x_ref, z + d).wait_send()

            @pl.when(has_down)
            def _():
                down_copy(x_ref, z + d).wait_send()

        return carry

    lax.fori_loop(1, nz, sent, 0)


def run_forward(x, e, ends, gain_one, shift_one, qkv_weight, qkv_bias, proj_weight, proj_bias, gain_two, shift_two, up_weight, up_bias, down_weight, down_bias, peers):
    rows, width = x.shape
    hidden = up_weight.shape[1]
    nz = peers // 2
    bf, f32 = jnp.bfloat16, jnp.float32
    vmem = pl.BlockSpec(memory_space=pltpu.VMEM)
    smem = pl.BlockSpec(memory_space=pltpu.SMEM)
    hbm = pl.BlockSpec(memory_space=pl.ANY)
    dma = pltpu.SemaphoreType.DMA
    outs = [
        ((rows, width), bf), ((peers * rows, width), bf), ((rows, width), bf), ((rows, width), bf), ((rows, width), bf),
        ((rows, width), bf), ((rows, width), bf), ((rows, hidden), bf), ((rows, hidden), bf), ((rows, width), f32),
        ((2, rows, LANES), f32), ((4 + hidden // width, width), f32),
    ]
    row = lambda v: v.reshape(1, -1)
    return pl.pallas_call(
        functools.partial(forward_kernel, nz, ends.shape[0]),
        out_shape=[jax.ShapeDtypeStruct(*o) for o in outs],
        in_specs=[vmem, vmem, smem] + [vmem] * 8 + [hbm] * 4,
        out_specs=[vmem] * len(outs),
        scratch_shapes=[
            pltpu.VMEM((peers * rows, width), bf),
            pltpu.VMEM(qkv_weight.shape, bf),
            pltpu.VMEM(proj_weight.shape, bf),
            pltpu.VMEM(up_weight.shape, bf),
            pltpu.VMEM(down_weight.shape, bf),
            pltpu.VMEM((2 * rows, 2 * width), bf),
            pltpu.VMEM((2 * rows, 2 * rows), f32),
            pltpu.VMEM((HEADS // 2, 2 * rows, LANES), f32),
            pltpu.VMEM((HEADS // 2, 2 * rows, LANES), f32),
            pltpu.VMEM((rows, width), f32),
            pltpu.VMEM((HEADS // 2, 2 * rows, LANES), bf),
            pltpu.VMEM((rows, width), f32),
            pltpu.VMEM((rows, width), f32),
            dma((nz,)), dma((nz,)), dma((nz,)), dma((nz,)), dma((nz,)), dma((nz,)), dma((4,)),
        ],
        compiler_params=pltpu.CompilerParams(collective_id=0, has_side_effects=True, vmem_limit_bytes=60 * 2**20),
        cost_estimate=pl.CostEstimate(flops=10**9, bytes_accessed=2 * 10**7, transcendentals=10**6),
    )(x, e, ends, row(gain_one), row(shift_one), row(qkv_bias), row(proj_bias), row(gain_two), row(shift_two), row(up_bias),
      row(down_bias), qkv_weight, proj_weight, up_weight, down_weight)


def backward_kernel(
    nz, items, orders,
    x_ref, e_ref, ends, gain_one, qkv_bias, n1_all, q_ref, attn_ref, da_ref, do_ref, n2_ref, g_ref, du_ref, dx_ref,
    stats_ref, first_small, qkv_hbm,
    input_grad, qkv_out, proj_out, up_out, down_out, small_out,
    qkv_w, buf, inbox, total, do_all, rows_all, g_cat, e_cat, n2_cat, du_cat, attn_cat, da_cat, n1_cat, dqkv_cat,
    two_q, two_do, two_k, two_v, lse_cols, delta_cols, kv, n1_held, mask, dq, dk, dv, small_in,
    down_send, down_recv, side_send, side_recv, ssem, rsem, lsem,
):
    rows, width = x_ref.shape
    pair = 2 * rows
    place = Place()
    seq, batch = place.seq, place.batch
    z = seq // 2
    x = seq % 2
    core = place.bit(CORE)
    sems = Sems(ssem, rsem)
    local = Sems(lsem, lsem)
    load = pltpu.make_async_copy(qkv_hbm, qkv_w, local.take()[0])
    load.start()
    small_axes = [CORE, ACROSS] + seq_axes(2 * nz)
    has_up = z + 1 < nz
    has_down = z > 0
    above = (seq + 2, batch)
    below = (seq - 2, batch)
    beside = (seq + 1 - 2 * x, batch)
    barrier = pltpu.get_barrier_semaphore()
    for axis in small_axes:
        pl.semaphore_signal(barrier, inc=1, device_id=place.partner(axis), device_id_type=MESH_ID)

    @pl.when(has_up)
    def _():
        pl.semaphore_signal(barrier, inc=1, device_id=above, device_id_type=MESH_ID)

    @pl.when(has_down)
    def _():
        pl.semaphore_signal(barrier, inc=1, device_id=below, device_id_type=MESH_ID)

    for k in range(2):
        rows_all[seq, k * TILE : (k + 1) * TILE] = stats_ref[k].T[:TILE]
    pl.semaphore_wait(barrier, len(small_axes) + has_up.astype(jnp.int32) + has_down.astype(jnp.int32))

    def cols(half, size):
        return pl.ds(pl.multiple_of(half * size, LANES), size)

    def to_core(source, into):
        return pltpu.make_async_remote_copy(
            source, into.at[rows:], *sems.take(), device_id=place.partner(CORE), device_id_type=MESH_ID
        )

    def keep_own(source, into):
        return pltpu.make_async_copy(source, into.at[:rows], local.take()[0])

    def exchange(ref, into, halved):
        size = into.shape[1]
        give = ref.at[:, cols(1 - core, size)] if halved else ref
        keep = ref.at[:, cols(core, size)] if halved else ref
        copies = [to_core(give, into), keep_own(keep, into)]
        for copy in copies:
            copy.start()
        return copies

    def done(copies):
        for copy in copies:
            copy.wait()

    down_parts = exchange(g_ref, g_cat, True) + exchange(e_ref, e_cat, False)
    up_parts = exchange(n2_ref, n2_cat, False) + exchange(du_ref, du_cat, True)

    def do_block(level, side):
        return do_all.at[rows_at((2 * level + side) * rows, rows)]

    def do_copies(level, side, to, send_sem, recv_sem, own=False):
        source = do_ref if own else do_block(level, side)
        stat = rows_all.at[2 * level + side]
        return [
            pltpu.make_async_remote_copy(
                source, do_block(level, side), send_sem.at[level, 0], recv_sem.at[level, 0], device_id=to, device_id_type=MESH_ID
            ),
            pltpu.make_async_remote_copy(
                stat, stat, send_sem.at[level, 1], recv_sem.at[level, 1], device_id=to, device_id_type=MESH_ID
            ),
        ]

    def down_copies(level, own=False):
        return do_copies(level, x, below, down_send, down_recv, own)

    def side_copies(level, own=False):
        return do_copies(level, x, beside, side_send, side_recv, own)

    def begin(copies):
        for copy in copies:
            copy.start()

    @pl.when(has_down)
    def _():
        begin(down_copies(z, True))

    begin(side_copies(z, True))
    do_all[rows_at(seq * rows, rows)] = do_ref[...]

    spread = [1]

    def spread_until(last):
        while spread[0] <= min(last, nz - 1):
            d = spread[0]
            spread[0] += 1

            @pl.when(z + d < nz)
            def _():
                level = z + d
                for copy in down_copies(level):
                    copy.wait_recv()

                @pl.when(has_down)
                def _():
                    begin(down_copies(level))

                begin(side_copies(level))

    def spread_end():
        def sent(copies):
            for copy in copies:
                copy.wait_send()

        sent(side_copies(z, True))

        @pl.when(has_down)
        def _():
            sent(down_copies(z, True))

        def each(level, carry):
            sent(side_copies(level))

            @pl.when(has_down)
            def _():
                sent(down_copies(level))

            return carry

        lax.fori_loop(z + 1, nz, each, 0)

    slots = []
    at = used = 0
    for size, kind, _ in items:
        slots.append((at, size, orders[kind], used))
        at += size
        used += sum(part for part, _ in parts_of(size, len(orders[kind])))
    places = [(name, r) for _, _, (name, r) in items]

    def destination(name, r, size):
        half = width // 2
        if name == "down":
            return down_out.at[rows_at(core * down_out.shape[0] // 2 + r, size)]
        if name[:2] == "up":
            return up_out.at[r : r + size, pl.ds(pl.multiple_of((core * (up_out.shape[1] // width // 2) + int(name[2:])) * width, width), width)]
        if name == "proj":
            return proj_out.at[rows_at(core * half + r, size)]
        return qkv_out.at[rows_at(core * half + r, size), int(name[3:]) * width : (int(name[3:]) + 1) * width]

    def item_task(k):
        at, size, order, used = slots[k]
        yield from sum_item(place, sems, buf, at, size, order, inbox, used, total)
        there = destination(*places[k], size)
        here = total.at[rows_at(at, size)]
        keep = pltpu.make_async_copy(here, there, local.take()[0])
        give = pltpu.make_async_remote_copy(here, there, *sems.take(), device_id=place.partner(CORE), device_id_type=MESH_ID)
        keep.start()
        give.start()
        yield
        keep.wait()
        give.wait()

    def small_task(group):
        held = small_out.at[8 * group : 8 * group + 8]
        for k, axis in enumerate(small_axes):
            copy = pltpu.make_async_remote_copy(
                held, small_in.at[group, k], *sems.take(), device_id=place.partner(axis), device_id_type=MESH_ID
            )
            copy.start()
            yield
            copy.wait()
            held[...] += small_in[group, k]

    live = []

    def turn(pieces):
        for task in list(live):
            if pieces:
                pieces.step()
            try:
                next(task)
            except StopIteration:
                live.remove(task)

    def enter(task):
        next(task)
        live.append(task)

    def weight_items(name, left, right):
        for k, (where, r) in enumerate(places):
            if where == name:
                at, size, _, _ = slots[k]
                buf[at : at + size] = dot(left[:, r : r + size], right, TN).astype(jnp.bfloat16)
                enter(item_task(k))

    small_out[:8] = first_small[...]
    done(down_parts)
    weight_items("down", g_cat, e_cat[...])
    done(up_parts)
    for j in range(du_cat.shape[1] // width):
        weight_items(f"up{j}", n2_cat, du_cat[:, j * width : (j + 1) * width])
    proj_parts = exchange(attn_ref, attn_cat, True) + exchange(da_ref, da_cat, False)
    own_n1 = rows_at(seq * rows, rows)
    n1_parts = exchange(n1_all.at[own_n1], n1_cat, True)
    enter(small_task(0))

    load.wait()
    scale = jnp.asarray(1.0 / math.sqrt(HD), jnp.bfloat16)

    chunk_sem = local.take()[0]

    def n1_chunk(level):
        copy = pltpu.make_async_copy(n1_all.at[rows_at(level * pair, pair)], n1_held, chunk_sem)
        copy.start()
        copy.wait()
        return n1_held[...]

    def prepare():
        n1_chunk(z)
        mine = n1_held[rows_at(x * rows, rows)]
        own_kv = (dot(mine, qkv_w[:, width:]) + qkv_bias[:, width:]).astype(jnp.bfloat16)
        for p in range(HEADS // 2):
            here = slice(p * LANES, (p + 1) * LANES)
            two_q[p] = both_heads(q_ref[:, here])
            two_do[p] = both_heads(do_ref[:, here])
            two_k[p] = both_heads(own_kv[:, here])
            two_v[p] = both_heads(own_kv[:, width + p * LANES : width + (p + 1) * LANES])
            for k, into in enumerate((lse_cols, delta_cols)):
                for h in range(2):
                    column = stats_ref[k, :, 2 * p + h : 2 * p + h + 1]
                    into[p, h * rows : (h + 1) * rows] = jnp.broadcast_to(column, (rows, LANES))
        dq[...] = jnp.zeros(dq.shape, jnp.float32)
        dk[...] = jnp.zeros(dk.shape, jnp.float32)
        dv[...] = jnp.zeros(dv.shape, jnp.float32)

    def columns_of(p):
        return pl.ds(pl.multiple_of(p * LANES, LANES), LANES)

    def query_step(level):
        n1 = n1_chunk(level)
        kv[...] = (dot(n1, qkv_w[:, width:]) + qkv_bias[:, width:]).astype(jnp.bfloat16)
        one = mask_of(ends, places_down(seq * rows, rows), places_along(level * pair, pair))
        mask[:rows] = one
        mask[rows:] = one

        def each(p, carry):
            k_pair = kv[:, columns_of(p)]
            v_pair = kv[:, columns_of(p + HEADS // 2)]
            s = dot(two_q[p], k_pair, NT)
            along = dot(two_do[p], v_pair, NT)
            low = mask[...] - lse_cols[p][:, :1]
            plus = jnp.exp(low + s)
            minus = jnp.exp(low - s)
            ds = ((plus + minus) * along - (plus - minus) * delta_cols[p][:, :1]).astype(jnp.bfloat16)
            dq[:, columns_of(p)] += own_columns(dot(ds, k_pair))
            return carry

        lax.fori_loop(0, HEADS // 2, each, 0)

    def key_step(level):
        side = 1 - x
        for copy in do_copies(level, side, beside, side_send, side_recv):
            copy.wait_recv()
        here = rows_at(level * pair, pair)
        n1 = n1_chunk(level)
        kv[:, :width] = (dot(n1, qkv_w[:, :width]) + qkv_bias[:, :width]).astype(jnp.bfloat16) * scale
        one = mask_of(ends, places_along(level * pair, pair), places_down(seq * rows, rows))
        mask[:rows] = one
        mask[rows:] = one

        def stat(row):
            both = [rows_all[2 * level + k, pl.ds(row, 1)] for k in range(2)]
            return jnp.concatenate(both, axis=1)

        def stat_rows(k, p):
            both = [jnp.broadcast_to(stat(k * TILE + 2 * p + h), (rows, pair)) for h in range(2)]
            return jnp.concatenate(both, axis=0)

        def each(p, carry):
            q_pair = kv[:, columns_of(p)]
            do_pair = do_all[here, columns_of(p)]
            s = dot(two_k[p], q_pair, NT)
            along = dot(two_v[p], do_pair, NT)
            low = mask[...] - stat_rows(0, p)
            plus = jnp.exp(low + s)
            minus = jnp.exp(low - s)
            signed = plus - minus
            ds = ((plus + minus) * along - signed * stat_rows(1, p)).astype(jnp.bfloat16)
            dk[:, columns_of(p)] += own_columns(dot(ds, q_pair))
            dv[:, columns_of(p)] += own_columns(dot(signed.astype(jnp.bfloat16), do_pair))
            return carry

        lax.fori_loop(0, HEADS // 2, each, 0)

    def one_step(t):
        @pl.when(t <= z)
        def _():
            query_step(z - t)

        @pl.when(t > z)
        def _():
            key_step(t - 1)

    def steps_piece(first, last):
        def piece():
            spread_until(last)
            if last - first == 1:
                one_step(first)
            else:

                def body(t, carry):
                    one_step(t)
                    return carry

                lax.fori_loop(first, last, body, 0)

        return piece

    def proj_piece():
        done(proj_parts)
        weight_items("proj", attn_cat, da_cat[...])

    groups = min(nz + 1, GROUPS)
    cuts = [(nz + 1) * k // groups for k in range(groups + 1)]
    pieces = Paced([prepare, proj_piece] + [steps_piece(a, b) for a, b in zip(cuts, cuts[1:])], PACE)
    while pieces.left():
        turn(pieces)

    dqkv = jnp.concatenate(
        [
            (dq[...] * (1.0 / math.sqrt(HD))).astype(jnp.bfloat16),
            dk[...].astype(jnp.bfloat16),
            dv[...].astype(jnp.bfloat16),
        ],
        axis=1,
    )
    dqkv_cat[:rows] = dqkv
    send = to_core(dqkv_cat.at[:rows], dqkv_cat)
    send.start()
    dh = dot(dqkv, qkv_w[...], NT)
    unit, inverse = norm_parts(x_ref[...].astype(jnp.float32))
    input_grad[...] = (dx_ref[...] + norm_back(dh, unit, inverse, gain_one[...])).astype(jnp.bfloat16)
    sums = jnp.sum(dqkv.astype(jnp.float32), axis=0, keepdims=True)
    for k in range(3):
        small_out[8 + k : 9 + k] = sums[:, k * width : (k + 1) * width]
    small_out[11:12] = jnp.sum(dh * unit, axis=0, keepdims=True)
    small_out[12:13] = jnp.sum(dh, axis=0, keepdims=True)
    small_out[13:16] = jnp.zeros((3, width), jnp.float32)
    done(n1_parts)
    send.wait()
    for j in range(3):
        weight_items(f"qkv{j}", n1_cat, dqkv_cat[:, j * width : (j + 1) * width])
    enter(small_task(1))
    while live:
        turn(None)
    spread_end()


class Paced:
    def __init__(self, pieces, every):
        self.pieces, self.every, self.asked = pieces, every, 0

    def left(self):
        return len(self.pieces)

    def step(self):
        if self.pieces and self.asked % self.every == 0:
            self.pieces.pop(0)()
        self.asked += 1


def plan_items(width, hidden):
    half = width // 2

    def cut(name, size):
        return [(min(ITEM, size - r), (name, r)) for r in range(0, size, ITEM)]

    found = cut("down", hidden // 2)
    for j in range(hidden // 2 // width):
        found += cut(f"up{j}", width)
    found += cut("proj", half)
    for j in range(3):
        found += cut(f"qkv{j}", half)
    return [(size, int(KINDS[k % len(KINDS)]), where) for k, (size, where) in enumerate(found)]


def run_backward(x, e, ends, gain_one, qkv_weight, qkv_bias, kept, peers):
    n1_all, q, attn, da, do, n2, g, du, dx, stats, small = kept
    rows, width = x.shape
    hidden = g.shape[1]
    nz = peers // 2
    bf, f32 = jnp.bfloat16, jnp.float32
    orders = axis_orders(peers)
    items = plan_items(width, hidden)
    counts = [parts_of(size, len(orders[kind])) for size, kind, _ in items]
    used = sum(part for count in counts for part, _ in count)
    height = sum(size for size, _, _ in items)
    stages = 2 + len(seq_axes(peers))
    copies = sum(1 + len(count) + sum(halve for _, halve in count) for count in counts) + 2 * stages + 8
    vmem = pl.BlockSpec(memory_space=pltpu.VMEM)
    smem = pl.BlockSpec(memory_space=pltpu.SMEM)
    hbm = pl.BlockSpec(memory_space=pl.ANY)
    dma = pltpu.SemaphoreType.DMA
    row = lambda v: v.reshape(1, -1)
    out = jax.ShapeDtypeStruct
    stack = (HEADS // 2, 2 * rows, LANES)
    return pl.pallas_call(
        functools.partial(backward_kernel, nz, items, orders),
        out_shape=[
            out((rows, width), bf), out((width, 3 * width), bf), out((width, width), bf), out((width, hidden), bf),
            out((hidden, width), bf), out((16, width), f32),
        ],
        in_specs=[vmem, hbm, smem, vmem, vmem, hbm, vmem, hbm, hbm, vmem, hbm, hbm, hbm, vmem, vmem, vmem, hbm],
        out_specs=[vmem, hbm, hbm, hbm, hbm, vmem],
        scratch_shapes=[
            pltpu.VMEM(qkv_weight.shape, bf),
            pltpu.VMEM((height, width), bf),
            pltpu.VMEM((used, width), bf),
            pltpu.VMEM((height, width), bf),
            pltpu.VMEM((peers * rows, width), bf),
            pltpu.VMEM((peers, 2 * TILE, LANES), f32),
            pltpu.VMEM((2 * rows, hidden // 2), bf),
            pltpu.VMEM((2 * rows, width), bf),
            pltpu.VMEM((2 * rows, width), bf),
            pltpu.VMEM((2 * rows, hidden // 2), bf),
            pltpu.VMEM((2 * rows, width // 2), bf),
            pltpu.VMEM((2 * rows, width), bf),
            pltpu.VMEM((2 * rows, width // 2), bf),
            pltpu.VMEM((2 * rows, 3 * width), bf),
            pltpu.VMEM(stack, bf), pltpu.VMEM(stack, bf), pltpu.VMEM(stack, bf), pltpu.VMEM(stack, bf),
            pltpu.VMEM(stack, f32), pltpu.VMEM(stack, f32),
            pltpu.VMEM((2 * rows, 2 * width), bf),
            pltpu.VMEM((2 * rows, width), bf),
            pltpu.VMEM((2 * rows, 2 * rows), f32),
            pltpu.VMEM((rows, width), f32), pltpu.VMEM((rows, width), f32), pltpu.VMEM((rows, width), f32),
            pltpu.VMEM((2, stages, 8, width), f32),
            dma((nz, 2)), dma((nz, 2)), dma((nz, 2)), dma((nz, 2)),
            dma((copies,)), dma((copies,)), dma((len(items) + 10,)),
        ],
        compiler_params=pltpu.CompilerParams(collective_id=1, has_side_effects=True, vmem_limit_bytes=62 * 2**20),
    )(x, e, ends, row(gain_one), row(qkv_bias), n1_all, q, attn, da, do, n2, g, du, dx, stats, small, qkv_weight)


def per_device(
    inputs,
    cotangent,
    doc_lengths,
    gain_one,
    shift_one,
    qkv_weight,
    qkv_bias,
    proj_weight,
    proj_bias,
    gain_two,
    shift_two,
    up_weight,
    up_bias,
    down_weight,
    down_bias,
):
    peers = lax.axis_size("seq")
    width = inputs.shape[2]
    ends = running_sum(doc_lengths[0])
    layer_out, *kept = run_forward(
        inputs[0], cotangent[0], ends, gain_one, shift_one, qkv_weight, qkv_bias, proj_weight, proj_bias, gain_two, shift_two,
        up_weight, up_bias, down_weight, down_bias, peers,
    )
    input_grad, qkv, proj, up, down, small = run_backward(
        inputs[0], cotangent[0], ends, gain_one, qkv_weight, qkv_bias, kept, peers
    )
    wide = jnp.float32
    return (
        layer_out[None],
        input_grad[None],
        small[11],
        small[12],
        qkv.astype(wide),
        small[8:11].reshape(-1),
        proj.astype(wide),
        small[3],
        small[0],
        small[1],
        up.astype(wide),
        small[4:8].reshape(-1),
        down.astype(wide),
        small[2],
    )


def solution(mesh):
    in_specs = (
        P("batch", "seq", None),
        P("batch", "seq", None),
        P("batch", None),
        P(),
        P(),
        P(),
        P(),
        P(),
        P(),
        P(),
        P(),
        P(),
        P(),
        P(),
        P(),
    )
    out_specs = (
        P("batch", "seq", None),
        P("batch", "seq", None),
        P(),
        P(),
        P(),
        P(),
        P(),
        P(),
        P(),
        P(),
        P(),
        P(),
        P(),
        P(),
    )
    return jax.shard_map(
        per_device, mesh=mesh, in_specs=in_specs, out_specs=out_specs, check_vma=False
    )
```

```python
import functools
import math

import jax
import jax.numpy as jnp
from jax import lax
from jax.experimental import pallas as pl
from jax.experimental.pallas import tpu as pltpu
from jax.sharding import PartitionSpec as P

HEADS = 12
HD = 64


norm_eps = 1e-05
masked_low = -1e30


MESH_ID = pl.DeviceIdType.MESH
TILE = 16
LANES = 128
FF_TILE = 768
ITEM = 256
KINDS = "032102111511030001100"
GROUPS = 5
PACE = 8
UNROLL = 6
SCHEDULE = (
    -1, 0, 10, 12, 6, 5, 11, -2, 13, 8, 3, -3, 11, 1, 12, 13, 7, -4, 9, 2, 3, 1, 5, 8, 11, -5, 4, 0, 3, -6, 10, 8, 7,
    13, 2, 4, 0, 3, 12, 11, 8, 5, 6, -7, 20, 14, 3, 17, 4, 7, 0, 3, 5, 11, 16, 15, 12, 19, 1, 7, 8, 9, 4, 6, 5, 14,
    18, 3, 10, 9, 1, 13, 14, 6, 16, 7, 4, 5, 11, 15, 20, 14, 17, 18, 19, 7, 15, 4, 3, 10, 6, 17, 8, 9, 13, 12, 7, 16,
    4, 0, 6, 15, 9, 17, 1, 20, 7, 14, 2, 19, 8, 16, 1, 11, 18, 2, 10, 12, 8, 16, 0, 17, 4, 2, 1, 9, 14, 19, 18, 15, 6,
    17, 5, 12, 10, 14, 20, 16, 0, 12, 13, 9, 11, 20, 10, 2, 19, 0, 16, 10, 17, 18, 13, 14, 18, 19, 6, 20, 8, 5, 16,
    15, 4, 18, 13, 3, 19, 9, 0, 10, 2, 1, 2, 14, 18, 17, 19, 1, 16, 15, 6, 7, 12, 5, 18, 9, 2, 15, 11,
)


class Place:
    def __init__(self):
        self.seq = lax.axis_index("seq")
        self.batch = lax.axis_index("batch")

    def bit(self, axis):
        name, k = axis
        return ((self.seq if name == "seq" else self.batch) // (1 << k)) % 2

    def partner(self, axis):
        name, k = axis
        step = (1 << k) * (1 - 2 * self.bit(axis))
        if name == "seq":
            return (self.seq + step, self.batch)
        return (self.seq, self.batch + step)


CORE = ("batch", 0)
ACROSS = ("batch", 1)


def seq_axes(peers):
    return [("seq", k) for k in range((peers - 1).bit_length())]


def axis_orders(peers):
    bits = seq_axes(peers)
    x, z = bits[:1], bits[1:]
    y = [ACROSS]
    return [x + y + z, y + x + z, z + x + y, z + y + x, x + z + y, y + z + x]


def parts_of(rows, stages):
    found = []
    for _ in range(stages):
        halve = (rows // 2) % TILE == 0
        rows = rows // 2 if halve else rows
        found.append((rows, halve))
    return found


class Sems:
    def __init__(self, send, recv):
        self.send, self.recv, self.count = send, recv, 0

    def take(self):
        k = self.count
        self.count += 1
        return self.send.at[k], self.recv.at[k]


def rows_at(start, size):
    return pl.ds(pl.multiple_of(start, TILE), size)


def add_rows(into, one, at, other, other_at, rows):
    step = 32 if rows % 32 == 0 else TILE

    def body(i, carry):
        here = rows_at(at + i * step, step)
        there = rows_at(other_at + i * step, step)
        both = one[here].astype(jnp.float32) + other[there].astype(jnp.float32)
        into[here] = both.astype(into.dtype)
        return carry

    lax.fori_loop(0, rows // step, body, 0)


def sum_item(place, sems, buf, at, rows, order, inbox, used, total):
    low, plan = at, []
    for k, (axis, (part, halve)) in enumerate(zip(order, parts_of(rows, len(order)))):
        bit = place.bit(axis)
        keep, give = (low + bit * part, low + (1 - bit) * part) if halve else (low, low)
        copy = pltpu.make_async_remote_copy(
            buf.at[rows_at(give, part)],
            inbox.at[rows_at(used, part)],
            *sems.take(),
            device_id=place.partner(axis),
            device_id_type=MESH_ID,
        )
        copy.start()
        yield
        copy.wait()
        add_rows(total if k == len(order) - 1 else buf, buf, keep, inbox, used, part)
        plan.append((axis, keep, part, halve))
        used += part
        low = keep
    for axis, keep, part, halve in reversed(plan):
        if halve:
            here = rows_at(keep, part)
            copy = pltpu.make_async_remote_copy(
                total.at[here],
                total.at[here],
                *sems.take(),
                device_id=place.partner(axis),
                device_id_type=MESH_ID,
            )
            copy.start()
            yield
            copy.wait()


def dot(a, b, dims=((1,), (0,))):
    return lax.dot_general(a, b, (dims, ((), ())), preferred_element_type=jnp.float32)


NT = ((1,), (1,))
TN = ((0,), (0,))


def norm_parts(rows):
    center = rows - jnp.mean(rows, axis=-1, keepdims=True)
    spread = jnp.mean(center * center, axis=-1, keepdims=True)
    inverse = lax.rsqrt(spread + norm_eps)
    return center * inverse, inverse


def norm_back(grad, unit, inverse, gain):
    scaled = grad * gain
    along = jnp.mean(scaled * unit, axis=-1, keepdims=True)
    return inverse * (scaled - jnp.mean(scaled, axis=-1, keepdims=True) - unit * along)


def doc_ids(lengths, places):
    found = jnp.zeros(places.shape, jnp.int32)
    end = 0
    for k in range(lengths.shape[1]):
        end += lengths[0, k]
        found += (end <= places).astype(jnp.int32)
    return found


def as_row(ref):
    return ref[...].reshape(1, -1)


def places_down(first, rows):
    return first + lax.broadcasted_iota(jnp.int32, (rows, 1), 0)


def places_along(first, rows):
    return first + lax.broadcasted_iota(jnp.int32, (1, rows), 1)


def mask_of(ends, q_places, k_places):
    allowed = (doc_ids(ends, q_places) == doc_ids(ends, k_places)) & (k_places <= q_places)
    return jnp.where(allowed, 0.0, masked_low)


def first_half():
    return lax.broadcasted_iota(jnp.int32, (1, LANES), 1) < HD


def both_heads(pair):
    left = first_half()
    none = jnp.zeros_like(pair)
    return jnp.concatenate([jnp.where(left, pair, none), jnp.where(left, none, pair)], axis=0)


def own_columns(stacked):
    rows = stacked.shape[0] // 2
    return jnp.where(first_half(), stacked[:rows], stacked[rows:])


def lanes(p):
    return pl.ds(p * LANES, LANES)


def forward_kernel(
    nz, x_ref, e_ref, ends, gain_one1, shift_one1, qkv_bias1, proj_bias1, gain_two1, shift_two1, up_bias1, down_bias1,
    qkv_hbm, proj_hbm, up_hbm, down_hbm,
    layer_out, n1_all, q_out, attn_out, da_out, do_out, n2_out, g_out, du_out, dx_out, stats_out, small_out,
    x_all, qkv_w, proj_w, up_w, down_w, kv, mask, top, total, acc, two_q, res_acc, dh_acc,
    gain_one, shift_one, qkv_bias, proj_bias, gain_two, shift_two, up_bias, down_bias,
    up_send, up_recv, down_send, down_recv, side_send, side_recv, w_sem,
):
    rows, width = x_ref.shape
    pair = 2 * rows
    seq = lax.axis_index("seq")
    batch = lax.axis_index("batch")
    z = seq // 2
    x = seq % 2
    loads = [
        pltpu.make_async_copy(hbm, vmem, w_sem.at[k])
        for k, (hbm, vmem) in enumerate(
            [(qkv_hbm, qkv_w), (proj_hbm, proj_w), (up_hbm, up_w), (down_hbm, down_w)]
        )
    ]
    loads[0].start()
    barrier = pltpu.get_barrier_semaphore()
    has_up = z + 1 < nz
    has_down = z > 0
    above = (seq + 2, batch)
    below = (seq - 2, batch)
    beside = (seq + 1 - 2 * x, batch)

    @pl.when(has_up)
    def _():
        pl.semaphore_signal(barrier, inc=1, device_id=above, device_id_type=MESH_ID)

    @pl.when(has_down)
    def _():
        pl.semaphore_signal(barrier, inc=1, device_id=below, device_id_type=MESH_ID)

    pl.semaphore_signal(barrier, inc=1, device_id=beside, device_id_type=MESH_ID)
    pl.semaphore_wait(barrier, 1 + has_up.astype(jnp.int32) + has_down.astype(jnp.int32))
    for load in loads[1:]:
        load.start()

    def block(level, side):
        return x_all.at[rows_at((2 * level + side) * rows, rows)]

    def send(source, level, to, send_sem, recv_sem):
        return pltpu.make_async_remote_copy(
            source, block(level, x), send_sem.at[level], recv_sem.at[level], device_id=to, device_id_type=MESH_ID
        )

    def up_copy(source, level):
        return send(source, level, above, up_send, up_recv)

    def down_copy(source, level):
        return send(source, level, below, down_send, down_recv)

    def side_copy(source, level):
        return send(source, level, beside, side_send, side_recv)

    def wait_side(level):
        pltpu.make_async_remote_copy(
            x_ref, block(level, 1 - x), side_send.at[level], side_recv.at[level], device_id=beside, device_id_type=MESH_ID
        ).wait_recv()

    @pl.when(has_up)
    def _():
        up_copy(x_ref, z).start()

    side_copy(x_ref, z).start()

    @pl.when(has_down)
    def _():
        down_copy(x_ref, z).start()

    vectors = [gain_one, shift_one, qkv_bias, proj_bias, gain_two, shift_two, up_bias, down_bias]
    flats = [gain_one1, shift_one1, qkv_bias1, proj_bias1, gain_two1, shift_two1, up_bias1, down_bias1]
    for vector, flat in zip(vectors, flats):
        vector[...] = as_row(flat)
    x_all[rows_at(seq * rows, rows)] = x_ref[...]
    x32 = x_ref[...].astype(jnp.float32)
    unit_one, _ = norm_parts(x32)
    mine = (unit_one * gain_one[...] + shift_one[...]).astype(jnp.bfloat16)
    top[...] = jnp.full(top.shape, masked_low, jnp.float32)
    total[...] = jnp.zeros(total.shape, jnp.float32)
    acc[...] = jnp.zeros(acc.shape, jnp.float32)
    loads[0].wait()
    q = (dot(mine, qkv_w[:, :width]) + qkv_bias[:, :width]).astype(jnp.bfloat16)
    q = q * jnp.asarray(1.0 / math.sqrt(HD), jnp.bfloat16)
    q_out[...] = q
    for p in range(HEADS // 2):
        two_q[p] = both_heads(q[:, p * LANES : (p + 1) * LANES])

    def pass_on(d):
        @pl.when(z >= d)
        def _():
            level = z - d
            up_copy(x_ref, level).wait_recv()

            @pl.when(has_up)
            def _():
                up_copy(block(level, x), level).start()

            side_copy(block(level, x), level).start()

        @pl.when(z + d < nz)
        def _():
            level = z + d
            down_copy(x_ref, level).wait_recv()

            @pl.when(has_down)
            def _():
                down_copy(block(level, x), level).start()

            side_copy(block(level, x), level).start()

    def normalize(level):
        here = rows_at(level * pair, pair)
        unit, _ = norm_parts(x_all[here].astype(jnp.float32))
        n1 = (unit * gain_one[...] + shift_one[...]).astype(jnp.bfloat16)
        n1_all[here] = n1
        return n1

    def attend(level):
        wait_side(level)
        n1 = normalize(level)
        kv[...] = (dot(n1, qkv_w[:, width:]) + qkv_bias[:, width:]).astype(jnp.bfloat16)
        one = mask_of(ends, places_down(seq * rows, rows), places_along(level * pair, pair))
        mask[:rows] = one
        mask[rows:] = one
        for p in range(HEADS // 2):
            k_pair = kv[:, p * LANES : (p + 1) * LANES]
            v_pair = kv[:, width + p * LANES : width + (p + 1) * LANES]
            s = dot(two_q[p], k_pair, NT)
            low = mask[...]
            before = top[p][:, :1]
            newer = jnp.maximum(before, jnp.max(jnp.abs(s) + low, axis=1, keepdims=True))
            low = low - newer
            plus = jnp.exp(low + s)
            minus = jnp.exp(low - s)
            keep = jnp.exp(before - newer)
            total[p] = total[p] * keep + jnp.sum(plus + minus, axis=1, keepdims=True)
            top[p] = jnp.broadcast_to(newer, (pair, LANES))
            out = own_columns(dot((plus - minus).astype(jnp.bfloat16), v_pair))
            keep = own_columns(jnp.broadcast_to(keep, (pair, LANES)))
            here = slice(p * LANES, (p + 1) * LANES)
            acc[:, here] = acc[:, here] * keep + out

    def level_step(d, carry):
        @pl.when(d + 1 < nz)
        def _():
            pass_on(d + 1)

        @pl.when(z >= d)
        def _():
            attend(z - d)

        @pl.when((d > 0) & (z + d < nz))
        def _():
            wait_side(z + d)
            normalize(z + d)

        return carry

    lax.fori_loop(0, nz, level_step, 0)

    column = lax.broadcasted_iota(jnp.int32, (1, LANES), 1)
    log_total = jnp.zeros((rows, LANES), jnp.float32)
    for p in range(HEADS // 2):
        here = slice(p * LANES, (p + 1) * LANES)
        acc[:, here] = acc[:, here] / own_columns(total[p])
        lse = top[p] + jnp.log(total[p])
        log_total = jnp.where(column == 2 * p, lse[:rows], log_total)
        log_total = jnp.where(column == 2 * p + 1, lse[rows:], log_total)
    attn = acc[...].astype(jnp.bfloat16)
    attn_out[...] = attn
    loads[1].wait()
    resid = x32 + dot(attn, proj_w[...]) + proj_bias[...]
    unit, inverse = norm_parts(resid)
    n2 = (unit * gain_two[...] + shift_two[...]).astype(jnp.bfloat16)
    n2_out[...] = n2
    res_acc[...] = resid + down_bias[...]
    dh_acc[...] = jnp.zeros(dh_acc.shape, jnp.float32)
    loads[2].wait()
    loads[3].wait()
    slope = math.sqrt(2.0 / math.pi)

    def ff_step(t, carry):
        here = pl.ds(pl.multiple_of(t * FF_TILE, FF_TILE), FF_TILE)
        u = dot(n2_out[...], up_w[:, here]) + up_bias[:, here]
        square = u * u
        bend = jnp.tanh(slope * (u + 0.044715 * (square * u)))
        half = 0.5 * (1.0 + bend)
        g = (u * half).astype(jnp.bfloat16)
        slant = half + (0.5 * u) * (1.0 - bend * bend) * (slope * (1.0 + 3.0 * 0.044715 * square))
        g_out[:, here] = g
        res_acc[...] += dot(g, down_w[here])
        du32 = dot(e_ref[...], down_w[here], NT) * slant
        du = du32.astype(jnp.bfloat16)
        du_out[:, here] = du
        small_out[pl.ds(4 + t, 1)] = jnp.sum(du.astype(jnp.float32), axis=0, keepdims=True)
        dh_acc[...] += dot(du, up_w[:, here], NT)
        return carry

    lax.fori_loop(0, up_w.shape[1] // FF_TILE, ff_step, 0)
    layer_out[...] = res_acc[...].astype(jnp.bfloat16)
    dh = dh_acc[...]
    grad_rows = e_ref[...].astype(jnp.float32)
    dx = grad_rows + norm_back(dh, unit, inverse, gain_two[...])
    dx_out[...] = dx
    da = dx.astype(jnp.bfloat16)
    da_out[...] = da
    do = dot(da, proj_w[...], NT).astype(jnp.bfloat16)
    do_out[...] = do
    product = do.astype(jnp.float32) * acc[...]
    delta = jnp.zeros((rows, LANES), jnp.float32)
    left = first_half()
    for p in range(HEADS // 2):
        here = product[:, p * LANES : (p + 1) * LANES]
        one = jnp.sum(jnp.where(left, here, 0.0), axis=1, keepdims=True)
        two = jnp.sum(jnp.where(left, 0.0, here), axis=1, keepdims=True)
        delta = jnp.where(column == 2 * p, one, delta)
        delta = jnp.where(column == 2 * p + 1, two, delta)
    stats_out[0] = log_total
    stats_out[1] = delta
    small_out[0:1] = jnp.sum(dh * unit, axis=0, keepdims=True)
    small_out[1:2] = jnp.sum(dh, axis=0, keepdims=True)
    small_out[2:3] = jnp.sum(grad_rows, axis=0, keepdims=True)
    small_out[3:4] = jnp.sum(da.astype(jnp.float32), axis=0, keepdims=True)

    side_copy(x_ref, z).wait_send()

    @pl.when(has_up)
    def _():
        up_copy(x_ref, z).wait_send()

    @pl.when(has_down)
    def _():
        down_copy(x_ref, z).wait_send()

    def sent(d, carry):
        @pl.when(z >= d)
        def _():
            side_copy(x_ref, z - d).wait_send()

            @pl.when(has_up)
            def _():
                up_copy(x_ref, z - d).wait_send()

        @pl.when(z + d < nz)
        def _():
            side_copy(x_ref, z + d).wait_send()

            @pl.when(has_down)
            def _():
                down_copy(x_ref, z + d).wait_send()

        return carry

    lax.fori_loop(1, nz, sent, 0)


def run_forward(x, e, lengths, gain_one, shift_one, qkv_weight, qkv_bias, proj_weight, proj_bias, gain_two, shift_two, up_weight, up_bias, down_weight, down_bias, peers):
    rows, width = x.shape
    hidden = up_weight.shape[1]
    nz = peers // 2
    bf, f32 = jnp.bfloat16, jnp.float32
    vmem = pl.BlockSpec(memory_space=pltpu.VMEM)
    smem = pl.BlockSpec(memory_space=pltpu.SMEM)
    hbm = pl.BlockSpec(memory_space=pl.ANY)
    dma = pltpu.SemaphoreType.DMA
    outs = [
        ((rows, width), bf), ((peers * rows, width), bf), ((rows, width), bf), ((rows, width), bf), ((rows, width), bf),
        ((rows, width), bf), ((rows, width), bf), ((rows, hidden), bf), ((rows, hidden), bf), ((rows, width), f32),
        ((2, rows, LANES), f32), ((4 + hidden // width, width), f32),
    ]
    vectors = [gain_one, shift_one, qkv_bias, proj_bias, gain_two, shift_two, up_bias, down_bias]
    return pl.pallas_call(
        functools.partial(forward_kernel, nz),
        out_shape=[jax.ShapeDtypeStruct(*o) for o in outs],
        in_specs=[vmem, vmem, smem] + [vmem] * 8 + [hbm] * 4,
        out_specs=[vmem] * len(outs),
        scratch_shapes=[
            pltpu.VMEM((peers * rows, width), bf),
            pltpu.VMEM(qkv_weight.shape, bf),
            pltpu.VMEM(proj_weight.shape, bf),
            pltpu.VMEM(up_weight.shape, bf),
            pltpu.VMEM(down_weight.shape, bf),
            pltpu.VMEM((2 * rows, 2 * width), bf),
            pltpu.VMEM((2 * rows, 2 * rows), f32),
            pltpu.VMEM((HEADS // 2, 2 * rows, LANES), f32),
            pltpu.VMEM((HEADS // 2, 2 * rows, LANES), f32),
            pltpu.VMEM((rows, width), f32),
            pltpu.VMEM((HEADS // 2, 2 * rows, LANES), bf),
            pltpu.VMEM((rows, width), f32),
            pltpu.VMEM((rows, width), f32),
            *[pltpu.VMEM((1, v.shape[0]), f32) for v in vectors],
            dma((nz,)), dma((nz,)), dma((nz,)), dma((nz,)), dma((nz,)), dma((nz,)), dma((4,)),
        ],
        compiler_params=pltpu.CompilerParams(collective_id=0, has_side_effects=True, vmem_limit_bytes=60 * 2**20),
        cost_estimate=pl.CostEstimate(flops=10**9, bytes_accessed=2 * 10**7, transcendentals=10**6),
    )(x, e, lengths, *vectors, qkv_weight, proj_weight, up_weight, down_weight)


def backward_kernel(
    nz, items, orders, schedule,
    x_ref, e_ref, ends, gain_flat, bias_flat, n1_all, q_ref, attn_ref, da_ref, do_ref, n2_ref, g_ref, du_ref, dx_ref,
    stats_ref, first_small, qkv_hbm,
    input_grad, qkv_out, proj_out, up_out, down_out, small_out,
    qkv_w, buf, inbox, total, do_all, rows_all, g_cat, e_cat, n2_cat, du_cat, attn_cat, da_cat, n1_cat, dqkv_cat,
    two_q, two_do, two_k, two_v, lse_cols, delta_cols, kv, n1_held, mask, dq, dk, dv, small_in, gain_one, qkv_bias,
    down_send, down_recv, side_send, side_recv, ssem, rsem, lsem,
):
    rows, width = x_ref.shape
    pair = 2 * rows
    place = Place()
    seq, batch = place.seq, place.batch
    z = seq // 2
    x = seq % 2
    core = place.bit(CORE)
    sems = Sems(ssem, rsem)
    local = Sems(lsem, lsem)
    load = pltpu.make_async_copy(qkv_hbm, qkv_w, local.take()[0])
    load.start()
    small_axes = [CORE, ACROSS] + seq_axes(2 * nz)
    has_up = z + 1 < nz
    has_down = z > 0
    above = (seq + 2, batch)
    below = (seq - 2, batch)
    beside = (seq + 1 - 2 * x, batch)
    barrier = pltpu.get_barrier_semaphore()
    for axis in small_axes:
        pl.semaphore_signal(barrier, inc=1, device_id=place.partner(axis), device_id_type=MESH_ID)

    @pl.when(has_up)
    def _():
        pl.semaphore_signal(barrier, inc=1, device_id=above, device_id_type=MESH_ID)

    @pl.when(has_down)
    def _():
        pl.semaphore_signal(barrier, inc=1, device_id=below, device_id_type=MESH_ID)

    gain_one[...] = as_row(gain_flat)
    qkv_bias[...] = as_row(bias_flat)
    for k in range(2):
        rows_all[seq, k * TILE : (k + 1) * TILE] = stats_ref[k].T[:TILE]
    pl.semaphore_wait(barrier, len(small_axes) + has_up.astype(jnp.int32) + has_down.astype(jnp.int32))

    def cols(half, size):
        return pl.ds(pl.multiple_of(half * size, LANES), size)

    def to_core(source, into):
        return pltpu.make_async_remote_copy(
            source, into.at[rows:], *sems.take(), device_id=place.partner(CORE), device_id_type=MESH_ID
        )

    def keep_own(source, into):
        return pltpu.make_async_copy(source, into.at[:rows], local.take()[0])

    def exchange(ref, into, halved):
        size = into.shape[1]
        give = ref.at[:, cols(1 - core, size)] if halved else ref
        keep = ref.at[:, cols(core, size)] if halved else ref
        copies = [to_core(give, into), keep_own(keep, into)]
        for copy in copies:
            copy.start()
        return copies

    def done(copies):
        for copy in copies:
            copy.wait()

    down_parts = exchange(g_ref, g_cat, True) + exchange(e_ref, e_cat, False)
    up_parts = exchange(n2_ref, n2_cat, False) + exchange(du_ref, du_cat, True)

    def do_block(level, side):
        return do_all.at[rows_at((2 * level + side) * rows, rows)]

    def do_copies(level, side, to, send_sem, recv_sem, own=False):
        source = do_ref if own else do_block(level, side)
        stat = rows_all.at[2 * level + side]
        return [
            pltpu.make_async_remote_copy(
                source, do_block(level, side), send_sem.at[level, 0], recv_sem.at[level, 0], device_id=to, device_id_type=MESH_ID
            ),
            pltpu.make_async_remote_copy(
                stat, stat, send_sem.at[level, 1], recv_sem.at[level, 1], device_id=to, device_id_type=MESH_ID
            ),
        ]

    def down_copies(level, own=False):
        return do_copies(level, x, below, down_send, down_recv, own)

    def side_copies(level, own=False):
        return do_copies(level, x, beside, side_send, side_recv, own)

    def begin(copies):
        for copy in copies:
            copy.start()

    @pl.when(has_down)
    def _():
        begin(down_copies(z, True))

    begin(side_copies(z, True))
    do_all[rows_at(seq * rows, rows)] = do_ref[...]

    spread = [1]

    def spread_until(last):
        while spread[0] <= min(last, nz - 1):
            d = spread[0]
            spread[0] += 1

            @pl.when(z + d < nz)
            def _():
                level = z + d
                for copy in down_copies(level):
                    copy.wait_recv()

                @pl.when(has_down)
                def _():
                    begin(down_copies(level))

                begin(side_copies(level))

    def spread_end():
        def sent(copies):
            for copy in copies:
                copy.wait_send()

        sent(side_copies(z, True))

        @pl.when(has_down)
        def _():
            sent(down_copies(z, True))

        def each(level, carry):
            sent(side_copies(level))

            @pl.when(has_down)
            def _():
                sent(down_copies(level))

            return carry

        lax.fori_loop(z + 1, nz, each, 0)

    slots = []
    at = used = 0
    for size, kind, _ in items:
        slots.append((at, size, orders[kind], used))
        at += size
        used += sum(part for part, _ in parts_of(size, len(orders[kind])))
    places = [(name, r) for _, _, (name, r) in items]

    def destination(name, r, size):
        half = width // 2
        if name == "down":
            return down_out.at[rows_at(core * down_out.shape[0] // 2 + r, size)]
        if name[:2] == "up":
            return up_out.at[r : r + size, pl.ds(pl.multiple_of((core * (up_out.shape[1] // width // 2) + int(name[2:])) * width, width), width)]
        if name == "proj":
            return proj_out.at[rows_at(core * half + r, size)]
        return qkv_out.at[rows_at(core * half + r, size), int(name[3:]) * width : (int(name[3:]) + 1) * width]

    ready = set()

    def item_task(k):
        at, size, order, used = slots[k]
        name, r = places[k]
        if name[:2] not in ready:
            ready.add(name[:2])
            done(parts.get(name[:2], []))
        left, right = operands(name)
        buf[at : at + size] = dot(left[:, r : r + size], right, TN).astype(jnp.bfloat16)
        yield from sum_item(place, sems, buf, at, size, order, inbox, used, total)
        there = destination(name, r, size)
        here = total.at[rows_at(at, size)]
        keep = pltpu.make_async_copy(here, there, local.take()[0])
        give = pltpu.make_async_remote_copy(here, there, *sems.take(), device_id=place.partner(CORE), device_id_type=MESH_ID)
        keep.start()
        give.start()
        leaving.extend([keep, give])

    def small_task():
        for k, axis in enumerate(small_axes):
            copy = pltpu.make_async_remote_copy(
                small_out, small_in.at[k], *sems.take(), device_id=place.partner(axis), device_id_type=MESH_ID
            )
            copy.start()
            yield
            copy.wait()
            small_out[...] += small_in[k]

    leaving = []

    def operands(name):
        if name == "down":
            return g_cat, e_cat[...]
        if name == "proj":
            return attn_cat, da_cat[...]
        j = int(name[-1])
        block = slice(j * width, (j + 1) * width)
        return (n2_cat, du_cat[:, block]) if name[:2] == "up" else (n1_cat, dqkv_cat[:, block])

    small_out[:8] = first_small[...]
    own_n1 = rows_at(seq * rows, rows)
    parts = {
        "do": down_parts,
        "up": up_parts,
        "pr": exchange(attn_ref, attn_cat, True) + exchange(da_ref, da_cat, False),
        "qk": exchange(n1_all.at[own_n1], n1_cat, True),
    }

    load.wait()
    scale = jnp.asarray(1.0 / math.sqrt(HD), jnp.bfloat16)

    chunk_sem = local.take()[0]

    def n1_chunk(level):
        copy = pltpu.make_async_copy(n1_all.at[rows_at(level * pair, pair)], n1_held, chunk_sem)
        copy.start()
        copy.wait()
        return n1_held[...]

    def prepare():
        n1_chunk(z)
        mine = n1_held[rows_at(x * rows, rows)]
        own_kv = (dot(mine, qkv_w[:, width:]) + qkv_bias[:, width:]).astype(jnp.bfloat16)
        for p in range(HEADS // 2):
            here = slice(p * LANES, (p + 1) * LANES)
            two_q[p] = both_heads(q_ref[:, here])
            two_do[p] = both_heads(do_ref[:, here])
            two_k[p] = both_heads(own_kv[:, here])
            two_v[p] = both_heads(own_kv[:, width + p * LANES : width + (p + 1) * LANES])
            for k, into in enumerate((lse_cols, delta_cols)):
                for h in range(2):
                    column = stats_ref[k, :, 2 * p + h : 2 * p + h + 1]
                    into[p, h * rows : (h + 1) * rows] = jnp.broadcast_to(column, (rows, LANES))
        dq[...] = jnp.zeros(dq.shape, jnp.float32)
        dk[...] = jnp.zeros(dk.shape, jnp.float32)
        dv[...] = jnp.zeros(dv.shape, jnp.float32)

    def columns_of(p):
        return pl.ds(pl.multiple_of(p * LANES, LANES), LANES)

    def query_step(level):
        n1 = n1_chunk(level)
        kv[...] = (dot(n1, qkv_w[:, width:]) + qkv_bias[:, width:]).astype(jnp.bfloat16)
        one = mask_of(ends, places_down(seq * rows, rows), places_along(level * pair, pair))
        mask[:rows] = one
        mask[rows:] = one

        def each(p, carry):
            k_pair = kv[:, columns_of(p)]
            v_pair = kv[:, columns_of(p + HEADS // 2)]
            s = dot(two_q[p], k_pair, NT)
            along = dot(two_do[p], v_pair, NT)
            low = mask[...] - lse_cols[p][:, :1]
            plus = jnp.exp(low + s)
            minus = jnp.exp(low - s)
            ds = ((plus + minus) * along - (plus - minus) * delta_cols[p][:, :1]).astype(jnp.bfloat16)
            dq[:, columns_of(p)] += own_columns(dot(ds, k_pair))
            return carry

        lax.fori_loop(0, HEADS // 2, each, 0, unroll=UNROLL)

    def key_step(level):
        side = 1 - x
        for copy in do_copies(level, side, beside, side_send, side_recv):
            copy.wait_recv()
        here = rows_at(level * pair, pair)
        n1 = n1_chunk(level)
        kv[:, :width] = (dot(n1, qkv_w[:, :width]) + qkv_bias[:, :width]).astype(jnp.bfloat16) * scale
        one = mask_of(ends, places_along(level * pair, pair), places_down(seq * rows, rows))
        mask[:rows] = one
        mask[rows:] = one

        def stat(row):
            both = [rows_all[2 * level + k, pl.ds(row, 1)] for k in range(2)]
            return jnp.concatenate(both, axis=1)

        def stat_rows(k, p):
            both = [jnp.broadcast_to(stat(k * TILE + 2 * p + h), (rows, pair)) for h in range(2)]
            return jnp.concatenate(both, axis=0)

        def each(p, carry):
            q_pair = kv[:, columns_of(p)]
            do_pair = do_all[here, columns_of(p)]
            s = dot(two_k[p], q_pair, NT)
            along = dot(two_v[p], do_pair, NT)
            low = mask[...] - stat_rows(0, p)
            plus = jnp.exp(low + s)
            minus = jnp.exp(low - s)
            signed = plus - minus
            ds = ((plus + minus) * along - signed * stat_rows(1, p)).astype(jnp.bfloat16)
            dk[:, columns_of(p)] += own_columns(dot(ds, q_pair))
            dv[:, columns_of(p)] += own_columns(dot(signed.astype(jnp.bfloat16), do_pair))
            return carry

        lax.fori_loop(0, HEADS // 2, each, 0, unroll=UNROLL)

    def one_step(t):
        @pl.when(t <= z)
        def _():
            query_step(z - t)

        @pl.when(t > z)
        def _():
            key_step(t - 1)

    def steps_piece(first, last):
        def piece():
            spread_until(last)
            if last - first == 1:
                one_step(first)
            else:

                def body(t, carry):
                    one_step(t)
                    return carry

                lax.fori_loop(first, last, body, 0)

        return piece

    def finish():
        dqkv = jnp.concatenate(
            [
                (dq[...] * (1.0 / math.sqrt(HD))).astype(jnp.bfloat16),
                dk[...].astype(jnp.bfloat16),
                dv[...].astype(jnp.bfloat16),
            ],
            axis=1,
        )
        dqkv_cat[:rows] = dqkv
        send = to_core(dqkv_cat.at[:rows], dqkv_cat)
        send.start()
        dh = dot(dqkv, qkv_w[...], NT)
        unit, inverse = norm_parts(x_ref[...].astype(jnp.float32))
        input_grad[...] = (dx_ref[...] + norm_back(dh, unit, inverse, gain_one[...])).astype(jnp.bfloat16)
        sums = jnp.sum(dqkv.astype(jnp.float32), axis=0, keepdims=True)
        for k in range(3):
            small_out[8 + k : 9 + k] = sums[:, k * width : (k + 1) * width]
        small_out[11:12] = jnp.sum(dh * unit, axis=0, keepdims=True)
        small_out[12:13] = jnp.sum(dh, axis=0, keepdims=True)
        small_out[13:16] = jnp.zeros((3, width), jnp.float32)
        parts["qk"].append(send)

    groups = min(nz + 1, GROUPS)
    cuts = [(nz + 1) * k // groups for k in range(groups + 1)]
    pieces = [prepare] + [steps_piece(a, b) for a, b in zip(cuts, cuts[1:])] + [finish]
    tasks = [item_task(k) for k in range(len(items))] + [small_task()]
    for token in schedule:
        if token < 0:
            pieces[-1 - token]()
        else:
            next(tasks[token], None)
    for copy in leaving:
        copy.wait()
    spread_end()


def in_turns(items, counts, n_pieces):
    early = [k for k, (_, _, (name, _)) in enumerate(items) if name[:3] != "qkv"]
    late = [k for k in range(len(counts)) if k not in early]
    tokens, piece = [], 0
    for waiting in (early, late):
        live = []
        while live or waiting:
            live, waiting = live + waiting[:3], waiting[3:]
            for k in live:
                tokens.append(k)
                if len(tokens) % PACE == 0 and piece < n_pieces:
                    piece += 1
                    tokens.append(-piece)
            live = [k for k in live if tokens.count(k) < counts[k]]
        while piece < n_pieces:
            piece += 1
            tokens.append(-piece)
    return tokens


def plan_items(width, hidden):
    half = width // 2

    def cut(name, size):
        return [(min(ITEM, size - r), (name, r)) for r in range(0, size, ITEM)]

    found = cut("down", hidden // 2)
    for j in range(hidden // 2 // width):
        found += cut(f"up{j}", width)
    found += cut("proj", half)
    for j in range(3):
        found += cut(f"qkv{j}", half)
    return [(size, int(KINDS[k % len(KINDS)]), where) for k, (size, where) in enumerate(found)]


def run_backward(x, e, lengths, gain_one, qkv_weight, qkv_bias, kept, peers):
    n1_all, q, attn, da, do, n2, g, du, dx, stats, small = kept
    rows, width = x.shape
    hidden = g.shape[1]
    nz = peers // 2
    bf, f32 = jnp.bfloat16, jnp.float32
    orders = axis_orders(peers)
    stages = 2 + len(seq_axes(peers))
    items = plan_items(width, hidden)
    counts = [parts_of(size, len(orders[kind])) for size, kind, _ in items]
    used = sum(part for count in counts for part, _ in count)
    height = sum(size for size, _, _ in items)
    turns = [1 + len(count) + sum(halve for _, halve in count) for count in counts] + [1 + stages]
    n_pieces = 2 + min(nz + 1, GROUPS)
    schedule = SCHEDULE
    if sorted(schedule) != sorted([k for k, n in enumerate(turns) for _ in range(n)] + [-1 - k for k in range(n_pieces)]):
        schedule = in_turns(items, turns, n_pieces)
    copies = sum(1 + len(count) + sum(halve for _, halve in count) for count in counts) + stages + 8
    vmem = pl.BlockSpec(memory_space=pltpu.VMEM)
    smem = pl.BlockSpec(memory_space=pltpu.SMEM)
    hbm = pl.BlockSpec(memory_space=pl.ANY)
    dma = pltpu.SemaphoreType.DMA
    out = jax.ShapeDtypeStruct
    stack = (HEADS // 2, 2 * rows, LANES)
    return pl.pallas_call(
        functools.partial(backward_kernel, nz, items, orders, schedule),
        out_shape=[
            out((rows, width), bf), out((width, 3 * width), bf), out((width, width), bf), out((width, hidden), bf),
            out((hidden, width), bf), out((16, width), f32),
        ],
        in_specs=[vmem, hbm, smem, vmem, vmem, hbm, vmem, hbm, hbm, vmem, hbm, hbm, hbm, vmem, vmem, vmem, hbm],
        out_specs=[vmem, hbm, hbm, hbm, hbm, vmem],
        scratch_shapes=[
            pltpu.VMEM(qkv_weight.shape, bf),
            pltpu.VMEM((height, width), bf),
            pltpu.VMEM((used, width), bf),
            pltpu.VMEM((height, width), bf),
            pltpu.VMEM((peers * rows, width), bf),
            pltpu.VMEM((peers, 2 * TILE, LANES), f32),
            pltpu.VMEM((2 * rows, hidden // 2), bf),
            pltpu.VMEM((2 * rows, width), bf),
            pltpu.VMEM((2 * rows, width), bf),
            pltpu.VMEM((2 * rows, hidden // 2), bf),
            pltpu.VMEM((2 * rows, width // 2), bf),
            pltpu.VMEM((2 * rows, width), bf),
            pltpu.VMEM((2 * rows, width // 2), bf),
            pltpu.VMEM((2 * rows, 3 * width), bf),
            pltpu.VMEM(stack, bf), pltpu.VMEM(stack, bf), pltpu.VMEM(stack, bf), pltpu.VMEM(stack, bf),
            pltpu.VMEM(stack, f32), pltpu.VMEM(stack, f32),
            pltpu.VMEM((2 * rows, 2 * width), bf),
            pltpu.VMEM((2 * rows, width), bf),
            pltpu.VMEM((2 * rows, 2 * rows), f32),
            pltpu.VMEM((rows, width), f32), pltpu.VMEM((rows, width), f32), pltpu.VMEM((rows, width), f32),
            pltpu.VMEM((stages, 16, width), f32),
            pltpu.VMEM((1, width), f32), pltpu.VMEM((1, 3 * width), f32),
            dma((nz, 2)), dma((nz, 2)), dma((nz, 2)), dma((nz, 2)),
            dma((copies,)), dma((copies,)), dma((len(items) + 10,)),
        ],
        compiler_params=pltpu.CompilerParams(collective_id=1, has_side_effects=True, vmem_limit_bytes=62 * 2**20),
    )(x, e, lengths, gain_one, qkv_bias, n1_all, q, attn, da, do, n2, g, du, dx, stats, small, qkv_weight)


def per_device(
    inputs,
    cotangent,
    doc_lengths,
    gain_one,
    shift_one,
    qkv_weight,
    qkv_bias,
    proj_weight,
    proj_bias,
    gain_two,
    shift_two,
    up_weight,
    up_bias,
    down_weight,
    down_bias,
):
    peers = lax.axis_size("seq")
    width = inputs.shape[2]
    layer_out, *kept = run_forward(
        inputs[0], cotangent[0], doc_lengths, gain_one, shift_one, qkv_weight, qkv_bias, proj_weight, proj_bias, gain_two, shift_two,
        up_weight, up_bias, down_weight, down_bias, peers,
    )
    input_grad, qkv, proj, up, down, small = run_backward(
        inputs[0], cotangent[0], doc_lengths, gain_one, qkv_weight, qkv_bias, kept, peers
    )
    wide = jnp.float32
    return (
        layer_out[None],
        input_grad[None],
        small[11],
        small[12],
        qkv.astype(wide),
        small[8:11].reshape(-1),
        proj.astype(wide),
        small[3],
        small[0],
        small[1],
        up.astype(wide),
        small[4:8].reshape(-1),
        down.astype(wide),
        small[2],
    )


def solution(mesh):
    in_specs = (
        P("batch", "seq", None),
        P("batch", "seq", None),
        P("batch", None),
        P(),
        P(),
        P(),
        P(),
        P(),
        P(),
        P(),
        P(),
        P(),
        P(),
        P(),
        P(),
    )
    out_specs = (
        P("batch", "seq", None),
        P("batch", "seq", None),
        P(),
        P(),
        P(),
        P(),
        P(),
        P(),
        P(),
        P(),
        P(),
        P(),
        P(),
        P(),
    )
    return jax.shard_map(
        per_device, mesh=mesh, in_specs=in_specs, out_specs=out_specs, check_vma=False
    )
```

```python
import functools
import math

import jax
import jax.numpy as jnp
from jax import lax
from jax.experimental import pallas as pl
from jax.experimental.pallas import tpu as pltpu
from jax.sharding import PartitionSpec as P

HEADS = 12
HD = 64


norm_eps = 1e-05
masked_low = -1e30


MESH_ID = pl.DeviceIdType.MESH
TILE = 16
LANES = 128
FF_TILE = 768
ITEM = 256
KINDS = "032102111511030001100"
GROUPS = 5
PACE = 8
UNROLL = 6
K2_LIMIT = 45
KEPT = (0,)
WIDEN = 128 * 2304
SMALL_ROWS = ((11, 1), (12, 1), (8, 3), (3, 1), (0, 1), (1, 1), (4, 4), (2, 1))
SCHEDULE = (
    -1, 0, 10, 12, 6, 5, 11, -2, 13, 8, 3, -3, 11, 1, 12, 13, 7, -4, 9, 2, 3, 1, 5, 8, 11, -5, 4, 0, 3, -6, 10, 8, 7,
    13, 2, 4, 0, 3, 12, 11, 8, 5, 6, -7, 20, 14, 3, 17, 4, 7, 0, 3, 5, 11, 16, 15, 12, 19, 1, 7, 8, 9, 4, 6, 5, 14,
    18, 3, 10, 9, 1, 13, 14, 6, 16, 7, 4, 5, 11, 15, 20, 14, 17, 18, 19, 7, 15, 4, 3, 10, 6, 17, 8, 9, 13, 12, 7, 16,
    4, 0, 6, 15, 9, 17, 1, 20, 7, 14, 2, 19, 8, 16, 1, 11, 18, 2, 10, 12, 8, 16, 0, 17, 4, 2, 1, 9, 14, 19, 18, 15, 6,
    17, 5, 12, 10, 14, 20, 16, 0, 12, 13, 9, 11, 20, 10, 2, 19, 0, 16, 10, 17, 18, 13, 14, 18, 19, 6, 20, 8, 5, 16,
    15, 4, 18, 13, 3, 19, 9, 0, 10, 2, 1, 2, 14, 18, 17, 19, 1, 16, 15, 6, 7, 12, 5, 18, 9, 2, 15, 11,
)


class Place:
    def __init__(self):
        self.seq = lax.axis_index("seq")
        self.batch = lax.axis_index("batch")

    def bit(self, axis):
        name, k = axis
        return ((self.seq if name == "seq" else self.batch) // (1 << k)) % 2

    def partner(self, axis):
        name, k = axis
        step = (1 << k) * (1 - 2 * self.bit(axis))
        if name == "seq":
            return (self.seq + step, self.batch)
        return (self.seq, self.batch + step)


CORE = ("batch", 0)
ACROSS = ("batch", 1)


def seq_axes(peers):
    return [("seq", k) for k in range((peers - 1).bit_length())]


def axis_orders(peers):
    bits = seq_axes(peers)
    x, z = bits[:1], bits[1:]
    y = [ACROSS]
    return [x + y + z, y + x + z, z + x + y, z + y + x, x + z + y, y + z + x]


def parts_of(rows, stages):
    found = []
    for _ in range(stages):
        halve = (rows // 2) % TILE == 0
        rows = rows // 2 if halve else rows
        found.append((rows, halve))
    return found


class Sems:
    def __init__(self, send, recv):
        self.send, self.recv, self.count = send, recv, 0

    def take(self):
        k = self.count
        self.count += 1
        return self.send.at[k], self.recv.at[k]


def rows_at(start, size):
    return pl.ds(pl.multiple_of(start, TILE), size)


def add_rows(into, one, at, other, other_at, rows):
    step = 32 if rows % 32 == 0 else TILE

    def body(i, carry):
        here = rows_at(at + i * step, step)
        there = rows_at(other_at + i * step, step)
        both = one[here].astype(jnp.float32) + other[there].astype(jnp.float32)
        into[here] = both.astype(into.dtype)
        return carry

    lax.fori_loop(0, rows // step, body, 0)


def sum_item(place, sems, buf, at, rows, order, inbox, used, total):
    low, plan = at, []
    for k, (axis, (part, halve)) in enumerate(zip(order, parts_of(rows, len(order)))):
        bit = place.bit(axis)
        keep, give = (low + bit * part, low + (1 - bit) * part) if halve else (low, low)
        copy = pltpu.make_async_remote_copy(
            buf.at[rows_at(give, part)],
            inbox.at[rows_at(used, part)],
            *sems.take(),
            device_id=place.partner(axis),
            device_id_type=MESH_ID,
        )
        copy.start()
        yield
        copy.wait()
        add_rows(total if k == len(order) - 1 else buf, buf, keep, inbox, used, part)
        plan.append((axis, keep, part, halve))
        used += part
        low = keep
    for axis, keep, part, halve in reversed(plan):
        if halve:
            here = rows_at(keep, part)
            copy = pltpu.make_async_remote_copy(
                total.at[here],
                total.at[here],
                *sems.take(),
                device_id=place.partner(axis),
                device_id_type=MESH_ID,
            )
            copy.start()
            yield
            copy.wait()


def dot(a, b, dims=((1,), (0,))):
    return lax.dot_general(a, b, (dims, ((), ())), preferred_element_type=jnp.float32)


NT = ((1,), (1,))
TN = ((0,), (0,))


def norm_parts(rows):
    center = rows - jnp.mean(rows, axis=-1, keepdims=True)
    spread = jnp.mean(center * center, axis=-1, keepdims=True)
    inverse = lax.rsqrt(spread + norm_eps)
    return center * inverse, inverse


def norm_back(grad, unit, inverse, gain):
    scaled = grad * gain
    along = jnp.mean(scaled * unit, axis=-1, keepdims=True)
    return inverse * (scaled - jnp.mean(scaled, axis=-1, keepdims=True) - unit * along)


def doc_ids(lengths, places):
    found = jnp.zeros(places.shape, jnp.int32)
    end = 0
    for k in range(lengths.shape[1]):
        end += lengths[0, k]
        found += (end <= places).astype(jnp.int32)
    return found


def as_row(ref):
    return ref[...].reshape(1, -1)


def places_down(first, rows):
    return first + lax.broadcasted_iota(jnp.int32, (rows, 1), 0)


def places_along(first, rows):
    return first + lax.broadcasted_iota(jnp.int32, (1, rows), 1)


def mask_of(ends, q_places, k_places):
    allowed = (doc_ids(ends, q_places) == doc_ids(ends, k_places)) & (k_places <= q_places)
    return jnp.where(allowed, 0.0, masked_low)


def first_half():
    return lax.broadcasted_iota(jnp.int32, (1, LANES), 1) < HD


def both_heads(pair):
    left = first_half()
    none = jnp.zeros_like(pair)
    return jnp.concatenate([jnp.where(left, pair, none), jnp.where(left, none, pair)], axis=0)


def own_columns(stacked):
    rows = stacked.shape[0] // 2
    return jnp.where(first_half(), stacked[:rows], stacked[rows:])


def lanes(p):
    return pl.ds(p * LANES, LANES)


def forward_kernel(
    nz, x_ref, e_ref, ends, gain_one1, shift_one1, qkv_bias1, proj_bias1, gain_two1, shift_two1, up_bias1, down_bias1,
    qkv_hbm, proj_hbm, up_hbm, down_hbm,
    layer_out, n1_all, q_out, attn_out, da_out, do_out, n2_out, g_out, du_out, dx_out, stats_out, small_out,
    x_all, qkv_w, proj_w, up_w, down_w, kv, scores, mask, top, total, acc, two_q, res_acc, dh_acc,
    gain_one, shift_one, qkv_bias, proj_bias, gain_two, shift_two, up_bias, down_bias,
    up_send, up_recv, down_send, down_recv, side_send, side_recv, w_sem,
):
    rows, width = x_ref.shape
    pair = 2 * rows
    seq = lax.axis_index("seq")
    batch = lax.axis_index("batch")
    z = seq // 2
    x = seq % 2
    loads = [
        pltpu.make_async_copy(hbm, vmem, w_sem.at[k])
        for k, (hbm, vmem) in enumerate(
            [(qkv_hbm, qkv_w), (proj_hbm, proj_w), (up_hbm, up_w), (down_hbm, down_w)]
        )
    ]
    loads[0].start()
    barrier = pltpu.get_barrier_semaphore()
    has_up = z + 1 < nz
    has_down = z > 0
    above = (seq + 2, batch)
    below = (seq - 2, batch)
    beside = (seq + 1 - 2 * x, batch)

    @pl.when(has_up)
    def _():
        pl.semaphore_signal(barrier, inc=1, device_id=above, device_id_type=MESH_ID)

    @pl.when(has_down)
    def _():
        pl.semaphore_signal(barrier, inc=1, device_id=below, device_id_type=MESH_ID)

    pl.semaphore_signal(barrier, inc=1, device_id=beside, device_id_type=MESH_ID)
    pl.semaphore_wait(barrier, 1 + has_up.astype(jnp.int32) + has_down.astype(jnp.int32))
    for load in loads[1:]:
        load.start()

    half = rows // 2

    def block(level, side, h):
        return x_all.at[rows_at((2 * level + side) * rows + h * half, half)]

    def copies(level, side, to, send_sem, recv_sem, own=False):
        found = []
        for h in range(2):
            source = x_ref.at[h * half : (h + 1) * half] if own else block(level, side, h)
            found.append(
                pltpu.make_async_remote_copy(
                    source, block(level, side, h), send_sem.at[level, h], recv_sem.at[level, h],
                    device_id=to, device_id_type=MESH_ID,
                )
            )
        return found

    def up_copies(level, own=False):
        return copies(level, x, above, up_send, up_recv, own)

    def down_copies(level, own=False):
        return copies(level, x, below, down_send, down_recv, own)

    def side_copies(level, own=False):
        return copies(level, x, beside, side_send, side_recv, own)

    def wait_side(level):
        for copy in copies(level, 1 - x, beside, side_send, side_recv):
            copy.wait_recv()

    own_up, own_side, own_down = up_copies(z, True), side_copies(z, True), down_copies(z, True)
    for h in range(2):

        @pl.when(has_up)
        def _(h=h):
            own_up[h].start()

        own_side[h].start()

        @pl.when(has_down)
        def _(h=h):
            own_down[h].start()

    vectors = [gain_one, shift_one, qkv_bias, proj_bias, gain_two, shift_two, up_bias, down_bias]
    flats = [gain_one1, shift_one1, qkv_bias1, proj_bias1, gain_two1, shift_two1, up_bias1, down_bias1]
    for vector, flat in zip(vectors, flats):
        vector[...] = as_row(flat)
    x_all[rows_at(seq * rows, rows)] = x_ref[...]
    x32 = x_ref[...].astype(jnp.float32)
    unit_one, _ = norm_parts(x32)
    mine = (unit_one * gain_one[...] + shift_one[...]).astype(jnp.bfloat16)
    top[...] = jnp.full(top.shape, masked_low, jnp.float32)
    total[...] = jnp.zeros(total.shape, jnp.float32)
    acc[...] = jnp.zeros(acc.shape, jnp.float32)
    loads[0].wait()
    q = (dot(mine, qkv_w[:, :width]) + qkv_bias[:, :width]).astype(jnp.bfloat16)
    q = q * jnp.asarray(1.0 / math.sqrt(HD), jnp.bfloat16)
    q_out[...] = q
    for p in range(HEADS // 2):
        two_q[p] = both_heads(q[:, p * LANES : (p + 1) * LANES])

    def pass_on(d):
        @pl.when(z >= d)
        def _():
            level = z - d
            ups, sides = up_copies(level), side_copies(level)
            for h in range(2):
                ups[h].wait_recv()

                @pl.when(has_up)
                def _(h=h):
                    ups[h].start()

                sides[h].start()

        @pl.when(z + d < nz)
        def _():
            level = z + d
            downs, sides = down_copies(level), side_copies(level)
            for h in range(2):
                downs[h].wait_recv()

                @pl.when(has_down)
                def _(h=h):
                    downs[h].start()

                sides[h].start()

    def normalize(level):
        here = rows_at(level * pair, pair)
        unit, _ = norm_parts(x_all[here].astype(jnp.float32))
        n1 = (unit * gain_one[...] + shift_one[...]).astype(jnp.bfloat16)
        n1_all[here] = n1
        return n1

    def attend(level):
        wait_side(level)
        n1 = normalize(level)
        kv[...] = (dot(n1, qkv_w[:, width:]) + qkv_bias[:, width:]).astype(jnp.bfloat16)
        one = mask_of(ends, places_down(seq * rows, rows), places_along(level * pair, pair))
        mask[:rows] = one
        mask[rows:] = one
        keeps = []
        for p in range(HEADS // 2):
            s = dot(two_q[p], kv[:, p * LANES : (p + 1) * LANES], NT)
            scores[p] = s
            low = jnp.abs(s) + mask[...]
            before = top[p]
            most = jnp.max(jnp.maximum(low[:, :LANES], low[:, LANES:]), axis=1, keepdims=True)
            newer = jnp.maximum(before, most)
            keeps.append(jnp.exp(before - newer))
            top[p] = newer
        for p in range(HEADS // 2):
            s = scores[p]
            low = mask[...] - jnp.concatenate([top[p], top[p]], axis=1)
            plus = jnp.exp(low + s)
            minus = jnp.exp(low - s)
            both = plus + minus
            total[p] = total[p] * keeps[p] + (both[:, :LANES] + both[:, LANES:])
            v_pair = kv[:, width + p * LANES : width + (p + 1) * LANES]
            out = own_columns(dot((plus - minus).astype(jnp.bfloat16), v_pair))
            here = slice(p * LANES, (p + 1) * LANES)
            acc[:, here] = acc[:, here] * own_columns(keeps[p]) + out

    def level_step(d, carry):
        @pl.when(d + 1 < nz)
        def _():
            pass_on(d + 1)

        @pl.when(z >= d)
        def _():
            attend(z - d)

        @pl.when((d > 0) & (z + d < nz))
        def _():
            wait_side(z + d)
            normalize(z + d)

        return carry

    lax.fori_loop(0, nz, level_step, 0)

    column = lax.broadcasted_iota(jnp.int32, (1, LANES), 1)
    log_total = jnp.zeros((rows, LANES), jnp.float32)
    for p in range(HEADS // 2):
        here = slice(p * LANES, (p + 1) * LANES)
        row_total = jnp.broadcast_to(jnp.sum(total[p], axis=1, keepdims=True), (pair, LANES))
        acc[:, here] = acc[:, here] / own_columns(row_total)
        lse = top[p] + jnp.log(row_total)
        log_total = jnp.where(column == 2 * p, lse[:rows], log_total)
        log_total = jnp.where(column == 2 * p + 1, lse[rows:], log_total)
    attn = acc[...].astype(jnp.bfloat16)
    attn_out[...] = attn
    loads[1].wait()
    resid = x32 + dot(attn, proj_w[...]) + proj_bias[...]
    unit, inverse = norm_parts(resid)
    n2 = (unit * gain_two[...] + shift_two[...]).astype(jnp.bfloat16)
    n2_out[...] = n2
    res_acc[...] = resid + down_bias[...]
    dh_acc[...] = jnp.zeros(dh_acc.shape, jnp.float32)
    loads[2].wait()
    loads[3].wait()
    slope = math.sqrt(2.0 / math.pi)

    def ff_step(t, carry):
        here = pl.ds(pl.multiple_of(t * FF_TILE, FF_TILE), FF_TILE)
        u = dot(n2_out[...], up_w[:, here]) + up_bias[:, here]
        square = u * u
        bend = jnp.tanh(slope * (u + 0.044715 * (square * u)))
        half = 0.5 * (1.0 + bend)
        g = (u * half).astype(jnp.bfloat16)
        slant = half + (0.5 * u) * (1.0 - bend * bend) * (slope * (1.0 + 3.0 * 0.044715 * square))
        g_out[:, here] = g
        res_acc[...] += dot(g, down_w[here])
        du32 = dot(e_ref[...], down_w[here], NT) * slant
        du = du32.astype(jnp.bfloat16)
        du_out[:, here] = du
        small_out[pl.ds(4 + t, 1)] = jnp.sum(du.astype(jnp.float32), axis=0, keepdims=True)
        dh_acc[...] += dot(du, up_w[:, here], NT)
        return carry

    lax.fori_loop(0, up_w.shape[1] // FF_TILE, ff_step, 0)
    layer_out[...] = res_acc[...].astype(jnp.bfloat16)
    dh = dh_acc[...]
    grad_rows = e_ref[...].astype(jnp.float32)
    dx = grad_rows + norm_back(dh, unit, inverse, gain_two[...])
    dx_out[...] = dx
    da = dx.astype(jnp.bfloat16)
    da_out[...] = da
    do = dot(da, proj_w[...], NT).astype(jnp.bfloat16)
    do_out[...] = do
    product = do.astype(jnp.float32) * acc[...]
    delta = jnp.zeros((rows, LANES), jnp.float32)
    left = first_half()
    for p in range(HEADS // 2):
        here = product[:, p * LANES : (p + 1) * LANES]
        one = jnp.sum(jnp.where(left, here, 0.0), axis=1, keepdims=True)
        two = jnp.sum(jnp.where(left, 0.0, here), axis=1, keepdims=True)
        delta = jnp.where(column == 2 * p, one, delta)
        delta = jnp.where(column == 2 * p + 1, two, delta)
    stats_out[0] = log_total
    stats_out[1] = delta
    small_out[0:1] = jnp.sum(dh * unit, axis=0, keepdims=True)
    small_out[1:2] = jnp.sum(dh, axis=0, keepdims=True)
    small_out[2:3] = jnp.sum(grad_rows, axis=0, keepdims=True)
    small_out[3:4] = jnp.sum(da.astype(jnp.float32), axis=0, keepdims=True)

    def left_all(found):
        for copy in found:
            copy.wait_send()

    left_all(side_copies(z, True))

    @pl.when(has_up)
    def _():
        left_all(up_copies(z, True))

    @pl.when(has_down)
    def _():
        left_all(down_copies(z, True))

    def sent(d, carry):
        @pl.when(z >= d)
        def _():
            left_all(side_copies(z - d))

            @pl.when(has_up)
            def _():
                left_all(up_copies(z - d))

        @pl.when(z + d < nz)
        def _():
            left_all(side_copies(z + d))

            @pl.when(has_down)
            def _():
                left_all(down_copies(z + d))

        return carry

    lax.fori_loop(1, nz, sent, 0)


def run_forward(x, e, lengths, gain_one, shift_one, qkv_weight, qkv_bias, proj_weight, proj_bias, gain_two, shift_two, up_weight, up_bias, down_weight, down_bias, peers):
    rows, width = x.shape
    hidden = up_weight.shape[1]
    nz = peers // 2
    bf, f32 = jnp.bfloat16, jnp.float32
    vmem = pl.BlockSpec(memory_space=pltpu.VMEM)
    smem = pl.BlockSpec(memory_space=pltpu.SMEM)
    hbm = pl.BlockSpec(memory_space=pl.ANY)
    dma = pltpu.SemaphoreType.DMA
    outs = [
        ((rows, width), bf), ((peers * rows, width), bf), ((rows, width), bf), ((rows, width), bf), ((rows, width), bf),
        ((rows, width), bf), ((rows, width), bf), ((rows, hidden), bf), ((rows, hidden), bf), ((rows, width), f32),
        ((2, rows, LANES), f32), ((4 + hidden // width, width), f32),
    ]
    vectors = [gain_one, shift_one, qkv_bias, proj_bias, gain_two, shift_two, up_bias, down_bias]
    return pl.pallas_call(
        functools.partial(forward_kernel, nz),
        out_shape=[(pltpu.VMEM if fits(peers, rows) and k in KEPT else jax.ShapeDtypeStruct)(*o) for k, o in enumerate(outs)],
        in_specs=[vmem, vmem, smem] + [vmem] * 8 + [hbm] * 4,
        out_specs=[vmem] * len(outs),
        scratch_shapes=[
            pltpu.VMEM((peers * rows, width), bf),
            pltpu.VMEM(qkv_weight.shape, bf),
            pltpu.VMEM(proj_weight.shape, bf),
            pltpu.VMEM(up_weight.shape, bf),
            pltpu.VMEM(down_weight.shape, bf),
            pltpu.VMEM((2 * rows, 2 * width), bf),
            pltpu.VMEM((HEADS // 2, 2 * rows, 2 * rows), f32),
            pltpu.VMEM((2 * rows, 2 * rows), f32),
            pltpu.VMEM((HEADS // 2, 2 * rows, LANES), f32),
            pltpu.VMEM((HEADS // 2, 2 * rows, LANES), f32),
            pltpu.VMEM((rows, width), f32),
            pltpu.VMEM((HEADS // 2, 2 * rows, LANES), bf),
            pltpu.VMEM((rows, width), f32),
            pltpu.VMEM((rows, width), f32),
            *[pltpu.VMEM((1, v.shape[0]), f32) for v in vectors],
            *[dma((nz, 2))] * 6, dma((4,)),
        ],
        compiler_params=pltpu.CompilerParams(collective_id=0, has_side_effects=True, vmem_limit_bytes=60 * 2**20),
        cost_estimate=pl.CostEstimate(flops=10**9, bytes_accessed=2 * 10**7, transcendentals=10**6),
    )(x, e, lengths, *vectors, qkv_weight, proj_weight, up_weight, down_weight)


def backward_kernel(
    nz, items, orders, schedule,
    x_ref, e_ref, ends, gain_flat, bias_flat, n1_all, q_ref, attn_ref, da_ref, do_ref, n2_ref, g_ref, du_ref, dx_ref,
    stats_ref, first_small, qkv_hbm,
    input_grad, qkv_out, proj_out, up_out, down_out, small_out,
    qkv_w, buf, inbox, total, do_all, rows_all, g_cat, e_cat, n2_cat, du_cat, attn_cat, da_cat, n1_cat, dqkv_cat,
    two_q, two_do, two_k, two_v, lse_cols, delta_cols, kv, n1_held, mask, dq, dk, dv, small_in, gain_one, qkv_bias,
    down_send, down_recv, side_send, side_recv, ssem, rsem, lsem,
):
    rows, width = x_ref.shape
    pair = 2 * rows
    place = Place()
    seq, batch = place.seq, place.batch
    z = seq // 2
    x = seq % 2
    core = place.bit(CORE)
    sems = Sems(ssem, rsem)
    local = Sems(lsem, lsem)
    load = pltpu.make_async_copy(qkv_hbm, qkv_w, local.take()[0])
    load.start()
    small_axes = [CORE, ACROSS] + seq_axes(2 * nz)
    has_up = z + 1 < nz
    has_down = z > 0
    above = (seq + 2, batch)
    below = (seq - 2, batch)
    beside = (seq + 1 - 2 * x, batch)
    barrier = pltpu.get_barrier_semaphore()
    for axis in small_axes:
        pl.semaphore_signal(barrier, inc=1, device_id=place.partner(axis), device_id_type=MESH_ID)

    @pl.when(has_up)
    def _():
        pl.semaphore_signal(barrier, inc=1, device_id=above, device_id_type=MESH_ID)

    @pl.when(has_down)
    def _():
        pl.semaphore_signal(barrier, inc=1, device_id=below, device_id_type=MESH_ID)

    gain_one[...] = as_row(gain_flat)
    qkv_bias[...] = as_row(bias_flat)
    for k in range(2):
        rows_all[seq, k * TILE : (k + 1) * TILE] = stats_ref[k].T[:TILE]
    pl.semaphore_wait(barrier, len(small_axes) + has_up.astype(jnp.int32) + has_down.astype(jnp.int32))

    def cols(half, size):
        return pl.ds(pl.multiple_of(half * size, LANES), size)

    def to_core(source, into):
        return pltpu.make_async_remote_copy(
            source, into.at[rows:], *sems.take(), device_id=place.partner(CORE), device_id_type=MESH_ID
        )

    def keep_own(source, into):
        return pltpu.make_async_copy(source, into.at[:rows], local.take()[0])

    def exchange(ref, into, halved):
        size = into.shape[1]
        give = ref.at[:, cols(1 - core, size)] if halved else ref
        keep = ref.at[:, cols(core, size)] if halved else ref
        copies = [to_core(give, into), keep_own(keep, into)]
        for copy in copies:
            copy.start()
        return copies

    def done(copies):
        for copy in copies:
            copy.wait()

    down_parts = exchange(g_ref, g_cat, True) + exchange(e_ref, e_cat, False)
    up_parts = exchange(n2_ref, n2_cat, False) + exchange(du_ref, du_cat, True)

    def do_block(level, side):
        return do_all.at[rows_at((2 * level + side) * rows, rows)]

    def do_copies(level, side, to, send_sem, recv_sem, own=False):
        source = do_ref if own else do_block(level, side)
        stat = rows_all.at[2 * level + side]
        return [
            pltpu.make_async_remote_copy(
                source, do_block(level, side), send_sem.at[level, 0], recv_sem.at[level, 0], device_id=to, device_id_type=MESH_ID
            ),
            pltpu.make_async_remote_copy(
                stat, stat, send_sem.at[level, 1], recv_sem.at[level, 1], device_id=to, device_id_type=MESH_ID
            ),
        ]

    def down_copies(level, own=False):
        return do_copies(level, x, below, down_send, down_recv, own)

    def side_copies(level, own=False):
        return do_copies(level, x, beside, side_send, side_recv, own)

    def begin(copies):
        for copy in copies:
            copy.start()

    @pl.when(has_down)
    def _():
        begin(down_copies(z, True))

    begin(side_copies(z, True))
    do_all[rows_at(seq * rows, rows)] = do_ref[...]

    spread = [1]

    def spread_until(last):
        while spread[0] <= min(last, nz - 1):
            d = spread[0]
            spread[0] += 1

            @pl.when(z + d < nz)
            def _():
                level = z + d
                for copy in down_copies(level):
                    copy.wait_recv()

                @pl.when(has_down)
                def _():
                    begin(down_copies(level))

                begin(side_copies(level))

    def spread_end():
        def sent(copies):
            for copy in copies:
                copy.wait_send()

        sent(side_copies(z, True))

        @pl.when(has_down)
        def _():
            sent(down_copies(z, True))

        def each(level, carry):
            sent(side_copies(level))

            @pl.when(has_down)
            def _():
                sent(down_copies(level))

            return carry

        lax.fori_loop(z + 1, nz, each, 0)

    slots = []
    at = used = 0
    for size, kind, _ in items:
        slots.append((at, size, orders[kind], used))
        at += size
        used += sum(part for part, _ in parts_of(size, len(orders[kind])))
    places = [(name, r) for _, _, (name, r) in items]

    def destination(name, r, size):
        half = width // 2
        if name == "down":
            return down_out.at[rows_at(core * down_out.shape[0] // 2 + r, size)]
        if name[:2] == "up":
            return up_out.at[r : r + size, pl.ds(pl.multiple_of((core * (up_out.shape[1] // width // 2) + int(name[2:])) * width, width), width)]
        if name == "proj":
            return proj_out.at[rows_at(core * half + r, size)]
        return qkv_out.at[rows_at(core * half + r, size), int(name[3:]) * width : (int(name[3:]) + 1) * width]

    ready = set()

    def item_task(k):
        at, size, order, used = slots[k]
        name, r = places[k]
        if name[:2] not in ready:
            ready.add(name[:2])
            done(parts.get(name[:2], []))
        left, right = operands(name)
        buf[at : at + size] = dot(left[:, r : r + size], right, TN).astype(jnp.bfloat16)
        yield from sum_item(place, sems, buf, at, size, order, inbox, used, total)
        there = destination(name, r, size)
        here = total.at[rows_at(at, size)]
        keep = pltpu.make_async_copy(here, there, local.take()[0])
        give = pltpu.make_async_remote_copy(here, there, *sems.take(), device_id=place.partner(CORE), device_id_type=MESH_ID)
        keep.start()
        give.start()
        leaving.extend([keep, give])

    def small_task():
        for k, axis in enumerate(small_axes):
            copy = pltpu.make_async_remote_copy(
                small_out, small_in.at[k], *sems.take(), device_id=place.partner(axis), device_id_type=MESH_ID
            )
            copy.start()
            yield
            copy.wait()
            small_out[...] += small_in[k]

    leaving = []

    def operands(name):
        if name == "down":
            return g_cat, e_cat[...]
        if name == "proj":
            return attn_cat, da_cat[...]
        j = int(name[-1])
        block = slice(j * width, (j + 1) * width)
        return (n2_cat, du_cat[:, block]) if name[:2] == "up" else (n1_cat, dqkv_cat[:, block])

    small_out[:8] = first_small[...]
    own_n1 = rows_at(seq * rows, rows)
    parts = {
        "do": down_parts,
        "up": up_parts,
        "pr": exchange(attn_ref, attn_cat, True) + exchange(da_ref, da_cat, False),
        "qk": exchange(n1_all.at[own_n1], n1_cat, True),
    }

    load.wait()
    scale = jnp.asarray(1.0 / math.sqrt(HD), jnp.bfloat16)

    chunk_sem = local.take()[0]

    def n1_chunk(level):
        copy = pltpu.make_async_copy(n1_all.at[rows_at(level * pair, pair)], n1_held, chunk_sem)
        copy.start()
        copy.wait()
        return n1_held[...]

    def prepare():
        n1_chunk(z)
        mine = n1_held[rows_at(x * rows, rows)]
        own_kv = (dot(mine, qkv_w[:, width:]) + qkv_bias[:, width:]).astype(jnp.bfloat16)
        for p in range(HEADS // 2):
            here = slice(p * LANES, (p + 1) * LANES)
            two_q[p] = both_heads(q_ref[:, here])
            two_do[p] = both_heads(do_ref[:, here])
            two_k[p] = both_heads(own_kv[:, here])
            two_v[p] = both_heads(own_kv[:, width + p * LANES : width + (p + 1) * LANES])
            for k, into in enumerate((lse_cols, delta_cols)):
                for h in range(2):
                    column = stats_ref[k, :, 2 * p + h : 2 * p + h + 1]
                    into[p, h * rows : (h + 1) * rows] = jnp.broadcast_to(column, (rows, LANES))
        dq[...] = jnp.zeros(dq.shape, jnp.float32)
        dk[...] = jnp.zeros(dk.shape, jnp.float32)
        dv[...] = jnp.zeros(dv.shape, jnp.float32)

    def columns_of(p):
        return pl.ds(pl.multiple_of(p * LANES, LANES), LANES)

    def query_step(level):
        n1 = n1_chunk(level)
        kv[...] = (dot(n1, qkv_w[:, width:]) + qkv_bias[:, width:]).astype(jnp.bfloat16)
        one = mask_of(ends, places_down(seq * rows, rows), places_along(level * pair, pair))
        mask[:rows] = one
        mask[rows:] = one

        def each(p, carry):
            k_pair = kv[:, columns_of(p)]
            v_pair = kv[:, columns_of(p + HEADS // 2)]
            s = dot(two_q[p], k_pair, NT)
            along = dot(two_do[p], v_pair, NT)
            low = mask[...] - lse_cols[p][:, :1]
            plus = jnp.exp(low + s)
            minus = jnp.exp(low - s)
            ds = ((plus + minus) * along - (plus - minus) * delta_cols[p][:, :1]).astype(jnp.bfloat16)
            dq[:, columns_of(p)] += own_columns(dot(ds, k_pair))
            return carry

        lax.fori_loop(0, HEADS // 2, each, 0, unroll=UNROLL)

    def key_step(level):
        side = 1 - x
        for copy in do_copies(level, side, beside, side_send, side_recv):
            copy.wait_recv()
        here = rows_at(level * pair, pair)
        n1 = n1_chunk(level)
        kv[:, :width] = (dot(n1, qkv_w[:, :width]) + qkv_bias[:, :width]).astype(jnp.bfloat16) * scale
        one = mask_of(ends, places_along(level * pair, pair), places_down(seq * rows, rows))
        mask[:rows] = one
        mask[rows:] = one

        def stat(row):
            both = [rows_all[2 * level + k, pl.ds(row, 1)] for k in range(2)]
            return jnp.concatenate(both, axis=1)

        def stat_rows(k, p):
            both = [jnp.broadcast_to(stat(k * TILE + 2 * p + h), (rows, pair)) for h in range(2)]
            return jnp.concatenate(both, axis=0)

        def each(p, carry):
            q_pair = kv[:, columns_of(p)]
            do_pair = do_all[here, columns_of(p)]
            s = dot(two_k[p], q_pair, NT)
            along = dot(two_v[p], do_pair, NT)
            low = mask[...] - stat_rows(0, p)
            plus = jnp.exp(low + s)
            minus = jnp.exp(low - s)
            signed = plus - minus
            ds = ((plus + minus) * along - signed * stat_rows(1, p)).astype(jnp.bfloat16)
            dk[:, columns_of(p)] += own_columns(dot(ds, q_pair))
            dv[:, columns_of(p)] += own_columns(dot(signed.astype(jnp.bfloat16), do_pair))
            return carry

        lax.fori_loop(0, HEADS // 2, each, 0, unroll=UNROLL)

    def one_step(t):
        @pl.when(t <= z)
        def _():
            query_step(z - t)

        @pl.when(t > z)
        def _():
            key_step(t - 1)

    def steps_piece(first, last):
        def piece():
            spread_until(last)
            if last - first == 1:
                one_step(first)
            else:

                def body(t, carry):
                    one_step(t)
                    return carry

                lax.fori_loop(first, last, body, 0)

        return piece

    def finish():
        dqkv = jnp.concatenate(
            [
                (dq[...] * (1.0 / math.sqrt(HD))).astype(jnp.bfloat16),
                dk[...].astype(jnp.bfloat16),
                dv[...].astype(jnp.bfloat16),
            ],
            axis=1,
        )
        dqkv_cat[:rows] = dqkv
        send = to_core(dqkv_cat.at[:rows], dqkv_cat)
        send.start()
        dh = dot(dqkv, qkv_w[...], NT)
        unit, inverse = norm_parts(x_ref[...].astype(jnp.float32))
        input_grad[...] = (dx_ref[...] + norm_back(dh, unit, inverse, gain_one[...])).astype(jnp.bfloat16)
        sums = jnp.sum(dqkv.astype(jnp.float32), axis=0, keepdims=True)
        for k in range(3):
            small_out[8 + k : 9 + k] = sums[:, k * width : (k + 1) * width]
        small_out[11:12] = jnp.sum(dh * unit, axis=0, keepdims=True)
        small_out[12:13] = jnp.sum(dh, axis=0, keepdims=True)
        small_out[13:16] = jnp.zeros((3, width), jnp.float32)
        parts["qk"].append(send)

    groups = min(nz + 1, GROUPS)
    cuts = [(nz + 1) * k // groups for k in range(groups + 1)]
    pieces = [prepare] + [steps_piece(a, b) for a, b in zip(cuts, cuts[1:])] + [finish]
    tasks = [item_task(k) for k in range(len(items))] + [small_task()]
    for token in schedule:
        if token < 0:
            pieces[-1 - token]()
        else:
            next(tasks[token], None)
    for copy in leaving:
        copy.wait()
    spread_end()


def in_turns(items, counts, n_pieces):
    early = [k for k, (_, _, (name, _)) in enumerate(items) if name[:3] != "qkv"]
    late = [k for k in range(len(counts)) if k not in early]
    tokens, piece = [], 0
    for waiting in (early, late):
        live = []
        while live or waiting:
            live, waiting = live + waiting[:3], waiting[3:]
            for k in live:
                tokens.append(k)
                if len(tokens) % PACE == 0 and piece < n_pieces:
                    piece += 1
                    tokens.append(-piece)
            live = [k for k in live if tokens.count(k) < counts[k]]
        while piece < n_pieces:
            piece += 1
            tokens.append(-piece)
    return tokens


def fits(peers, rows):
    return peers * rows <= 2048


def plan_items(width, hidden):
    half = width // 2

    def cut(name, size):
        return [(min(ITEM, size - r), (name, r)) for r in range(0, size, ITEM)]

    found = cut("down", hidden // 2)
    for j in range(hidden // 2 // width):
        found += cut(f"up{j}", width)
    found += cut("proj", half)
    for j in range(3):
        found += cut(f"qkv{j}", half)
    return [(size, int(KINDS[k % len(KINDS)]), where) for k, (size, where) in enumerate(found)]


def run_backward(x, e, lengths, gain_one, qkv_weight, qkv_bias, kept, peers):
    n1_all, q, attn, da, do, n2, g, du, dx, stats, small = kept
    rows, width = x.shape
    hidden = g.shape[1]
    nz = peers // 2
    bf, f32 = jnp.bfloat16, jnp.float32
    orders = axis_orders(peers)
    stages = 2 + len(seq_axes(peers))
    items = plan_items(width, hidden)
    counts = [parts_of(size, len(orders[kind])) for size, kind, _ in items]
    used = sum(part for count in counts for part, _ in count)
    height = sum(size for size, _, _ in items)
    turns = [1 + len(count) + sum(halve for _, halve in count) for count in counts] + [1 + stages]
    n_pieces = 2 + min(nz + 1, GROUPS)
    schedule = SCHEDULE
    if sorted(schedule) != sorted([k for k, n in enumerate(turns) for _ in range(n)] + [-1 - k for k in range(n_pieces)]):
        schedule = in_turns(items, turns, n_pieces)
    copies = sum(1 + len(count) + sum(halve for _, halve in count) for count in counts) + stages + 8
    vmem = pl.BlockSpec(memory_space=pltpu.VMEM)
    smem = pl.BlockSpec(memory_space=pltpu.SMEM)
    hbm = pl.BlockSpec(memory_space=pl.ANY)
    dma = pltpu.SemaphoreType.DMA
    out = jax.ShapeDtypeStruct
    small_mesh = fits(peers, rows)
    grad = pltpu.VMEM if small_mesh else out
    stack = (HEADS // 2, 2 * rows, LANES)
    return pl.pallas_call(
        functools.partial(backward_kernel, nz, items, orders, schedule),
        out_shape=[
            grad((rows, width), bf), grad((width, 3 * width), bf), grad((width, width), bf), grad((width, hidden), bf),
            grad((hidden, width), bf), out((16, width), f32),
        ],
        in_specs=[vmem, hbm, smem, vmem, vmem]
        + [vmem if k in (2, 5, 9, 10, 11) or (small_mesh and k in KEPT) else hbm for k in range(1, 12)]
        + [hbm],
        out_specs=[vmem] + [vmem if small_mesh else hbm] * 4 + [vmem],
        scratch_shapes=[
            pltpu.VMEM(qkv_weight.shape, bf),
            pltpu.VMEM((height, width), bf),
            pltpu.VMEM((used, width), bf),
            pltpu.VMEM((height, width), bf),
            pltpu.VMEM((peers * rows, width), bf),
            pltpu.VMEM((peers, 2 * TILE, LANES), f32),
            pltpu.VMEM((2 * rows, hidden // 2), bf),
            pltpu.VMEM((2 * rows, width), bf),
            pltpu.VMEM((2 * rows, width), bf),
            pltpu.VMEM((2 * rows, hidden // 2), bf),
            pltpu.VMEM((2 * rows, width // 2), bf),
            pltpu.VMEM((2 * rows, width), bf),
            pltpu.VMEM((2 * rows, width // 2), bf),
            pltpu.VMEM((2 * rows, 3 * width), bf),
            pltpu.VMEM(stack, bf), pltpu.VMEM(stack, bf), pltpu.VMEM(stack, bf), pltpu.VMEM(stack, bf),
            pltpu.VMEM(stack, f32), pltpu.VMEM(stack, f32),
            pltpu.VMEM((2 * rows, 2 * width), bf),
            pltpu.VMEM((2 * rows, width), bf),
            pltpu.VMEM((2 * rows, 2 * rows), f32),
            pltpu.VMEM((rows, width), f32), pltpu.VMEM((rows, width), f32), pltpu.VMEM((rows, width), f32),
            pltpu.VMEM((stages, 16, width), f32),
            pltpu.VMEM((1, width), f32), pltpu.VMEM((1, 3 * width), f32),
            dma((nz, 2)), dma((nz, 2)), dma((nz, 2)), dma((nz, 2)),
            dma((copies,)), dma((copies,)), dma((len(items) + 10,)),
        ],
        compiler_params=pltpu.CompilerParams(collective_id=1, has_side_effects=True, vmem_limit_bytes=(K2_LIMIT if small_mesh else 62) * 2**20),
    )(x, e, lengths, gain_one, qkv_bias, n1_all, q, attn, da, do, n2, g, du, dx, stats, small, qkv_weight)


def widen_kernel(grads, small, passed, outs, rests, passed_outs, slots, sems, pass_sems):
    moved = [pltpu.make_async_copy(a, b, pass_sems.at[k]) for k, (a, b) in enumerate(zip(passed, passed_outs))]
    for copy in moved:
        copy.start()
    for k, (grad, out) in enumerate(zip(grads, outs)):
        slot = slots[k]
        rows = slot.shape[1]
        flying = []
        for n in range(grad.shape[0] // rows):
            at = n % slot.shape[0]
            if len(flying) >= slot.shape[0]:
                flying[n - slot.shape[0]].wait()

            def body(i, carry, n=n, at=at, grad=grad, slot=slot, rows=rows):
                here = pl.ds(pl.multiple_of(i * TILE, TILE), TILE)
                there = pl.ds(pl.multiple_of(n * rows + i * TILE, TILE), TILE)
                slot[at, here] = grad[there].astype(jnp.float32)
                return carry

            lax.fori_loop(0, rows // TILE, body, 0)
            copy = pltpu.make_async_copy(slot.at[at], out.at[n * rows : (n + 1) * rows], sems.at[k, n % slot.shape[0]])
            copy.start()
            flying.append(copy)
        moved += flying[-slot.shape[0] :]
    for (first, count), rest in zip(SMALL_ROWS, rests):
        for k in range(count):
            rest[k * small.shape[1] : (k + 1) * small.shape[1]] = small[first + k : first + k + 1].reshape(small.shape[1])
    for copy in moved:
        copy.wait()


def widen(grads, small, passed):
    width = small.shape[1]
    depth = 3
    sizes = [(g.shape, max(TILE, WIDEN // g.shape[1] // TILE * TILE)) for g in grads]
    vmem = pl.BlockSpec(memory_space=pltpu.VMEM)
    hbm = pl.BlockSpec(memory_space=pl.ANY)
    n = len(grads)
    m = len(SMALL_ROWS)
    q = len(passed)

    def kernel(*refs):
        found = []
        for count in (n, 1, q, n, m, q, n):
            found.append(refs[:count])
            refs = refs[count:]
        found[1] = found[1][0]
        widen_kernel(*found, *refs)

    return pl.pallas_call(
        kernel,
        out_shape=[jax.ShapeDtypeStruct(g.shape, jnp.float32) for g in grads]
        + [jax.ShapeDtypeStruct((count * width,), jnp.float32) for _, count in SMALL_ROWS]
        + [jax.ShapeDtypeStruct(p.shape, p.dtype) for p in passed],
        in_specs=[vmem] * (n + 1) + [vmem] * q,
        out_specs=[hbm] * n + [vmem] * m + [hbm] * q,
        scratch_shapes=[pltpu.VMEM((depth, rows, shape[1]), jnp.float32) for shape, rows in sizes]
        + [pltpu.SemaphoreType.DMA((n, depth)), pltpu.SemaphoreType.DMA((q,))],
        compiler_params=pltpu.CompilerParams(vmem_limit_bytes=34 * 2**20),
    )(*grads, small, *passed)


def per_device(
    inputs,
    cotangent,
    doc_lengths,
    gain_one,
    shift_one,
    qkv_weight,
    qkv_bias,
    proj_weight,
    proj_bias,
    gain_two,
    shift_two,
    up_weight,
    up_bias,
    down_weight,
    down_bias,
):
    peers = lax.axis_size("seq")
    width = inputs.shape[2]
    layer_out, *kept = run_forward(
        inputs[0], cotangent[0], doc_lengths, gain_one, shift_one, qkv_weight, qkv_bias, proj_weight, proj_bias, gain_two, shift_two,
        up_weight, up_bias, down_weight, down_bias, peers,
    )
    input_grad, qkv, proj, up, down, small = run_backward(
        inputs[0], cotangent[0], doc_lengths, gain_one, qkv_weight, qkv_bias, kept, peers
    )
    large = (qkv, proj, up, down)
    if fits(peers, inputs.shape[1]):
        qkv, proj, up, down, *rest, layer_out, input_grad = widen(large, small, (layer_out, input_grad))
    else:
        qkv, proj, up, down = (g.astype(jnp.float32) for g in large)
        rest = [small[first : first + count].reshape(-1) for first, count in SMALL_ROWS]
    gain_1, shift_1, qkv_b, proj_b, gain_2, shift_2, up_b, down_b = rest
    return (
        layer_out[None], input_grad[None], gain_1, shift_1, qkv, qkv_b, proj, proj_b, gain_2, shift_2, up, up_b, down, down_b,
    )


def solution(mesh):
    in_specs = (
        P("batch", "seq", None),
        P("batch", "seq", None),
        P("batch", None),
        P(),
        P(),
        P(),
        P(),
        P(),
        P(),
        P(),
        P(),
        P(),
        P(),
        P(),
        P(),
    )
    out_specs = (
        P("batch", "seq", None),
        P("batch", "seq", None),
        P(),
        P(),
        P(),
        P(),
        P(),
        P(),
        P(),
        P(),
        P(),
        P(),
        P(),
        P(),
    )
    return jax.shard_map(
        per_device, mesh=mesh, in_specs=in_specs, out_specs=out_specs, check_vma=False
    )
```

```python
import functools
import math

import jax
import jax.numpy as jnp
from jax import lax
from jax.experimental import pallas as pl
from jax.experimental.pallas import tpu as pltpu
from jax.sharding import PartitionSpec as P

HEADS = 12
HD = 64


norm_eps = 1e-05
masked_low = -1e30


MESH_ID = pl.DeviceIdType.MESH
TILE = 16
LANES = 128
FF_TILE = 768
ITEM = 256
KINDS = "345411530314532305010"
GROUPS = 5
PACE = 8
UNROLL = 6
K2_LIMIT = 45
KEPT = (0,)
WIDEN = 128 * 2304
SMALL_ROWS = ((11, 1), (12, 1), (8, 3), (3, 1), (0, 1), (1, 1), (4, 4), (2, 1))
SCHEDULE = (
    9, 3, 5, 2, 10, -1, -2, 12, 2, 3, 6, -3, 12, 10, 0, 5, 13, 2, 9, -4, 11, 6, 4, 2, 8, -5, 7, 9, 3, 5, 6, -6, 4, 12,
    1, 11, 10, -7, 5, 17, 9, 11, 0, 3, 8, 17, 13, 18, 4, 12, 11, 8, 7, 19, 1, 0, 14, 8, 3, 6, 5, 9, 17, 1, 3, 8, 20,
    16, 15, 4, 18, 19, 13, 8, 1, 0, 11, 14, 7, 19, 9, 8, 6, 0, 3, 20, 10, 1, 9, 5, 17, 7, 18, 15, 2, 16, 1, 11, 5, 14,
    18, 13, 6, 17, 15, 4, 8, 16, 2, 10, 5, 1, 6, 19, 8, 16, 4, 18, 2, 11, 15, 17, 14, 4, 19, 12, 10, 9, 5, 17, 3, 18,
    14, 15, 7, 15, 5, 1, 13, 4, 19, 0, 12, 13, 7, 16, 9, 16, 11, 19, 1, 18, 14, 12, 4, 3, 10, 15, 0, 8, 14, 20, 7, 6,
    13, 16, 19, 15, 11, 4, 2, 0, 18, 9, 15, 7, 11, 8, 10, 6, 16, 18, 14, 13, 19, 15, 7, 20, 16, 1, 10, 10, 13, 9, 2,
    6, 0, 14, 12, 4, 2, 17, 3, 7, 12, 1, 19, 0, 14, 20, 17, 18, 12, 16, 7, 5, 17, 20, 13, 19, 11, 18, 13, 17, 10, 14,
    12, 16, 15, 3, 2, 6, 0,
)


class Place:
    def __init__(self):
        self.seq = lax.axis_index("seq")
        self.batch = lax.axis_index("batch")
        self.level = self.seq // 2
        self.levels = lax.axis_size("seq") // 2

    def bit(self, axis):
        name, k = axis
        return ((self.seq if name == "seq" else self.batch) // (1 << k)) % 2

    def partner(self, axis):
        name, k = axis
        step = (1 << k) * (1 - 2 * self.bit(axis))
        if name == "seq":
            return (self.seq + step, self.batch)
        return (self.seq, self.batch + step)


CORE = ("batch", 0)
ACROSS = ("batch", 1)
LEVELS = ("seq", None)


def seq_axes(peers):
    return [("seq", k) for k in range((peers - 1).bit_length())]


def axis_orders():
    x, y, z = ("seq", 0), ACROSS, LEVELS
    return [[x, y, z], [y, z, x], [z, x, y], [y, x, z], [x, z, y], [z, y, x]]


class Sems:
    def __init__(self, send, recv):
        self.send, self.recv, self.count = send, recv, 0

    def take(self):
        k = self.count
        self.count += 1
        return self.send.at[k], self.recv.at[k]


def rows_at(start, size):
    return pl.ds(pl.multiple_of(start, TILE), size)


def add_rows(into, one, at, other, other_at, rows):
    step = 32 if rows % 32 == 0 else TILE

    def body(i, carry):
        here = rows_at(at + i * step, step)
        there = rows_at(other_at + i * step, step)
        both = one[here].astype(jnp.float32) + other[there].astype(jnp.float32)
        into[here] = both.astype(into.dtype)
        return carry

    lax.fori_loop(0, rows // step, body, 0)


def sum_item(place, sems, buf, at, rows, order, inbox, used, total, leaving):
    z, nz = place.level, place.levels
    above, below = (place.seq + 2, place.batch), (place.seq - 2, place.batch)
    at_end = (z == 0) | (z == nz - 1)
    low, length, held, plan = at, rows, None, []

    def where(condition, act):
        if condition is None:
            act()
        else:
            pl.when(condition)(act)

    def remote(source, into, to):
        return pltpu.make_async_remote_copy(source, into, *sems.take(), device_id=to, device_id_type=MESH_ID)

    def part_of(ref, start, size):
        return ref.at[rows_at(start, size)]

    def chain(up, down, step_up, step_down):
        pl.when(z == 0)(up.start)
        pl.when(z == nz - 1)(down.start)
        yield
        for first, last in hop_groups(nz):
            for hop, copy, step in ((z, up, step_up), (nz - 1 - z, down, step_down)):
                here = (hop >= first) & (hop < last)

                @pl.when(here)
                def _(copy=copy, step=step):
                    copy.wait_recv()
                    step(False)

                @pl.when(here & (hop < nz - 1))
                def _(copy=copy):
                    copy.start()

                @pl.when(here & (hop == nz - 1))
                def _(step=step):
                    step(True)

            if last < nz:
                yield

        def sent():
            pl.when(z < nz - 1)(up.wait_send)
            pl.when(z > 0)(down.wait_send)

        leaving.append(sent)

    for k, axis in enumerate(order):
        last = k == len(order) - 1
        part = length // 2
        if axis == LEVELS:
            ups, downs = low + part, low

            def adder(start, slot, part=part, last=last):
                def step(end):
                    if not last:
                        if not end:
                            add_rows(buf, buf, start, inbox, slot, part)
                    elif end:
                        add_rows(total, buf, start, inbox, slot, part)

                return step

            def adder_last(start, slot, hop, part=part):
                def step(end):
                    if end:
                        add_rows(total, buf, start, inbox, slot, part)
                    else:
                        pl.when(hop < nz - 1)(lambda: add_rows(buf, buf, start, inbox, slot, part))

                return step

            make_up = adder_last(ups, used, z) if last else adder(ups, used)
            make_down = adder_last(downs, used + part, nz - 1 - z) if last else adder(downs, used + part)
            yield from chain(
                remote(part_of(buf, ups, part), part_of(inbox, used, part), above),
                remote(part_of(buf, downs, part), part_of(inbox, used + part, part), below),
                make_up,
                make_down,
            )
            used += 2 * part
            plan.append((axis, low, part, held))
            low = low + jnp.where(z == nz - 1, part, 0)
            held = at_end
        else:
            bit = place.bit(axis)
            keep, give = low + bit * part, low + (1 - bit) * part
            copy = remote(part_of(buf, give, part), part_of(inbox, used, part), place.partner(axis))
            where(held, copy.start)
            yield

            def take(copy=copy, keep=keep, used=used, part=part, last=last):
                copy.wait()
                add_rows(total if last else buf, buf, keep, inbox, used, part)

            where(held, take)
            used += part
            plan.append((axis, keep, part, held))
            low = keep
        length = part
    for axis, low, part, held in reversed(plan):
        if axis == LEVELS:
            ups, downs = part_of(total, low + part, part), part_of(total, low, part)
            nothing = lambda end: None
            yield from chain(remote(downs, downs, above), remote(ups, ups, below), nothing, nothing)
        else:
            here = part_of(total, low, part)
            copy = remote(here, here, place.partner(axis))
            where(held, copy.start)
            yield
            where(held, copy.wait)


def hop_groups(levels):
    groups = min(levels - 1, 3)
    cuts = [1 + (levels - 1) * k // groups for k in range(groups + 1)]
    return list(zip(cuts, cuts[1:]))


def inbox_rows(rows, order):
    used = 0
    for axis in order:
        rows //= 2
        used += 2 * rows if axis == LEVELS else rows
    return used


def dot(a, b, dims=((1,), (0,))):
    return lax.dot_general(a, b, (dims, ((), ())), preferred_element_type=jnp.float32)


NT = ((1,), (1,))
TN = ((0,), (0,))


def norm_parts(rows):
    center = rows - jnp.mean(rows, axis=-1, keepdims=True)
    spread = jnp.mean(center * center, axis=-1, keepdims=True)
    inverse = lax.rsqrt(spread + norm_eps)
    return center * inverse, inverse


def norm_back(grad, unit, inverse, gain):
    scaled = grad * gain
    along = jnp.mean(scaled * unit, axis=-1, keepdims=True)
    return inverse * (scaled - jnp.mean(scaled, axis=-1, keepdims=True) - unit * along)


def doc_ids(lengths, places):
    found = jnp.zeros(places.shape, jnp.int32)
    end = 0
    for k in range(lengths.shape[1]):
        end += lengths[0, k]
        found += (end <= places).astype(jnp.int32)
    return found


def as_row(ref):
    return ref[...].reshape(1, -1)


def places_down(first, rows):
    return first + lax.broadcasted_iota(jnp.int32, (rows, 1), 0)


def places_along(first, rows):
    return first + lax.broadcasted_iota(jnp.int32, (1, rows), 1)


def mask_of(ends, q_places, k_places):
    allowed = (doc_ids(ends, q_places) == doc_ids(ends, k_places)) & (k_places <= q_places)
    return jnp.where(allowed, 0.0, masked_low)


def first_half():
    return lax.broadcasted_iota(jnp.int32, (1, LANES), 1) < HD


def both_heads(pair):
    left = first_half()
    none = jnp.zeros_like(pair)
    return jnp.concatenate([jnp.where(left, pair, none), jnp.where(left, none, pair)], axis=0)


def own_columns(stacked):
    rows = stacked.shape[0] // 2
    return jnp.where(first_half(), stacked[:rows], stacked[rows:])


def lanes(p):
    return pl.ds(p * LANES, LANES)


def forward_kernel(
    nz, x_ref, e_ref, ends, gain_one1, shift_one1, qkv_bias1, proj_bias1, gain_two1, shift_two1, up_bias1, down_bias1,
    qkv_hbm, proj_hbm, up_hbm, down_hbm,
    layer_out, n1_all, q_out, attn_out, da_out, do_out, n2_out, g_out, du_out, dx_out, stats_out, small_out,
    x_all, qkv_w, proj_w, up_w, down_w, kv, scores, mask, top, total, acc, two_q, res_acc, dh_acc,
    gain_one, shift_one, qkv_bias, proj_bias, gain_two, shift_two, up_bias, down_bias,
    up_send, up_recv, down_send, down_recv, side_send, side_recv, w_sem,
):
    rows, width = x_ref.shape
    pair = 2 * rows
    seq = lax.axis_index("seq")
    batch = lax.axis_index("batch")
    z = seq // 2
    x = seq % 2
    loads = [
        pltpu.make_async_copy(hbm, vmem, w_sem.at[k])
        for k, (hbm, vmem) in enumerate(
            [(qkv_hbm, qkv_w), (proj_hbm, proj_w), (up_hbm, up_w), (down_hbm, down_w)]
        )
    ]
    loads[0].start()
    barrier = pltpu.get_barrier_semaphore()
    has_up = z + 1 < nz
    has_down = z > 0
    above = (seq + 2, batch)
    below = (seq - 2, batch)
    beside = (seq + 1 - 2 * x, batch)

    @pl.when(has_up)
    def _():
        pl.semaphore_signal(barrier, inc=1, device_id=above, device_id_type=MESH_ID)

    @pl.when(has_down)
    def _():
        pl.semaphore_signal(barrier, inc=1, device_id=below, device_id_type=MESH_ID)

    pl.semaphore_signal(barrier, inc=1, device_id=beside, device_id_type=MESH_ID)
    pl.semaphore_wait(barrier, 1 + has_up.astype(jnp.int32) + has_down.astype(jnp.int32))
    for load in loads[1:]:
        load.start()

    half = rows // 2

    def block(level, side, h):
        return x_all.at[rows_at((2 * level + side) * rows + h * half, half)]

    def copies(level, side, to, send_sem, recv_sem, own=False):
        found = []
        for h in range(2):
            source = x_ref.at[h * half : (h + 1) * half] if own else block(level, side, h)
            found.append(
                pltpu.make_async_remote_copy(
                    source, block(level, side, h), send_sem.at[level, h], recv_sem.at[level, h],
                    device_id=to, device_id_type=MESH_ID,
                )
            )
        return found

    def up_copies(level, own=False):
        return copies(level, x, above, up_send, up_recv, own)

    def down_copies(level, own=False):
        return copies(level, x, below, down_send, down_recv, own)

    def side_copies(level, own=False):
        return copies(level, x, beside, side_send, side_recv, own)

    def wait_side(level):
        for copy in copies(level, 1 - x, beside, side_send, side_recv):
            copy.wait_recv()

    own_up, own_side, own_down = up_copies(z, True), side_copies(z, True), down_copies(z, True)
    for h in range(2):

        @pl.when(has_up)
        def _(h=h):
            own_up[h].start()

        own_side[h].start()

        @pl.when(has_down)
        def _(h=h):
            own_down[h].start()

    vectors = [gain_one, shift_one, qkv_bias, proj_bias, gain_two, shift_two, up_bias, down_bias]
    flats = [gain_one1, shift_one1, qkv_bias1, proj_bias1, gain_two1, shift_two1, up_bias1, down_bias1]
    for vector, flat in zip(vectors, flats):
        vector[...] = as_row(flat)
    x_all[rows_at(seq * rows, rows)] = x_ref[...]
    x32 = x_ref[...].astype(jnp.float32)
    unit_one, _ = norm_parts(x32)
    mine = (unit_one * gain_one[...] + shift_one[...]).astype(jnp.bfloat16)
    top[...] = jnp.full(top.shape, masked_low, jnp.float32)
    total[...] = jnp.zeros(total.shape, jnp.float32)
    acc[...] = jnp.zeros(acc.shape, jnp.float32)
    loads[0].wait()
    q = (dot(mine, qkv_w[:, :width]) + qkv_bias[:, :width]).astype(jnp.bfloat16)
    q = q * jnp.asarray(1.0 / math.sqrt(HD), jnp.bfloat16)
    q_out[...] = q
    for p in range(HEADS // 2):
        two_q[p] = both_heads(q[:, p * LANES : (p + 1) * LANES])

    def pass_on(d):
        @pl.when(z >= d)
        def _():
            level = z - d
            ups, sides = up_copies(level), side_copies(level)
            for h in range(2):
                ups[h].wait_recv()

                @pl.when(has_up)
                def _(h=h):
                    ups[h].start()

                sides[h].start()

        @pl.when(z + d < nz)
        def _():
            level = z + d
            downs, sides = down_copies(level), side_copies(level)
            for h in range(2):
                downs[h].wait_recv()

                @pl.when(has_down)
                def _(h=h):
                    downs[h].start()

                sides[h].start()

    def normalize(level):
        here = rows_at(level * pair, pair)
        unit, _ = norm_parts(x_all[here].astype(jnp.float32))
        n1 = (unit * gain_one[...] + shift_one[...]).astype(jnp.bfloat16)
        n1_all[here] = n1
        return n1

    def attend(level):
        wait_side(level)
        n1 = normalize(level)
        kv[...] = (dot(n1, qkv_w[:, width:]) + qkv_bias[:, width:]).astype(jnp.bfloat16)
        one = mask_of(ends, places_down(seq * rows, rows), places_along(level * pair, pair))
        mask[:rows] = one
        mask[rows:] = one
        keeps = []
        for p in range(HEADS // 2):
            s = dot(two_q[p], kv[:, p * LANES : (p + 1) * LANES], NT)
            scores[p] = s
            low = jnp.abs(s) + mask[...]
            before = top[p]
            most = jnp.max(jnp.maximum(low[:, :LANES], low[:, LANES:]), axis=1, keepdims=True)
            newer = jnp.maximum(before, most)
            keeps.append(jnp.exp(before - newer))
            top[p] = newer
        for p in range(HEADS // 2):
            s = scores[p]
            low = mask[...] - jnp.concatenate([top[p], top[p]], axis=1)
            plus = jnp.exp(low + s)
            minus = jnp.exp(low - s)
            both = plus + minus
            total[p] = total[p] * keeps[p] + (both[:, :LANES] + both[:, LANES:])
            v_pair = kv[:, width + p * LANES : width + (p + 1) * LANES]
            out = own_columns(dot((plus - minus).astype(jnp.bfloat16), v_pair))
            here = slice(p * LANES, (p + 1) * LANES)
            acc[:, here] = acc[:, here] * own_columns(keeps[p]) + out

    def level_step(d, carry):
        @pl.when(d + 1 < nz)
        def _():
            pass_on(d + 1)

        @pl.when(z >= d)
        def _():
            attend(z - d)

        @pl.when((d > 0) & (z + d < nz))
        def _():
            wait_side(z + d)
            normalize(z + d)

        return carry

    lax.fori_loop(0, nz, level_step, 0)

    column = lax.broadcasted_iota(jnp.int32, (1, LANES), 1)
    log_total = jnp.zeros((rows, LANES), jnp.float32)
    for p in range(HEADS // 2):
        here = slice(p * LANES, (p + 1) * LANES)
        row_total = jnp.broadcast_to(jnp.sum(total[p], axis=1, keepdims=True), (pair, LANES))
        acc[:, here] = acc[:, here] / own_columns(row_total)
        lse = top[p] + jnp.log(row_total)
        log_total = jnp.where(column == 2 * p, lse[:rows], log_total)
        log_total = jnp.where(column == 2 * p + 1, lse[rows:], log_total)
    attn = acc[...].astype(jnp.bfloat16)
    attn_out[...] = attn
    loads[1].wait()
    resid = x32 + dot(attn, proj_w[...]) + proj_bias[...]
    unit, inverse = norm_parts(resid)
    n2 = (unit * gain_two[...] + shift_two[...]).astype(jnp.bfloat16)
    n2_out[...] = n2
    res_acc[...] = resid + down_bias[...]
    dh_acc[...] = jnp.zeros(dh_acc.shape, jnp.float32)
    loads[2].wait()
    loads[3].wait()
    slope = math.sqrt(2.0 / math.pi)

    def ff_step(t, carry):
        here = pl.ds(pl.multiple_of(t * FF_TILE, FF_TILE), FF_TILE)
        u = dot(n2_out[...], up_w[:, here]) + up_bias[:, here]
        square = u * u
        bend = jnp.tanh(slope * (u + 0.044715 * (square * u)))
        half = 0.5 * (1.0 + bend)
        g = (u * half).astype(jnp.bfloat16)
        slant = half + (0.5 * u) * (1.0 - bend * bend) * (slope * (1.0 + 3.0 * 0.044715 * square))
        g_out[:, here] = g
        res_acc[...] += dot(g, down_w[here])
        du32 = dot(e_ref[...], down_w[here], NT) * slant
        du = du32.astype(jnp.bfloat16)
        du_out[:, here] = du
        small_out[pl.ds(4 + t, 1)] = jnp.sum(du.astype(jnp.float32), axis=0, keepdims=True)
        dh_acc[...] += dot(du, up_w[:, here], NT)
        return carry

    lax.fori_loop(0, up_w.shape[1] // FF_TILE, ff_step, 0)
    layer_out[...] = res_acc[...].astype(jnp.bfloat16)
    dh = dh_acc[...]
    grad_rows = e_ref[...].astype(jnp.float32)
    dx = grad_rows + norm_back(dh, unit, inverse, gain_two[...])
    dx_out[...] = dx
    da = dx.astype(jnp.bfloat16)
    da_out[...] = da
    do = dot(da, proj_w[...], NT).astype(jnp.bfloat16)
    do_out[...] = do
    product = do.astype(jnp.float32) * acc[...]
    delta = jnp.zeros((rows, LANES), jnp.float32)
    left = first_half()
    for p in range(HEADS // 2):
        here = product[:, p * LANES : (p + 1) * LANES]
        one = jnp.sum(jnp.where(left, here, 0.0), axis=1, keepdims=True)
        two = jnp.sum(jnp.where(left, 0.0, here), axis=1, keepdims=True)
        delta = jnp.where(column == 2 * p, one, delta)
        delta = jnp.where(column == 2 * p + 1, two, delta)
    stats_out[0] = log_total
    stats_out[1] = delta
    small_out[0:1] = jnp.sum(dh * unit, axis=0, keepdims=True)
    small_out[1:2] = jnp.sum(dh, axis=0, keepdims=True)
    small_out[2:3] = jnp.sum(grad_rows, axis=0, keepdims=True)
    small_out[3:4] = jnp.sum(da.astype(jnp.float32), axis=0, keepdims=True)

    def left_all(found):
        for copy in found:
            copy.wait_send()

    left_all(side_copies(z, True))

    @pl.when(has_up)
    def _():
        left_all(up_copies(z, True))

    @pl.when(has_down)
    def _():
        left_all(down_copies(z, True))

    def sent(d, carry):
        @pl.when(z >= d)
        def _():
            left_all(side_copies(z - d))

            @pl.when(has_up)
            def _():
                left_all(up_copies(z - d))

        @pl.when(z + d < nz)
        def _():
            left_all(side_copies(z + d))

            @pl.when(has_down)
            def _():
                left_all(down_copies(z + d))

        return carry

    lax.fori_loop(1, nz, sent, 0)


def run_forward(x, e, lengths, gain_one, shift_one, qkv_weight, qkv_bias, proj_weight, proj_bias, gain_two, shift_two, up_weight, up_bias, down_weight, down_bias, peers):
    rows, width = x.shape
    hidden = up_weight.shape[1]
    nz = peers // 2
    bf, f32 = jnp.bfloat16, jnp.float32
    vmem = pl.BlockSpec(memory_space=pltpu.VMEM)
    smem = pl.BlockSpec(memory_space=pltpu.SMEM)
    hbm = pl.BlockSpec(memory_space=pl.ANY)
    dma = pltpu.SemaphoreType.DMA
    outs = [
        ((rows, width), bf), ((peers * rows, width), bf), ((rows, width), bf), ((rows, width), bf), ((rows, width), bf),
        ((rows, width), bf), ((rows, width), bf), ((rows, hidden), bf), ((rows, hidden), bf), ((rows, width), f32),
        ((2, rows, LANES), f32), ((4 + hidden // width, width), f32),
    ]
    vectors = [gain_one, shift_one, qkv_bias, proj_bias, gain_two, shift_two, up_bias, down_bias]
    return pl.pallas_call(
        functools.partial(forward_kernel, nz),
        out_shape=[(pltpu.VMEM if fits(peers, rows) and k in KEPT else jax.ShapeDtypeStruct)(*o) for k, o in enumerate(outs)],
        in_specs=[vmem, vmem, smem] + [vmem] * 8 + [hbm] * 4,
        out_specs=[vmem] * len(outs),
        scratch_shapes=[
            pltpu.VMEM((peers * rows, width), bf),
            pltpu.VMEM(qkv_weight.shape, bf),
            pltpu.VMEM(proj_weight.shape, bf),
            pltpu.VMEM(up_weight.shape, bf),
            pltpu.VMEM(down_weight.shape, bf),
            pltpu.VMEM((2 * rows, 2 * width), bf),
            pltpu.VMEM((HEADS // 2, 2 * rows, 2 * rows), f32),
            pltpu.VMEM((2 * rows, 2 * rows), f32),
            pltpu.VMEM((HEADS // 2, 2 * rows, LANES), f32),
            pltpu.VMEM((HEADS // 2, 2 * rows, LANES), f32),
            pltpu.VMEM((rows, width), f32),
            pltpu.VMEM((HEADS // 2, 2 * rows, LANES), bf),
            pltpu.VMEM((rows, width), f32),
            pltpu.VMEM((rows, width), f32),
            *[pltpu.VMEM((1, v.shape[0]), f32) for v in vectors],
            *[dma((nz, 2))] * 6, dma((4,)),
        ],
        compiler_params=pltpu.CompilerParams(collective_id=0, has_side_effects=True, vmem_limit_bytes=60 * 2**20),
        cost_estimate=pl.CostEstimate(flops=10**9, bytes_accessed=2 * 10**7, transcendentals=10**6),
    )(x, e, lengths, *vectors, qkv_weight, proj_weight, up_weight, down_weight)


def backward_kernel(
    nz, items, orders, schedule,
    x_ref, e_ref, ends, gain_flat, bias_flat, n1_all, q_ref, attn_ref, da_ref, do_ref, n2_ref, g_ref, du_ref, dx_ref,
    stats_ref, first_small, qkv_hbm,
    input_grad, qkv_out, proj_out, up_out, down_out, small_out,
    qkv_w, buf, inbox, total, do_all, rows_all, g_cat, e_cat, n2_cat, du_cat, attn_cat, da_cat, n1_cat, dqkv_cat,
    two_q, two_do, two_k, two_v, lse_cols, delta_cols, kv, n1_held, mask, dq, dk, dv, small_in, gain_one, qkv_bias,
    down_send, down_recv, side_send, side_recv, ssem, rsem, lsem,
):
    rows, width = x_ref.shape
    pair = 2 * rows
    place = Place()
    seq, batch = place.seq, place.batch
    z = seq // 2
    x = seq % 2
    core = place.bit(CORE)
    sems = Sems(ssem, rsem)
    local = Sems(lsem, lsem)
    load = pltpu.make_async_copy(qkv_hbm, qkv_w, local.take()[0])
    load.start()
    small_axes = [CORE, ACROSS] + seq_axes(2 * nz)
    has_up = z + 1 < nz
    has_down = z > 0
    above = (seq + 2, batch)
    below = (seq - 2, batch)
    beside = (seq + 1 - 2 * x, batch)
    barrier = pltpu.get_barrier_semaphore()
    for axis in small_axes:
        pl.semaphore_signal(barrier, inc=1, device_id=place.partner(axis), device_id_type=MESH_ID)

    @pl.when(has_up)
    def _():
        pl.semaphore_signal(barrier, inc=1, device_id=above, device_id_type=MESH_ID)

    @pl.when(has_down)
    def _():
        pl.semaphore_signal(barrier, inc=1, device_id=below, device_id_type=MESH_ID)

    gain_one[...] = as_row(gain_flat)
    qkv_bias[...] = as_row(bias_flat)
    for k in range(2):
        rows_all[seq, k * TILE : (k + 1) * TILE] = stats_ref[k].T[:TILE]
    pl.semaphore_wait(barrier, len(small_axes) + has_up.astype(jnp.int32) + has_down.astype(jnp.int32))

    def cols(half, size):
        return pl.ds(pl.multiple_of(half * size, LANES), size)

    def to_core(source, into):
        return pltpu.make_async_remote_copy(
            source, into.at[rows:], *sems.take(), device_id=place.partner(CORE), device_id_type=MESH_ID
        )

    def keep_own(source, into):
        return pltpu.make_async_copy(source, into.at[:rows], local.take()[0])

    def exchange(ref, into, halved):
        size = into.shape[1]
        give = ref.at[:, cols(1 - core, size)] if halved else ref
        keep = ref.at[:, cols(core, size)] if halved else ref
        copies = [to_core(give, into), keep_own(keep, into)]
        for copy in copies:
            copy.start()
        return copies

    def done(copies):
        for copy in copies:
            copy.wait()

    down_parts = exchange(g_ref, g_cat, True) + exchange(e_ref, e_cat, False)
    up_parts = exchange(n2_ref, n2_cat, False) + exchange(du_ref, du_cat, True)

    def do_block(level, side):
        return do_all.at[rows_at((2 * level + side) * rows, rows)]

    def do_copies(level, side, to, send_sem, recv_sem, own=False):
        source = do_ref if own else do_block(level, side)
        stat = rows_all.at[2 * level + side]
        return [
            pltpu.make_async_remote_copy(
                source, do_block(level, side), send_sem.at[level, 0], recv_sem.at[level, 0], device_id=to, device_id_type=MESH_ID
            ),
            pltpu.make_async_remote_copy(
                stat, stat, send_sem.at[level, 1], recv_sem.at[level, 1], device_id=to, device_id_type=MESH_ID
            ),
        ]

    def down_copies(level, own=False):
        return do_copies(level, x, below, down_send, down_recv, own)

    def side_copies(level, own=False):
        return do_copies(level, x, beside, side_send, side_recv, own)

    def begin(copies):
        for copy in copies:
            copy.start()

    @pl.when(has_down)
    def _():
        begin(down_copies(z, True))

    begin(side_copies(z, True))
    do_all[rows_at(seq * rows, rows)] = do_ref[...]

    spread = [1]

    def spread_until(last):
        while spread[0] <= min(last, nz - 1):
            d = spread[0]
            spread[0] += 1

            @pl.when(z + d < nz)
            def _():
                level = z + d
                for copy in down_copies(level):
                    copy.wait_recv()

                @pl.when(has_down)
                def _():
                    begin(down_copies(level))

                begin(side_copies(level))

    def spread_end():
        def sent(copies):
            for copy in copies:
                copy.wait_send()

        sent(side_copies(z, True))

        @pl.when(has_down)
        def _():
            sent(down_copies(z, True))

        def each(level, carry):
            sent(side_copies(level))

            @pl.when(has_down)
            def _():
                sent(down_copies(level))

            return carry

        lax.fori_loop(z + 1, nz, each, 0)

    slots = []
    at = used = 0
    for size, kind, _ in items:
        slots.append((at, size, orders[kind], used))
        at += size
        used += inbox_rows(size, orders[kind])
    places = [(name, r) for _, _, (name, r) in items]

    def destination(name, r, size):
        half = width // 2
        if name == "down":
            return down_out.at[rows_at(core * down_out.shape[0] // 2 + r, size)]
        if name[:2] == "up":
            return up_out.at[r : r + size, pl.ds(pl.multiple_of((core * (up_out.shape[1] // width // 2) + int(name[2:])) * width, width), width)]
        if name == "proj":
            return proj_out.at[rows_at(core * half + r, size)]
        return qkv_out.at[rows_at(core * half + r, size), int(name[3:]) * width : (int(name[3:]) + 1) * width]

    ready = set()

    def item_task(k):
        at, size, order, used = slots[k]
        name, r = places[k]
        if name[:2] not in ready:
            ready.add(name[:2])
            done(parts.get(name[:2], []))
        left, right = operands(name)
        buf[at : at + size] = dot(left[:, r : r + size], right, TN).astype(jnp.bfloat16)
        yield from sum_item(place, sems, buf, at, size, order, inbox, used, total, ending)
        there = destination(name, r, size)
        here = total.at[rows_at(at, size)]
        keep = pltpu.make_async_copy(here, there, local.take()[0])
        give = pltpu.make_async_remote_copy(here, there, *sems.take(), device_id=place.partner(CORE), device_id_type=MESH_ID)
        keep.start()
        give.start()
        leaving.extend([keep, give])

    def small_task():
        for k, axis in enumerate(small_axes):
            copy = pltpu.make_async_remote_copy(
                small_out, small_in.at[k], *sems.take(), device_id=place.partner(axis), device_id_type=MESH_ID
            )
            copy.start()
            yield
            copy.wait()
            small_out[...] += small_in[k]

    leaving, ending = [], []

    def operands(name):
        if name == "down":
            return g_cat, e_cat[...]
        if name == "proj":
            return attn_cat, da_cat[...]
        j = int(name[-1])
        block = slice(j * width, (j + 1) * width)
        return (n2_cat, du_cat[:, block]) if name[:2] == "up" else (n1_cat, dqkv_cat[:, block])

    small_out[:8] = first_small[...]
    own_n1 = rows_at(seq * rows, rows)
    parts = {
        "do": down_parts,
        "up": up_parts,
        "pr": exchange(attn_ref, attn_cat, True) + exchange(da_ref, da_cat, False),
        "qk": exchange(n1_all.at[own_n1], n1_cat, True),
    }

    load.wait()
    scale = jnp.asarray(1.0 / math.sqrt(HD), jnp.bfloat16)

    chunk_sem = local.take()[0]

    def n1_chunk(level):
        copy = pltpu.make_async_copy(n1_all.at[rows_at(level * pair, pair)], n1_held, chunk_sem)
        copy.start()
        copy.wait()
        return n1_held[...]

    def prepare():
        n1_chunk(z)
        mine = n1_held[rows_at(x * rows, rows)]
        own_kv = (dot(mine, qkv_w[:, width:]) + qkv_bias[:, width:]).astype(jnp.bfloat16)
        for p in range(HEADS // 2):
            here = slice(p * LANES, (p + 1) * LANES)
            two_q[p] = both_heads(q_ref[:, here])
            two_do[p] = both_heads(do_ref[:, here])
            two_k[p] = both_heads(own_kv[:, here])
            two_v[p] = both_heads(own_kv[:, width + p * LANES : width + (p + 1) * LANES])
            for k, into in enumerate((lse_cols, delta_cols)):
                for h in range(2):
                    column = stats_ref[k, :, 2 * p + h : 2 * p + h + 1]
                    into[p, h * rows : (h + 1) * rows] = jnp.broadcast_to(column, (rows, LANES))
        dq[...] = jnp.zeros(dq.shape, jnp.float32)
        dk[...] = jnp.zeros(dk.shape, jnp.float32)
        dv[...] = jnp.zeros(dv.shape, jnp.float32)

    def columns_of(p):
        return pl.ds(pl.multiple_of(p * LANES, LANES), LANES)

    def query_step(level):
        n1 = n1_chunk(level)
        kv[...] = (dot(n1, qkv_w[:, width:]) + qkv_bias[:, width:]).astype(jnp.bfloat16)
        one = mask_of(ends, places_down(seq * rows, rows), places_along(level * pair, pair))
        mask[:rows] = one
        mask[rows:] = one

        def each(p, carry):
            k_pair = kv[:, columns_of(p)]
            v_pair = kv[:, columns_of(p + HEADS // 2)]
            s = dot(two_q[p], k_pair, NT)
            along = dot(two_do[p], v_pair, NT)
            low = mask[...] - lse_cols[p][:, :1]
            plus = jnp.exp(low + s)
            minus = jnp.exp(low - s)
            ds = ((plus + minus) * along - (plus - minus) * delta_cols[p][:, :1]).astype(jnp.bfloat16)
            dq[:, columns_of(p)] += own_columns(dot(ds, k_pair))
            return carry

        lax.fori_loop(0, HEADS // 2, each, 0, unroll=UNROLL)

    def key_step(level):
        side = 1 - x
        for copy in do_copies(level, side, beside, side_send, side_recv):
            copy.wait_recv()
        here = rows_at(level * pair, pair)
        n1 = n1_chunk(level)
        kv[:, :width] = (dot(n1, qkv_w[:, :width]) + qkv_bias[:, :width]).astype(jnp.bfloat16) * scale
        one = mask_of(ends, places_along(level * pair, pair), places_down(seq * rows, rows))
        mask[:rows] = one
        mask[rows:] = one

        def stat(row):
            both = [rows_all[2 * level + k, pl.ds(row, 1)] for k in range(2)]
            return jnp.concatenate(both, axis=1)

        def stat_rows(k, p):
            both = [jnp.broadcast_to(stat(k * TILE + 2 * p + h), (rows, pair)) for h in range(2)]
            return jnp.concatenate(both, axis=0)

        def each(p, carry):
            q_pair = kv[:, columns_of(p)]
            do_pair = do_all[here, columns_of(p)]
            s = dot(two_k[p], q_pair, NT)
            along = dot(two_v[p], do_pair, NT)
            low = mask[...] - stat_rows(0, p)
            plus = jnp.exp(low + s)
            minus = jnp.exp(low - s)
            signed = plus - minus
            ds = ((plus + minus) * along - signed * stat_rows(1, p)).astype(jnp.bfloat16)
            dk[:, columns_of(p)] += own_columns(dot(ds, q_pair))
            dv[:, columns_of(p)] += own_columns(dot(signed.astype(jnp.bfloat16), do_pair))
            return carry

        lax.fori_loop(0, HEADS // 2, each, 0, unroll=UNROLL)

    def one_step(t):
        @pl.when(t <= z)
        def _():
            query_step(z - t)

        @pl.when(t > z)
        def _():
            key_step(t - 1)

    def steps_piece(first, last):
        def piece():
            spread_until(last)
            if last - first == 1:
                one_step(first)
            else:

                def body(t, carry):
                    one_step(t)
                    return carry

                lax.fori_loop(first, last, body, 0)

        return piece

    def finish():
        dqkv = jnp.concatenate(
            [
                (dq[...] * (1.0 / math.sqrt(HD))).astype(jnp.bfloat16),
                dk[...].astype(jnp.bfloat16),
                dv[...].astype(jnp.bfloat16),
            ],
            axis=1,
        )
        dqkv_cat[:rows] = dqkv
        send = to_core(dqkv_cat.at[:rows], dqkv_cat)
        send.start()
        dh = dot(dqkv, qkv_w[...], NT)
        unit, inverse = norm_parts(x_ref[...].astype(jnp.float32))
        input_grad[...] = (dx_ref[...] + norm_back(dh, unit, inverse, gain_one[...])).astype(jnp.bfloat16)
        sums = jnp.sum(dqkv.astype(jnp.float32), axis=0, keepdims=True)
        for k in range(3):
            small_out[8 + k : 9 + k] = sums[:, k * width : (k + 1) * width]
        small_out[11:12] = jnp.sum(dh * unit, axis=0, keepdims=True)
        small_out[12:13] = jnp.sum(dh, axis=0, keepdims=True)
        small_out[13:16] = jnp.zeros((3, width), jnp.float32)
        parts["qk"].append(send)

    groups = min(nz + 1, GROUPS)
    cuts = [(nz + 1) * k // groups for k in range(groups + 1)]
    pieces = [prepare] + [steps_piece(a, b) for a, b in zip(cuts, cuts[1:])] + [finish]
    tasks = [item_task(k) for k in range(len(items))] + [small_task()]
    for token in schedule:
        if token < 0:
            pieces[-1 - token]()
        else:
            next(tasks[token], None)
    for copy in leaving:
        copy.wait()
    for sent in ending:
        sent()
    spread_end()


def in_turns(items, counts, n_pieces):
    early = [k for k, (_, _, (name, _)) in enumerate(items) if name[:3] != "qkv"]
    late = [k for k in range(len(counts)) if k not in early]
    tokens, piece = [], 0
    for waiting in (early, late):
        live = []
        while live or waiting:
            live, waiting = live + waiting[:3], waiting[3:]
            for k in live:
                tokens.append(k)
                if len(tokens) % PACE == 0 and piece < n_pieces:
                    piece += 1
                    tokens.append(-piece)
            live = [k for k in live if tokens.count(k) < counts[k]]
        while piece < n_pieces:
            piece += 1
            tokens.append(-piece)
    return tokens


def fits(peers, rows):
    return peers * rows <= 2048


def plan_items(width, hidden):
    half = width // 2

    def cut(name, size):
        return [(min(ITEM, size - r), (name, r)) for r in range(0, size, ITEM)]

    found = cut("down", hidden // 2)
    for j in range(hidden // 2 // width):
        found += cut(f"up{j}", width)
    found += cut("proj", half)
    for j in range(3):
        found += cut(f"qkv{j}", half)
    return [(size, int(KINDS[k % len(KINDS)]), where) for k, (size, where) in enumerate(found)]


def run_backward(x, e, lengths, gain_one, qkv_weight, qkv_bias, kept, peers):
    n1_all, q, attn, da, do, n2, g, du, dx, stats, small = kept
    rows, width = x.shape
    hidden = g.shape[1]
    nz = peers // 2
    bf, f32 = jnp.bfloat16, jnp.float32
    orders = axis_orders()
    stages = 2 + len(seq_axes(peers))
    items = plan_items(width, hidden)
    used = sum(inbox_rows(size, orders[kind]) for size, kind, _ in items)
    height = sum(size for size, _, _ in items)
    turns = [1 + 2 * (2 + len(hop_groups(nz)))] * len(items) + [1 + stages]
    n_pieces = 2 + min(nz + 1, GROUPS)
    schedule = SCHEDULE
    if sorted(schedule) != sorted([k for k, n in enumerate(turns) for _ in range(n)] + [-1 - k for k in range(n_pieces)]):
        schedule = in_turns(items, turns, n_pieces)
    copies = 9 * len(items) + stages + 8
    vmem = pl.BlockSpec(memory_space=pltpu.VMEM)
    smem = pl.BlockSpec(memory_space=pltpu.SMEM)
    hbm = pl.BlockSpec(memory_space=pl.ANY)
    dma = pltpu.SemaphoreType.DMA
    out = jax.ShapeDtypeStruct
    small_mesh = fits(peers, rows)
    grad = pltpu.VMEM if small_mesh else out
    stack = (HEADS // 2, 2 * rows, LANES)
    return pl.pallas_call(
        functools.partial(backward_kernel, nz, items, orders, schedule),
        out_shape=[
            grad((rows, width), bf), grad((width, 3 * width), bf), grad((width, width), bf), grad((width, hidden), bf),
            grad((hidden, width), bf), out((16, width), f32),
        ],
        in_specs=[vmem, hbm, smem, vmem, vmem]
        + [vmem if k in (2, 5, 9, 10, 11) or (small_mesh and k in KEPT) else hbm for k in range(1, 12)]
        + [hbm],
        out_specs=[vmem] + [vmem if small_mesh else hbm] * 4 + [vmem],
        scratch_shapes=[
            pltpu.VMEM(qkv_weight.shape, bf),
            pltpu.VMEM((height, width), bf),
            pltpu.VMEM((used, width), bf),
            pltpu.VMEM((height, width), bf),
            pltpu.VMEM((peers * rows, width), bf),
            pltpu.VMEM((peers, 2 * TILE, LANES), f32),
            pltpu.VMEM((2 * rows, hidden // 2), bf),
            pltpu.VMEM((2 * rows, width), bf),
            pltpu.VMEM((2 * rows, width), bf),
            pltpu.VMEM((2 * rows, hidden // 2), bf),
            pltpu.VMEM((2 * rows, width // 2), bf),
            pltpu.VMEM((2 * rows, width), bf),
            pltpu.VMEM((2 * rows, width // 2), bf),
            pltpu.VMEM((2 * rows, 3 * width), bf),
            pltpu.VMEM(stack, bf), pltpu.VMEM(stack, bf), pltpu.VMEM(stack, bf), pltpu.VMEM(stack, bf),
            pltpu.VMEM(stack, f32), pltpu.VMEM(stack, f32),
            pltpu.VMEM((2 * rows, 2 * width), bf),
            pltpu.VMEM((2 * rows, width), bf),
            pltpu.VMEM((2 * rows, 2 * rows), f32),
            pltpu.VMEM((rows, width), f32), pltpu.VMEM((rows, width), f32), pltpu.VMEM((rows, width), f32),
            pltpu.VMEM((stages, 16, width), f32),
            pltpu.VMEM((1, width), f32), pltpu.VMEM((1, 3 * width), f32),
            dma((nz, 2)), dma((nz, 2)), dma((nz, 2)), dma((nz, 2)),
            dma((copies,)), dma((copies,)), dma((len(items) + 10,)),
        ],
        compiler_params=pltpu.CompilerParams(collective_id=1, has_side_effects=True, vmem_limit_bytes=(K2_LIMIT if small_mesh else 62) * 2**20),
    )(x, e, lengths, gain_one, qkv_bias, n1_all, q, attn, da, do, n2, g, du, dx, stats, small, qkv_weight)


def widen_kernel(grads, small, passed, outs, rests, passed_outs, slots, sems, pass_sems):
    moved = [pltpu.make_async_copy(a, b, pass_sems.at[k]) for k, (a, b) in enumerate(zip(passed, passed_outs))]
    for copy in moved:
        copy.start()
    for k, (grad, out) in enumerate(zip(grads, outs)):
        slot = slots[k]
        rows = slot.shape[1]
        flying = []
        for n in range(grad.shape[0] // rows):
            at = n % slot.shape[0]
            if len(flying) >= slot.shape[0]:
                flying[n - slot.shape[0]].wait()

            def body(i, carry, n=n, at=at, grad=grad, slot=slot, rows=rows):
                here = pl.ds(pl.multiple_of(i * TILE, TILE), TILE)
                there = pl.ds(pl.multiple_of(n * rows + i * TILE, TILE), TILE)
                slot[at, here] = grad[there].astype(jnp.float32)
                return carry

            lax.fori_loop(0, rows // TILE, body, 0)
            copy = pltpu.make_async_copy(slot.at[at], out.at[n * rows : (n + 1) * rows], sems.at[k, n % slot.shape[0]])
            copy.start()
            flying.append(copy)
        moved += flying[-slot.shape[0] :]
    for (first, count), rest in zip(SMALL_ROWS, rests):
        for k in range(count):
            rest[k * small.shape[1] : (k + 1) * small.shape[1]] = small[first + k : first + k + 1].reshape(small.shape[1])
    for copy in moved:
        copy.wait()


def widen(grads, small, passed):
    width = small.shape[1]
    depth = 3
    sizes = [(g.shape, max(TILE, WIDEN // g.shape[1] // TILE * TILE)) for g in grads]
    vmem = pl.BlockSpec(memory_space=pltpu.VMEM)
    hbm = pl.BlockSpec(memory_space=pl.ANY)
    n = len(grads)
    m = len(SMALL_ROWS)
    q = len(passed)

    def kernel(*refs):
        found = []
        for count in (n, 1, q, n, m, q, n):
            found.append(refs[:count])
            refs = refs[count:]
        found[1] = found[1][0]
        widen_kernel(*found, *refs)

    return pl.pallas_call(
        kernel,
        out_shape=[jax.ShapeDtypeStruct(g.shape, jnp.float32) for g in grads]
        + [jax.ShapeDtypeStruct((count * width,), jnp.float32) for _, count in SMALL_ROWS]
        + [jax.ShapeDtypeStruct(p.shape, p.dtype) for p in passed],
        in_specs=[vmem] * (n + 1) + [vmem] * q,
        out_specs=[hbm] * n + [vmem] * m + [hbm] * q,
        scratch_shapes=[pltpu.VMEM((depth, rows, shape[1]), jnp.float32) for shape, rows in sizes]
        + [pltpu.SemaphoreType.DMA((n, depth)), pltpu.SemaphoreType.DMA((q,))],
        compiler_params=pltpu.CompilerParams(vmem_limit_bytes=34 * 2**20),
    )(*grads, small, *passed)


def per_device(
    inputs,
    cotangent,
    doc_lengths,
    gain_one,
    shift_one,
    qkv_weight,
    qkv_bias,
    proj_weight,
    proj_bias,
    gain_two,
    shift_two,
    up_weight,
    up_bias,
    down_weight,
    down_bias,
):
    peers = lax.axis_size("seq")
    width = inputs.shape[2]
    layer_out, *kept = run_forward(
        inputs[0], cotangent[0], doc_lengths, gain_one, shift_one, qkv_weight, qkv_bias, proj_weight, proj_bias, gain_two, shift_two,
        up_weight, up_bias, down_weight, down_bias, peers,
    )
    input_grad, qkv, proj, up, down, small = run_backward(
        inputs[0], cotangent[0], doc_lengths, gain_one, qkv_weight, qkv_bias, kept, peers
    )
    large = (qkv, proj, up, down)
    if fits(peers, inputs.shape[1]):
        qkv, proj, up, down, *rest, layer_out, input_grad = widen(large, small, (layer_out, input_grad))
    else:
        qkv, proj, up, down = (g.astype(jnp.float32) for g in large)
        rest = [small[first : first + count].reshape(-1) for first, count in SMALL_ROWS]
    gain_1, shift_1, qkv_b, proj_b, gain_2, shift_2, up_b, down_b = rest
    return (
        layer_out[None], input_grad[None], gain_1, shift_1, qkv, qkv_b, proj, proj_b, gain_2, shift_2, up, up_b, down, down_b,
    )


def solution(mesh):
    in_specs = (
        P("batch", "seq", None),
        P("batch", "seq", None),
        P("batch", None),
        P(),
        P(),
        P(),
        P(),
        P(),
        P(),
        P(),
        P(),
        P(),
        P(),
        P(),
        P(),
    )
    out_specs = (
        P("batch", "seq", None),
        P("batch", "seq", None),
        P(),
        P(),
        P(),
        P(),
        P(),
        P(),
        P(),
        P(),
        P(),
        P(),
        P(),
        P(),
    )
    return jax.shard_map(
        per_device, mesh=mesh, in_specs=in_specs, out_specs=out_specs, check_vma=False
    )
```

```python
import functools
import math

import jax
import jax.numpy as jnp
from jax import lax
from jax.experimental import pallas as pl
from jax.experimental.pallas import tpu as pltpu
from jax.sharding import PartitionSpec as P

HEADS = 12
HD = 64


norm_eps = 1e-05
masked_low = -1e30


MESH_ID = pl.DeviceIdType.MESH
TILE = 16
LANES = 128
FF_TILE = 768
ITEM = 256
KINDS = "11133300404055354145"
GROUPS = 5
PACE = 8
UNROLL = 2
FAR = ("down", "up")
TURNED = 2
K2_LIMIT = 45
KEPT = (0,)
WIDEN = 128 * 2304
SMALL_ROWS = ((11, 1), (12, 1), (8, 3), (3, 1), (0, 1), (1, 1), (4, 4), (2, 1))
SCHEDULE = (
    -1, 12, -2, 13, 12, 0, 6, 13, -3, 12, 6, 0, 1, 2, 9, 10, 11, 13, 6, 8, 7, -4, 6, 11, 10, 4, 12, 0, 3, 2, 5, 6, 7,
    -5, 2, 9, 1, 13, 12, 11, -6, 9, 2, 1, 4, 6, 8, 3, 10, -7, 18, 4, 19, 6, 14, 5, 3, 8, 16, 1, 7, 10, 9, 6, 19, 7, 4,
    15, 18, 12, 17, 5, 3, 20, 15, 11, 0, 7, 9, 20, 14, 5, 18, 3, 2, 16, 7, 15, 4, 9, 13, 3, 19, 16, 10, 7, 5, 18, 5,
    6, 17, 8, 17, 12, 14, 15, 2, 1, 19, 7, 16, 13, 10, 15, 14, 20, 18, 3, 8, 14, 16, 0, 18, 17, 2, 7, 10, 1, 15, 11,
    9, 2, 14, 13, 16, 19, 17, 5, 9, 18, 1, 3, 0, 2, 4, 19, 8, 17, 7, 14, 18, 11, 15, 10, 20, 5, 0, 14, 19, 9, 4, 3,
    18, 16, 15, 14, 19, 13, 16, 5, 4, 1, 10, 1, 8, 11, 3, 16, 15, 11, 8, 12, 0, 5, 17, 18, 15, 8, 9, 19, 10, 12, 14,
    20, 17, 11, 4, 12, 13, 16, 0, 14, 17, 20, 15, 8, 13, 19, 12, 6, 4, 17, 16, 0, 17, 18, 11, 19, 13, 1, 2,
)


class Place:
    def __init__(self):
        self.seq = lax.axis_index("seq")
        self.batch = lax.axis_index("batch")
        self.level = self.seq // 2
        self.levels = lax.axis_size("seq") // 2

    def bit(self, axis):
        name, k = axis
        return ((self.seq if name == "seq" else self.batch) // (1 << k)) % 2

    def partner(self, axis):
        name, k = axis
        step = (1 << k) * (1 - 2 * self.bit(axis))
        if name == "seq":
            return (self.seq + step, self.batch)
        return (self.seq, self.batch + step)


CORE = ("batch", 0)
ACROSS = ("batch", 1)
LEVELS = ("seq", None)


def seq_axes(peers):
    return [("seq", k) for k in range((peers - 1).bit_length())]


def axis_orders():
    x, y, z = ("seq", 0), ACROSS, LEVELS
    return [[x, y, z], [y, z, x], [z, x, y], [y, x, z], [x, z, y], [z, y, x]]


class Sems:
    def __init__(self, send, recv):
        self.send, self.recv, self.count = send, recv, 0

    def take(self):
        k = self.count
        self.count += 1
        return self.send.at[k], self.recv.at[k]


def rows_at(start, size):
    return pl.ds(pl.multiple_of(start, TILE), size)


def add_rows(into, one, at, other, other_at, rows):
    step = 32 if rows % 32 == 0 else TILE

    def body(i, carry):
        here = rows_at(at + i * step, step)
        there = rows_at(other_at + i * step, step)
        both = one[here].astype(jnp.float32) + other[there].astype(jnp.float32)
        into[here] = both.astype(into.dtype)
        return carry

    lax.fori_loop(0, rows // step, body, 0)


def sum_item(place, sems, buf, at, rows, order, inbox, used, total, leaving, begun=False):
    z, nz = place.level, place.levels
    above, below = (place.seq + 2, place.batch), (place.seq - 2, place.batch)
    at_end = (z == 0) | (z == nz - 1)
    low, length, held, plan = at, rows, None, []

    def where(condition, act):
        if condition is None:
            act()
        else:
            pl.when(condition)(act)

    def remote(source, into, to):
        return pltpu.make_async_remote_copy(source, into, *sems.take(), device_id=to, device_id_type=MESH_ID)

    def part_of(ref, start, size):
        return ref.at[rows_at(start, size)]

    def chain(up, down, step_up, step_down):
        pl.when(z == 0)(up.start)
        pl.when(z == nz - 1)(down.start)
        yield
        for first, last in hop_groups(nz):
            for hop, copy, step in ((z, up, step_up), (nz - 1 - z, down, step_down)):
                here = (hop >= first) & (hop < last)

                @pl.when(here)
                def _(copy=copy, step=step):
                    copy.wait_recv()
                    step(False)

                @pl.when(here & (hop < nz - 1))
                def _(copy=copy):
                    copy.start()

                @pl.when(here & (hop == nz - 1))
                def _(step=step):
                    step(True)

            if last < nz:
                yield

        def sent():
            pl.when(z < nz - 1)(up.wait_send)
            pl.when(z > 0)(down.wait_send)

        leaving.append(sent)

    for k, axis in enumerate(order):
        last = k == len(order) - 1
        part = length // 2
        if axis == LEVELS:
            ups, downs = low + part, low

            def adder(start, slot, part=part, last=last):
                def step(end):
                    if not last:
                        if not end:
                            add_rows(buf, buf, start, inbox, slot, part)
                    elif end:
                        add_rows(total, buf, start, inbox, slot, part)

                return step

            def adder_last(start, slot, hop, part=part):
                def step(end):
                    if end:
                        add_rows(total, buf, start, inbox, slot, part)
                    else:
                        pl.when(hop < nz - 1)(lambda: add_rows(buf, buf, start, inbox, slot, part))

                return step

            make_up = adder_last(ups, used, z) if last else adder(ups, used)
            make_down = adder_last(downs, used + part, nz - 1 - z) if last else adder(downs, used + part)
            yield from chain(
                remote(part_of(buf, ups, part), part_of(inbox, used, part), above),
                remote(part_of(buf, downs, part), part_of(inbox, used + part, part), below),
                make_up,
                make_down,
            )
            used += 2 * part
            plan.append((axis, low, part, held))
            low = low + jnp.where(z == nz - 1, part, 0)
            held = at_end
        else:
            bit = place.bit(axis)
            keep, give = low + bit * part, low + (1 - bit) * part
            if begun and k == 0:
                plan.append((axis, keep, part, held))
                low, length = keep, part
                continue
            copy = remote(part_of(buf, give, part), part_of(inbox, used, part), place.partner(axis))
            where(held, copy.start)
            yield

            def take(copy=copy, keep=keep, used=used, part=part, last=last):
                copy.wait()
                add_rows(total if last else buf, buf, keep, inbox, used, part)

            where(held, take)
            used += part
            plan.append((axis, keep, part, held))
            low = keep
        length = part
    for axis, low, part, held in reversed(plan):
        if axis == LEVELS:
            ups, downs = part_of(total, low + part, part), part_of(total, low, part)
            nothing = lambda end: None
            yield from chain(remote(downs, downs, above), remote(ups, ups, below), nothing, nothing)
        else:
            here = part_of(total, low, part)
            copy = remote(here, here, place.partner(axis))
            where(held, copy.start)
            yield
            where(held, copy.wait)


def hop_groups(levels):
    groups = min(levels - 1, 3)
    cuts = [1 + (levels - 1) * k // groups for k in range(groups + 1)]
    return list(zip(cuts, cuts[1:]))


def inbox_rows(rows, order, begun):
    used = 0
    for k, axis in enumerate(order):
        rows //= 2
        if begun and k == 0:
            continue
        used += 2 * rows if axis == LEVELS else rows
    return used


def dot(a, b, dims=((1,), (0,))):
    return lax.dot_general(a, b, (dims, ((), ())), preferred_element_type=jnp.float32)


NT = ((1,), (1,))
TN = ((0,), (0,))


def norm_parts(rows):
    center = rows - jnp.mean(rows, axis=-1, keepdims=True)
    spread = jnp.mean(center * center, axis=-1, keepdims=True)
    inverse = lax.rsqrt(spread + norm_eps)
    return center * inverse, inverse


def norm_back(grad, unit, inverse, gain):
    scaled = grad * gain
    along = jnp.mean(scaled * unit, axis=-1, keepdims=True)
    return inverse * (scaled - jnp.mean(scaled, axis=-1, keepdims=True) - unit * along)


def doc_ids(lengths, places):
    found = jnp.zeros(places.shape, jnp.int32)
    end = 0
    for k in range(lengths.shape[1]):
        end += lengths[0, k]
        found += (end <= places).astype(jnp.int32)
    return found


def as_row(ref):
    return ref[...].reshape(1, -1)


def places_down(first, rows):
    return first + lax.broadcasted_iota(jnp.int32, (rows, 1), 0)


def places_along(first, rows):
    return first + lax.broadcasted_iota(jnp.int32, (1, rows), 1)


def mask_of(ends, q_places, k_places):
    allowed = (doc_ids(ends, q_places) == doc_ids(ends, k_places)) & (k_places <= q_places)
    return jnp.where(allowed, 0.0, masked_low)


def first_half():
    return lax.broadcasted_iota(jnp.int32, (1, LANES), 1) < HD


def both_heads(pair):
    left = first_half()
    none = jnp.zeros_like(pair)
    return jnp.concatenate([jnp.where(left, pair, none), jnp.where(left, none, pair)], axis=0)


def own_columns(stacked):
    rows = stacked.shape[0] // 2
    return jnp.where(first_half(), stacked[:rows], stacked[rows:])


def lanes(p):
    return pl.ds(p * LANES, LANES)


def forward_kernel(
    nz, x_ref, e_ref, ends, gain_one1, shift_one1, qkv_bias1, proj_bias1, gain_two1, shift_two1, up_bias1, down_bias1,
    qkv_hbm, proj_hbm, up_hbm, down_hbm,
    layer_out, n1_all, q_out, attn_out, da_out, do_out, n2_out, g_out, du_out, dx_out, stats_out, small_out,
    x_all, qkv_w, proj_w, up_w, down_w, kv, scores, mask, top, total, acc, two_q, res_acc, dh_acc,
    gain_one, shift_one, qkv_bias, proj_bias, gain_two, shift_two, up_bias, down_bias,
    up_send, up_recv, down_send, down_recv, side_send, side_recv, w_sem,
):
    rows, width = x_ref.shape
    pair = 2 * rows
    seq = lax.axis_index("seq")
    batch = lax.axis_index("batch")
    z = seq // 2
    x = seq % 2
    loads = [
        pltpu.make_async_copy(hbm, vmem, w_sem.at[k])
        for k, (hbm, vmem) in enumerate(
            [(qkv_hbm, qkv_w), (proj_hbm, proj_w), (up_hbm, up_w), (down_hbm, down_w)]
        )
    ]
    loads[0].start()
    barrier = pltpu.get_barrier_semaphore()
    has_up = z + 1 < nz
    has_down = z > 0
    above = (seq + 2, batch)
    below = (seq - 2, batch)
    beside = (seq + 1 - 2 * x, batch)

    @pl.when(has_up)
    def _():
        pl.semaphore_signal(barrier, inc=1, device_id=above, device_id_type=MESH_ID)

    @pl.when(has_down)
    def _():
        pl.semaphore_signal(barrier, inc=1, device_id=below, device_id_type=MESH_ID)

    pl.semaphore_signal(barrier, inc=1, device_id=beside, device_id_type=MESH_ID)
    pl.semaphore_wait(barrier, 1 + has_up.astype(jnp.int32) + has_down.astype(jnp.int32))
    for load in loads[1:]:
        load.start()

    half = rows // 2

    def block(level, side, h):
        return x_all.at[rows_at((2 * level + side) * rows + h * half, half)]

    def copies(level, side, to, send_sem, recv_sem, own=False):
        found = []
        for h in range(2):
            source = x_ref.at[h * half : (h + 1) * half] if own else block(level, side, h)
            found.append(
                pltpu.make_async_remote_copy(
                    source, block(level, side, h), send_sem.at[level, h], recv_sem.at[level, h],
                    device_id=to, device_id_type=MESH_ID,
                )
            )
        return found

    def up_copies(level, own=False):
        return copies(level, x, above, up_send, up_recv, own)

    def down_copies(level, own=False):
        return copies(level, x, below, down_send, down_recv, own)

    def side_copies(level, own=False):
        return copies(level, x, beside, side_send, side_recv, own)

    def wait_side(level):
        for copy in copies(level, 1 - x, beside, side_send, side_recv):
            copy.wait_recv()

    own_up, own_side, own_down = up_copies(z, True), side_copies(z, True), down_copies(z, True)
    for h in range(2):

        @pl.when(has_up)
        def _(h=h):
            own_up[h].start()

        own_side[h].start()

        @pl.when(has_down)
        def _(h=h):
            own_down[h].start()

    vectors = [gain_one, shift_one, qkv_bias, proj_bias, gain_two, shift_two, up_bias, down_bias]
    flats = [gain_one1, shift_one1, qkv_bias1, proj_bias1, gain_two1, shift_two1, up_bias1, down_bias1]
    for vector, flat in zip(vectors, flats):
        vector[...] = as_row(flat)
    x_all[rows_at(seq * rows, rows)] = x_ref[...]
    x32 = x_ref[...].astype(jnp.float32)
    unit_one, _ = norm_parts(x32)
    mine = (unit_one * gain_one[...] + shift_one[...]).astype(jnp.bfloat16)
    top[...] = jnp.full(top.shape, masked_low, jnp.float32)
    total[...] = jnp.zeros(total.shape, jnp.float32)
    acc[...] = jnp.zeros(acc.shape, jnp.float32)
    loads[0].wait()
    q = (dot(mine, qkv_w[:, :width]) + qkv_bias[:, :width]).astype(jnp.bfloat16)
    q = q * jnp.asarray(1.0 / math.sqrt(HD), jnp.bfloat16)
    q_out[...] = q
    for p in range(HEADS // 2):
        two_q[p] = both_heads(q[:, p * LANES : (p + 1) * LANES])

    def pass_on(d):
        @pl.when(z >= d)
        def _():
            level = z - d
            ups, sides = up_copies(level), side_copies(level)
            for h in range(2):
                ups[h].wait_recv()

                @pl.when(has_up)
                def _(h=h):
                    ups[h].start()

                sides[h].start()

        @pl.when(z + d < nz)
        def _():
            level = z + d
            downs, sides = down_copies(level), side_copies(level)
            for h in range(2):
                downs[h].wait_recv()

                @pl.when(has_down)
                def _(h=h):
                    downs[h].start()

                sides[h].start()

    def normalize(level):
        here = rows_at(level * pair, pair)
        unit, _ = norm_parts(x_all[here].astype(jnp.float32))
        n1 = (unit * gain_one[...] + shift_one[...]).astype(jnp.bfloat16)
        n1_all[here] = n1
        return n1

    def attend(level):
        wait_side(level)
        n1 = normalize(level)
        kv[...] = (dot(n1, qkv_w[:, width:]) + qkv_bias[:, width:]).astype(jnp.bfloat16)
        one = mask_of(ends, places_down(seq * rows, rows), places_along(level * pair, pair))
        mask[:rows] = one
        mask[rows:] = one
        keeps = []
        for p in range(HEADS // 2):
            s = dot(two_q[p], kv[:, p * LANES : (p + 1) * LANES], NT)
            scores[p] = s
            low = jnp.abs(s) + mask[...]
            before = top[p]
            most = jnp.max(jnp.maximum(low[:, :LANES], low[:, LANES:]), axis=1, keepdims=True)
            newer = jnp.maximum(before, most)
            keeps.append(jnp.exp(before - newer))
            top[p] = newer
        for p in range(HEADS // 2):
            s = scores[p]
            low = mask[...] - jnp.concatenate([top[p], top[p]], axis=1)
            plus = jnp.exp(low + s)
            minus = jnp.exp(low - s)
            both = plus + minus
            total[p] = total[p] * keeps[p] + (both[:, :LANES] + both[:, LANES:])
            v_pair = kv[:, width + p * LANES : width + (p + 1) * LANES]
            out = own_columns(dot((plus - minus).astype(jnp.bfloat16), v_pair))
            here = slice(p * LANES, (p + 1) * LANES)
            acc[:, here] = acc[:, here] * own_columns(keeps[p]) + out

    def level_step(d, carry):
        @pl.when(d + 1 < nz)
        def _():
            pass_on(d + 1)

        @pl.when(z >= d)
        def _():
            attend(z - d)

        @pl.when((d > 0) & (z + d < nz))
        def _():
            wait_side(z + d)
            normalize(z + d)

        return carry

    lax.fori_loop(0, nz, level_step, 0)

    column = lax.broadcasted_iota(jnp.int32, (1, LANES), 1)
    log_total = jnp.zeros((rows, LANES), jnp.float32)
    for p in range(HEADS // 2):
        here = slice(p * LANES, (p + 1) * LANES)
        row_total = jnp.broadcast_to(jnp.sum(total[p], axis=1, keepdims=True), (pair, LANES))
        acc[:, here] = acc[:, here] / own_columns(row_total)
        lse = top[p] + jnp.log(row_total)
        log_total = jnp.where(column == 2 * p, lse[:rows], log_total)
        log_total = jnp.where(column == 2 * p + 1, lse[rows:], log_total)
    attn = acc[...].astype(jnp.bfloat16)
    attn_out[...] = attn
    loads[1].wait()
    resid = x32 + dot(attn, proj_w[...]) + proj_bias[...]
    unit, inverse = norm_parts(resid)
    n2 = (unit * gain_two[...] + shift_two[...]).astype(jnp.bfloat16)
    n2_out[...] = n2
    res_acc[...] = resid + down_bias[...]
    dh_acc[...] = jnp.zeros(dh_acc.shape, jnp.float32)
    loads[2].wait()
    loads[3].wait()
    slope = math.sqrt(2.0 / math.pi)

    def ff_step(t, carry):
        here = pl.ds(pl.multiple_of(t * FF_TILE, FF_TILE), FF_TILE)
        u = dot(n2_out[...], up_w[:, here]) + up_bias[:, here]
        square = u * u
        bend = jnp.tanh(slope * (u + 0.044715 * (square * u)))
        half = 0.5 * (1.0 + bend)
        g = (u * half).astype(jnp.bfloat16)
        slant = half + (0.5 * u) * (1.0 - bend * bend) * (slope * (1.0 + 3.0 * 0.044715 * square))
        g_out[:, here] = g
        res_acc[...] += dot(g, down_w[here])
        du32 = dot(e_ref[...], down_w[here], NT) * slant
        du = du32.astype(jnp.bfloat16)
        du_out[:, here] = du
        small_out[pl.ds(4 + t, 1)] = jnp.sum(du.astype(jnp.float32), axis=0, keepdims=True)
        dh_acc[...] += dot(du, up_w[:, here], NT)
        return carry

    lax.fori_loop(0, up_w.shape[1] // FF_TILE, ff_step, 0)
    layer_out[...] = res_acc[...].astype(jnp.bfloat16)
    dh = dh_acc[...]
    grad_rows = e_ref[...].astype(jnp.float32)
    dx = grad_rows + norm_back(dh, unit, inverse, gain_two[...])
    dx_out[...] = dx
    da = dx.astype(jnp.bfloat16)
    da_out[...] = da
    do = dot(da, proj_w[...], NT).astype(jnp.bfloat16)
    do_out[...] = do
    product = do.astype(jnp.float32) * acc[...]
    delta = jnp.zeros((rows, LANES), jnp.float32)
    left = first_half()
    for p in range(HEADS // 2):
        here = product[:, p * LANES : (p + 1) * LANES]
        one = jnp.sum(jnp.where(left, here, 0.0), axis=1, keepdims=True)
        two = jnp.sum(jnp.where(left, 0.0, here), axis=1, keepdims=True)
        delta = jnp.where(column == 2 * p, one, delta)
        delta = jnp.where(column == 2 * p + 1, two, delta)
    stats_out[0] = log_total
    stats_out[1] = delta
    small_out[0:1] = jnp.sum(dh * unit, axis=0, keepdims=True)
    small_out[1:2] = jnp.sum(dh, axis=0, keepdims=True)
    small_out[2:3] = jnp.sum(grad_rows, axis=0, keepdims=True)
    small_out[3:4] = jnp.sum(da.astype(jnp.float32), axis=0, keepdims=True)

    def left_all(found):
        for copy in found:
            copy.wait_send()

    left_all(side_copies(z, True))

    @pl.when(has_up)
    def _():
        left_all(up_copies(z, True))

    @pl.when(has_down)
    def _():
        left_all(down_copies(z, True))

    def sent(d, carry):
        @pl.when(z >= d)
        def _():
            left_all(side_copies(z - d))

            @pl.when(has_up)
            def _():
                left_all(up_copies(z - d))

        @pl.when(z + d < nz)
        def _():
            left_all(side_copies(z + d))

            @pl.when(has_down)
            def _():
                left_all(down_copies(z + d))

        return carry

    lax.fori_loop(1, nz, sent, 0)


def run_forward(x, e, lengths, gain_one, shift_one, qkv_weight, qkv_bias, proj_weight, proj_bias, gain_two, shift_two, up_weight, up_bias, down_weight, down_bias, peers):
    rows, width = x.shape
    hidden = up_weight.shape[1]
    nz = peers // 2
    bf, f32 = jnp.bfloat16, jnp.float32
    vmem = pl.BlockSpec(memory_space=pltpu.VMEM)
    smem = pl.BlockSpec(memory_space=pltpu.SMEM)
    hbm = pl.BlockSpec(memory_space=pl.ANY)
    dma = pltpu.SemaphoreType.DMA
    outs = [
        ((rows, width), bf), ((peers * rows, width), bf), ((rows, width), bf), ((rows, width), bf), ((rows, width), bf),
        ((rows, width), bf), ((rows, width), bf), ((rows, hidden), bf), ((rows, hidden), bf), ((rows, width), f32),
        ((2, rows, LANES), f32), ((4 + hidden // width, width), f32),
    ]
    vectors = [gain_one, shift_one, qkv_bias, proj_bias, gain_two, shift_two, up_bias, down_bias]
    return pl.pallas_call(
        functools.partial(forward_kernel, nz),
        out_shape=[(pltpu.VMEM if fits(peers, rows) and k in KEPT else jax.ShapeDtypeStruct)(*o) for k, o in enumerate(outs)],
        in_specs=[vmem, vmem, smem] + [vmem] * 8 + [hbm] * 4,
        out_specs=[vmem] * len(outs),
        scratch_shapes=[
            pltpu.VMEM((peers * rows, width), bf),
            pltpu.VMEM(qkv_weight.shape, bf),
            pltpu.VMEM(proj_weight.shape, bf),
            pltpu.VMEM(up_weight.shape, bf),
            pltpu.VMEM(down_weight.shape, bf),
            pltpu.VMEM((2 * rows, 2 * width), bf),
            pltpu.VMEM((HEADS // 2, 2 * rows, 2 * rows), f32),
            pltpu.VMEM((2 * rows, 2 * rows), f32),
            pltpu.VMEM((HEADS // 2, 2 * rows, LANES), f32),
            pltpu.VMEM((HEADS // 2, 2 * rows, LANES), f32),
            pltpu.VMEM((rows, width), f32),
            pltpu.VMEM((HEADS // 2, 2 * rows, LANES), bf),
            pltpu.VMEM((rows, width), f32),
            pltpu.VMEM((rows, width), f32),
            *[pltpu.VMEM((1, v.shape[0]), f32) for v in vectors],
            *[dma((nz, 2))] * 6, dma((4,)),
        ],
        compiler_params=pltpu.CompilerParams(collective_id=0, has_side_effects=True, vmem_limit_bytes=60 * 2**20),
        cost_estimate=pl.CostEstimate(flops=10**9, bytes_accessed=2 * 10**7, transcendentals=10**6),
    )(x, e, lengths, *vectors, qkv_weight, proj_weight, up_weight, down_weight)


def backward_kernel(
    nz, items, orders, schedule,
    x_ref, e_ref, ends, gain_flat, bias_flat, n1_all, q_ref, attn_ref, da_ref, do_ref, n2_ref, g_ref, du_ref, dx_ref,
    stats_ref, first_small, qkv_hbm,
    input_grad, qkv_out, proj_out, up_out, down_out, small_out,
    qkv_w, buf, inbox, total, do_all, rows_all, g_cat, e_cat, n2_cat, du_cat, attn_cat, da_cat, n1_cat, dqkv_cat,
    two_q, two_do, two_k, two_v, lse_cols, delta_cols, kv, n1_held, mask, dq, dk, dv, small_in, gain_one, qkv_bias,
    e_far, g_far, n2_far, du_far,
    down_send, down_recv, side_send, side_recv, ssem, rsem, lsem,
):
    rows, width = x_ref.shape
    pair = 2 * rows
    place = Place()
    seq, batch = place.seq, place.batch
    z = seq // 2
    x = seq % 2
    core = place.bit(CORE)
    sems = Sems(ssem, rsem)
    local = Sems(lsem, lsem)
    load = pltpu.make_async_copy(qkv_hbm, qkv_w, local.take()[0])
    load.start()
    small_axes = [CORE, ACROSS] + seq_axes(2 * nz)
    has_up = z + 1 < nz
    has_down = z > 0
    above = (seq + 2, batch)
    below = (seq - 2, batch)
    beside = (seq + 1 - 2 * x, batch)
    barrier = pltpu.get_barrier_semaphore()
    for axis in small_axes:
        pl.semaphore_signal(barrier, inc=1, device_id=place.partner(axis), device_id_type=MESH_ID)

    @pl.when(has_up)
    def _():
        pl.semaphore_signal(barrier, inc=1, device_id=above, device_id_type=MESH_ID)

    @pl.when(has_down)
    def _():
        pl.semaphore_signal(barrier, inc=1, device_id=below, device_id_type=MESH_ID)

    gain_one[...] = as_row(gain_flat)
    qkv_bias[...] = as_row(bias_flat)
    for k in range(2):
        rows_all[seq, k * TILE : (k + 1) * TILE] = stats_ref[k].T[:TILE]
    pl.semaphore_wait(barrier, len(small_axes) + has_up.astype(jnp.int32) + has_down.astype(jnp.int32))

    def cols(half, size):
        return pl.ds(pl.multiple_of(half * size, LANES), size)

    def to_core(source, into):
        return pltpu.make_async_remote_copy(
            source, into.at[rows:], *sems.take(), device_id=place.partner(CORE), device_id_type=MESH_ID
        )

    def keep_own(source, into):
        return pltpu.make_async_copy(source, into.at[:rows], local.take()[0])

    def exchange(ref, into, halved):
        size = into.shape[1]
        give = ref.at[:, cols(1 - core, size)] if halved else ref
        keep = ref.at[:, cols(core, size)] if halved else ref
        copies = [to_core(give, into), keep_own(keep, into)]
        for copy in copies:
            copy.start()
        return copies

    def done(copies):
        for copy in copies:
            copy.wait()

    down_parts = exchange(g_ref, g_cat, True) + exchange(e_ref, e_cat, False)
    up_parts = exchange(n2_ref, n2_cat, False) + exchange(du_ref, du_cat, True)

    def do_block(level, side):
        return do_all.at[rows_at((2 * level + side) * rows, rows)]

    def do_copies(level, side, to, send_sem, recv_sem, own=False):
        source = do_ref if own else do_block(level, side)
        stat = rows_all.at[2 * level + side]
        return [
            pltpu.make_async_remote_copy(
                source, do_block(level, side), send_sem.at[level, 0], recv_sem.at[level, 0], device_id=to, device_id_type=MESH_ID
            ),
            pltpu.make_async_remote_copy(
                stat, stat, send_sem.at[level, 1], recv_sem.at[level, 1], device_id=to, device_id_type=MESH_ID
            ),
        ]

    def down_copies(level, own=False):
        return do_copies(level, x, below, down_send, down_recv, own)

    def side_copies(level, own=False):
        return do_copies(level, x, beside, side_send, side_recv, own)

    def begin(copies):
        for copy in copies:
            copy.start()

    @pl.when(has_down)
    def _():
        begin(down_copies(z, True))

    begin(side_copies(z, True))
    do_all[rows_at(seq * rows, rows)] = do_ref[...]

    spread = [1]

    def spread_until(last):
        while spread[0] <= min(last, nz - 1):
            d = spread[0]
            spread[0] += 1

            @pl.when(z + d < nz)
            def _():
                level = z + d
                for copy in down_copies(level):
                    copy.wait_recv()

                @pl.when(has_down)
                def _():
                    begin(down_copies(level))

                begin(side_copies(level))

    def spread_end():
        def sent(copies):
            for copy in copies:
                copy.wait_send()

        sent(side_copies(z, True))

        @pl.when(has_down)
        def _():
            sent(down_copies(z, True))

        def each(level, carry):
            sent(side_copies(level))

            @pl.when(has_down)
            def _():
                sent(down_copies(level))

            return carry

        lax.fori_loop(z + 1, nz, each, 0)

    slots = []
    at = used = 0
    for size, kind, (name, _) in items:
        slots.append((at, size, orders[kind], used))
        at += size
        used += inbox_rows(size, orders[kind], name in FAR)
    places = [(name, r) for _, _, (name, r) in items]

    def destination(name, r, size):
        half = width // 2
        if name == "down":
            return down_out.at[rows_at(core * down_out.shape[0] // 2 + r, size)]
        if name == "up":
            return up_out.at[rows_at(core * up_out.shape[0] // 2 + r, size)]
        if name == "proj":
            return proj_out.at[rows_at(core * half + r, size)]
        return qkv_out.at[rows_at(core * half + r, size), int(name[3:]) * width : (int(name[3:]) + 1) * width]

    ready = set()

    def item_task(k):
        at, size, order, used = slots[k]
        name, r = places[k]
        begun = name[:2] in far
        if begun:
            axis, left, right, left_far, right_far, copy, columns = far[name[:2]]
            if name[:2] not in ready:
                ready.add(name[:2])
                share(copy, right_far)
            part = size // 2
            n = r // size
            columns[n].wait()
            mine = left[:, pl.ds(pl.multiple_of(r + place.bit(axis) * part, LANES), part)]
            both = dot(mine, right[...], TN) + dot(left_far[:, n * part : (n + 1) * part], right_far[...], TN)
            buf[rows_at(at + place.bit(axis) * part, part)] = both.astype(jnp.bfloat16)
        else:
            if name[:2] not in ready:
                ready.add(name[:2])
                done(parts[name[:2]])
            left, right = operands(name)
            buf[at : at + size] = dot(left[:, r : r + size], right, TN).astype(jnp.bfloat16)
        yield from sum_item(place, sems, buf, at, size, order, inbox, used, total, ending, begun)
        there = destination(name, r, size)
        here = total.at[rows_at(at, size)]
        keep = pltpu.make_async_copy(here, there, local.take()[0])
        give = pltpu.make_async_remote_copy(here, there, *sems.take(), device_id=place.partner(CORE), device_id_type=MESH_ID)
        keep.start()
        give.start()
        leaving.extend([keep, give])

    def small_task():
        for k, axis in enumerate(small_axes):
            copy = pltpu.make_async_remote_copy(
                small_out, small_in.at[k], *sems.take(), device_id=place.partner(axis), device_id_type=MESH_ID
            )
            copy.start()
            yield
            copy.wait()
            small_out[...] += small_in[k]

    leaving, ending = [], []

    def operands(name):
        if name == "proj":
            return attn_cat, da_cat[...]
        j = int(name[-1])
        block = slice(j * width, (j + 1) * width)
        return n1_cat, dqkv_cat[:, block]

    x_axis = ("seq", 0)

    def far_start(ref, into, axis):
        copy = pltpu.make_async_remote_copy(
            ref, into.at[:rows], *sems.take(), device_id=place.partner(axis), device_id_type=MESH_ID
        )
        copy.start()
        return copy

    def far_columns(cat, into, axis):
        copies = []
        for n in range(into.shape[1] // LANES):
            columns = pl.ds(pl.multiple_of((2 * n + 1 - place.bit(axis)) * LANES, LANES), LANES)
            copy = pltpu.make_async_remote_copy(
                cat.at[:, columns], into.at[:, n * LANES : (n + 1) * LANES], *sems.take(),
                device_id=place.partner(axis), device_id_type=MESH_ID,
            )
            copy.start()
            copies.append(copy)
        return copies

    def share(copy, into):
        copy.wait()
        other = pltpu.make_async_remote_copy(
            into.at[:rows], into.at[rows:], *sems.take(), device_id=place.partner(CORE), device_id_type=MESH_ID
        )
        other.start()
        other.wait()

    e_copy = far_start(e_ref, e_far, ACROSS)
    n2_copy = far_start(n2_ref, n2_far, x_axis)
    done(down_parts)
    done(up_parts)
    far = {
        "do": (ACROSS, g_cat, e_cat, g_far, e_far, e_copy, far_columns(g_cat, g_far, ACROSS)),
        "up": (x_axis, du_cat, n2_cat, du_far, n2_far, n2_copy, far_columns(du_cat, du_far, x_axis)),
    }
    small_out[:8] = first_small[...]
    own_n1 = rows_at(seq * rows, rows)
    parts = {
        "pr": exchange(attn_ref, attn_cat, True) + exchange(da_ref, da_cat, False),
        "qk": exchange(n1_all.at[own_n1], n1_cat, True),
    }

    load.wait()
    scale = jnp.asarray(1.0 / math.sqrt(HD), jnp.bfloat16)

    chunk_sem = local.take()[0]

    def n1_chunk(level):
        copy = pltpu.make_async_copy(n1_all.at[rows_at(level * pair, pair)], n1_held, chunk_sem)
        copy.start()
        copy.wait()
        return n1_held[...]

    def prepare():
        n1_chunk(z)
        mine = n1_held[rows_at(x * rows, rows)]
        own_kv = (dot(mine, qkv_w[:, width:]) + qkv_bias[:, width:]).astype(jnp.bfloat16)
        for p in range(HEADS // 2):
            here = slice(p * LANES, (p + 1) * LANES)
            two_q[p] = both_heads(q_ref[:, here])
            two_do[p] = both_heads(do_ref[:, here])
            two_k[p] = both_heads(own_kv[:, here])
            two_v[p] = both_heads(own_kv[:, width + p * LANES : width + (p + 1) * LANES])
            for k, into in enumerate((lse_cols, delta_cols)):
                for h in range(2):
                    column = stats_ref[k, :, 2 * p + h : 2 * p + h + 1]
                    into[p, h * rows : (h + 1) * rows] = jnp.broadcast_to(column, (rows, LANES))
        dq[...] = jnp.zeros(dq.shape, jnp.float32)
        dk[...] = jnp.zeros(dk.shape, jnp.float32)
        dv[...] = jnp.zeros(dv.shape, jnp.float32)

    def columns_of(p):
        return pl.ds(pl.multiple_of(p * LANES, LANES), LANES)

    def query_step(level):
        n1 = n1_chunk(level)
        kv[...] = (dot(n1, qkv_w[:, width:]) + qkv_bias[:, width:]).astype(jnp.bfloat16)
        one = mask_of(ends, places_down(seq * rows, rows), places_along(level * pair, pair))
        mask[:rows] = one
        mask[rows:] = one

        def each(p, carry):
            k_pair = kv[:, columns_of(p)]
            v_pair = kv[:, columns_of(p + HEADS // 2)]
            s = dot(two_q[p], k_pair, NT)
            along = dot(two_do[p], v_pair, NT)
            low = mask[...] - lse_cols[p][:, :1]
            plus = jnp.exp(low + s)
            minus = jnp.exp(low - s)
            ds = ((plus + minus) * along - (plus - minus) * delta_cols[p][:, :1]).astype(jnp.bfloat16)
            dq[:, columns_of(p)] += own_columns(dot(ds, k_pair))
            return carry

        lax.fori_loop(0, HEADS // 2, each, 0, unroll=UNROLL)

    def key_step(level):
        side = 1 - x
        for copy in do_copies(level, side, beside, side_send, side_recv):
            copy.wait_recv()
        here = rows_at(level * pair, pair)
        n1 = n1_chunk(level)
        kv[:, :width] = (dot(n1, qkv_w[:, :width]) + qkv_bias[:, :width]).astype(jnp.bfloat16) * scale
        one = mask_of(ends, places_along(level * pair, pair), places_down(seq * rows, rows))
        mask[:rows] = one
        mask[rows:] = one

        def stat(row):
            both = [rows_all[2 * level + k, pl.ds(row, 1)] for k in range(2)]
            return jnp.concatenate(both, axis=1)

        def stat_rows(k, p):
            both = [jnp.broadcast_to(stat(k * TILE + 2 * p + h), (rows, pair)) for h in range(2)]
            return jnp.concatenate(both, axis=0)

        def each(p, carry):
            q_pair = kv[:, columns_of(p)]
            do_pair = do_all[here, columns_of(p)]
            s = dot(two_k[p], q_pair, NT)
            along = dot(two_v[p], do_pair, NT)
            low = mask[...] - stat_rows(0, p)
            plus = jnp.exp(low + s)
            minus = jnp.exp(low - s)
            signed = plus - minus
            ds = ((plus + minus) * along - signed * stat_rows(1, p)).astype(jnp.bfloat16)
            dk[:, columns_of(p)] += own_columns(dot(ds, q_pair))
            dv[:, columns_of(p)] += own_columns(dot(signed.astype(jnp.bfloat16), do_pair))
            return carry

        lax.fori_loop(0, HEADS // 2, each, 0, unroll=UNROLL)

    def one_step(t):
        @pl.when(t <= z)
        def _():
            query_step(z - t)

        @pl.when(t > z)
        def _():
            key_step(t - 1)

    def steps_piece(first, last):
        def piece():
            spread_until(last)
            if last - first == 1:
                one_step(first)
            else:

                def body(t, carry):
                    one_step(t)
                    return carry

                lax.fori_loop(first, last, body, 0)

        return piece

    def finish():
        dqkv = jnp.concatenate(
            [
                (dq[...] * (1.0 / math.sqrt(HD))).astype(jnp.bfloat16),
                dk[...].astype(jnp.bfloat16),
                dv[...].astype(jnp.bfloat16),
            ],
            axis=1,
        )
        dqkv_cat[:rows] = dqkv
        send = to_core(dqkv_cat.at[:rows], dqkv_cat)
        send.start()
        dh = dot(dqkv, qkv_w[...], NT)
        unit, inverse = norm_parts(x_ref[...].astype(jnp.float32))
        input_grad[...] = (dx_ref[...] + norm_back(dh, unit, inverse, gain_one[...])).astype(jnp.bfloat16)
        sums = jnp.sum(dqkv.astype(jnp.float32), axis=0, keepdims=True)
        for k in range(3):
            small_out[8 + k : 9 + k] = sums[:, k * width : (k + 1) * width]
        small_out[11:12] = jnp.sum(dh * unit, axis=0, keepdims=True)
        small_out[12:13] = jnp.sum(dh, axis=0, keepdims=True)
        small_out[13:16] = jnp.zeros((3, width), jnp.float32)
        parts["qk"].append(send)

    groups = min(nz + 1, GROUPS)
    cuts = [(nz + 1) * k // groups for k in range(groups + 1)]
    pieces = [prepare] + [steps_piece(a, b) for a, b in zip(cuts, cuts[1:])] + [finish]
    tasks = [item_task(k) for k in range(len(items))] + [small_task()]
    for token in schedule:
        if token < 0:
            pieces[-1 - token]()
        else:
            next(tasks[token], None)
    for copy in leaving:
        copy.wait()
    for sent in ending:
        sent()
    spread_end()


def in_turns(items, counts, n_pieces):
    early = [k for k, (_, _, (name, _)) in enumerate(items) if name[:3] != "qkv"]
    late = [k for k in range(len(counts)) if k not in early]
    tokens, piece = [], 0
    for waiting in (early, late):
        live = []
        while live or waiting:
            live, waiting = live + waiting[:3], waiting[3:]
            for k in live:
                tokens.append(k)
                if len(tokens) % PACE == 0 and piece < n_pieces:
                    piece += 1
                    tokens.append(-piece)
            live = [k for k in live if tokens.count(k) < counts[k]]
        while piece < n_pieces:
            piece += 1
            tokens.append(-piece)
    return tokens


def fits(peers, rows):
    return peers * rows <= 2048


def plan_items(width, hidden):
    half = width // 2

    def cut(name, size):
        return [(min(ITEM, size - r), (name, r)) for r in range(0, size, ITEM)]

    found = cut("down", hidden // 2)
    found += cut("up", hidden // 2)
    found += cut("proj", half)
    for j in range(3):
        found += cut(f"qkv{j}", half)
    return [(size, int(KINDS[k % len(KINDS)]), where) for k, (size, where) in enumerate(found)]


def run_backward(x, e, lengths, gain_one, qkv_weight, qkv_bias, kept, peers):
    n1_all, q, attn, da, do, n2, g, du, dx, stats, small = kept
    rows, width = x.shape
    hidden = g.shape[1]
    nz = peers // 2
    bf, f32 = jnp.bfloat16, jnp.float32
    orders = axis_orders()
    stages = 2 + len(seq_axes(peers))
    items = plan_items(width, hidden)
    used = sum(inbox_rows(size, orders[kind], name in FAR) for size, kind, (name, _) in items)
    height = sum(size for size, _, _ in items)
    turns = [1 + 2 * (2 + len(hop_groups(nz))) - (name in FAR) for _, _, (name, _) in items] + [1 + stages]
    n_pieces = 2 + min(nz + 1, GROUPS)
    schedule = SCHEDULE
    if sorted(schedule) != sorted([k for k, n in enumerate(turns) for _ in range(n)] + [-1 - k for k in range(n_pieces)]):
        schedule = in_turns(items, turns, n_pieces)
    copies = 9 * len(items) + stages + 8 + 4 + hidden // LANES // 2
    vmem = pl.BlockSpec(memory_space=pltpu.VMEM)
    smem = pl.BlockSpec(memory_space=pltpu.SMEM)
    hbm = pl.BlockSpec(memory_space=pl.ANY)
    dma = pltpu.SemaphoreType.DMA
    out = jax.ShapeDtypeStruct
    small_mesh = fits(peers, rows)
    grad = pltpu.VMEM if small_mesh else out
    stack = (HEADS // 2, 2 * rows, LANES)
    return pl.pallas_call(
        functools.partial(backward_kernel, nz, items, orders, schedule),
        out_shape=[
            grad((rows, width), bf), grad((width, 3 * width), bf), grad((width, width), bf), grad((hidden, width), bf),
            grad((hidden, width), bf), out((16, width), f32),
        ],
        in_specs=[vmem, hbm, smem, vmem, vmem]
        + [vmem if k in (2, 5, 9, 10, 11) or (small_mesh and k in KEPT) else hbm for k in range(1, 12)]
        + [hbm],
        out_specs=[vmem] + [vmem if small_mesh else hbm] * 4 + [vmem],
        scratch_shapes=[
            pltpu.VMEM(qkv_weight.shape, bf),
            pltpu.VMEM((height, width), bf),
            pltpu.VMEM((used, width), bf),
            pltpu.VMEM((height, width), bf),
            pltpu.VMEM((peers * rows, width), bf),
            pltpu.VMEM((peers, 2 * TILE, LANES), f32),
            pltpu.VMEM((2 * rows, hidden // 2), bf),
            pltpu.VMEM((2 * rows, width), bf),
            pltpu.VMEM((2 * rows, width), bf),
            pltpu.VMEM((2 * rows, hidden // 2), bf),
            pltpu.VMEM((2 * rows, width // 2), bf),
            pltpu.VMEM((2 * rows, width), bf),
            pltpu.VMEM((2 * rows, width // 2), bf),
            pltpu.VMEM((2 * rows, 3 * width), bf),
            pltpu.VMEM(stack, bf), pltpu.VMEM(stack, bf), pltpu.VMEM(stack, bf), pltpu.VMEM(stack, bf),
            pltpu.VMEM(stack, f32), pltpu.VMEM(stack, f32),
            pltpu.VMEM((2 * rows, 2 * width), bf),
            pltpu.VMEM((2 * rows, width), bf),
            pltpu.VMEM((2 * rows, 2 * rows), f32),
            pltpu.VMEM((rows, width), f32), pltpu.VMEM((rows, width), f32), pltpu.VMEM((rows, width), f32),
            pltpu.VMEM((stages, 16, width), f32),
            pltpu.VMEM((1, width), f32), pltpu.VMEM((1, 3 * width), f32),
            pltpu.VMEM((2 * rows, width), bf), pltpu.VMEM((2 * rows, hidden // 4), bf),
            pltpu.VMEM((2 * rows, width), bf), pltpu.VMEM((2 * rows, hidden // 4), bf),
            dma((nz, 2)), dma((nz, 2)), dma((nz, 2)), dma((nz, 2)),
            dma((copies,)), dma((copies,)), dma((len(items) + 10,)),
        ],
        compiler_params=pltpu.CompilerParams(collective_id=1, has_side_effects=True, vmem_limit_bytes=(K2_LIMIT if small_mesh else 62) * 2**20),
    )(x, e, lengths, gain_one, qkv_bias, n1_all, q, attn, da, do, n2, g, du, dx, stats, small, qkv_weight)


def widen_kernel(grads, small, passed, outs, rests, passed_outs, slots, sems, pass_sems):
    moved = [pltpu.make_async_copy(a, b, pass_sems.at[k]) for k, (a, b) in enumerate(zip(passed, passed_outs))]
    for copy in moved:
        copy.start()
    for k, (grad, out) in enumerate(zip(grads, outs)):
        slot = slots[k]
        turned = k == TURNED
        rows = slot.shape[2] if turned else slot.shape[1]
        flying = []
        for n in range(grad.shape[0] // rows):
            at = n % slot.shape[0]
            if len(flying) >= slot.shape[0]:
                flying[n - slot.shape[0]].wait()

            def body(i, carry, n=n, at=at, grad=grad, slot=slot, rows=rows):
                here = pl.ds(pl.multiple_of(i * TILE, TILE), TILE)
                there = pl.ds(pl.multiple_of(n * rows + i * TILE, TILE), TILE)
                slot[at, here] = grad[there].astype(jnp.float32)
                return carry

            def turn(i, carry, n=n, at=at, grad=grad, slot=slot, rows=rows):
                here = pl.ds(pl.multiple_of(i * LANES, LANES), LANES)
                there = pl.ds(pl.multiple_of(n * rows + i * LANES, LANES), LANES)
                for c in range(0, grad.shape[1], LANES):
                    slot[at, c : c + LANES, here] = grad[there, c : c + LANES].astype(jnp.float32).T
                return carry

            if turned:
                lax.fori_loop(0, rows // LANES, turn, 0)
            else:
                lax.fori_loop(0, rows // TILE, body, 0)
            into = out.at[:, n * rows : (n + 1) * rows] if turned else out.at[n * rows : (n + 1) * rows]
            copy = pltpu.make_async_copy(slot.at[at], into, sems.at[k, n % slot.shape[0]])
            copy.start()
            flying.append(copy)
        moved += flying[-slot.shape[0] :]
    for (first, count), rest in zip(SMALL_ROWS, rests):
        for k in range(count):
            rest[k * small.shape[1] : (k + 1) * small.shape[1]] = small[first + k : first + k + 1].reshape(small.shape[1])
    for copy in moved:
        copy.wait()


def widen(grads, small, passed):
    width = small.shape[1]
    depth = 3
    sizes = [(g.shape, max(TILE, WIDEN // g.shape[1] // TILE * TILE)) for g in grads]
    vmem = pl.BlockSpec(memory_space=pltpu.VMEM)
    hbm = pl.BlockSpec(memory_space=pl.ANY)
    n = len(grads)
    m = len(SMALL_ROWS)
    q = len(passed)

    def kernel(*refs):
        found = []
        for count in (n, 1, q, n, m, q, n):
            found.append(refs[:count])
            refs = refs[count:]
        found[1] = found[1][0]
        widen_kernel(*found, *refs)

    return pl.pallas_call(
        kernel,
        out_shape=[jax.ShapeDtypeStruct(g.shape[::-1] if k == TURNED else g.shape, jnp.float32) for k, g in enumerate(grads)]
        + [jax.ShapeDtypeStruct((count * width,), jnp.float32) for _, count in SMALL_ROWS]
        + [jax.ShapeDtypeStruct(p.shape, p.dtype) for p in passed],
        in_specs=[vmem] * (n + 1) + [vmem] * q,
        out_specs=[hbm] * n + [vmem] * m + [hbm] * q,
        scratch_shapes=[
            pltpu.VMEM((depth, shape[1], rows) if k == TURNED else (depth, rows, shape[1]), jnp.float32)
            for k, (shape, rows) in enumerate(sizes)
        ]
        + [pltpu.SemaphoreType.DMA((n, depth)), pltpu.SemaphoreType.DMA((q,))],
        compiler_params=pltpu.CompilerParams(vmem_limit_bytes=34 * 2**20),
    )(*grads, small, *passed)


def per_device(
    inputs,
    cotangent,
    doc_lengths,
    gain_one,
    shift_one,
    qkv_weight,
    qkv_bias,
    proj_weight,
    proj_bias,
    gain_two,
    shift_two,
    up_weight,
    up_bias,
    down_weight,
    down_bias,
):
    peers = lax.axis_size("seq")
    width = inputs.shape[2]
    layer_out, *kept = run_forward(
        inputs[0], cotangent[0], doc_lengths, gain_one, shift_one, qkv_weight, qkv_bias, proj_weight, proj_bias, gain_two, shift_two,
        up_weight, up_bias, down_weight, down_bias, peers,
    )
    input_grad, qkv, proj, up, down, small = run_backward(
        inputs[0], cotangent[0], doc_lengths, gain_one, qkv_weight, qkv_bias, kept, peers
    )
    large = (qkv, proj, up, down)
    if fits(peers, inputs.shape[1]):
        qkv, proj, up, down, *rest, layer_out, input_grad = widen(large, small, (layer_out, input_grad))
    else:
        qkv, proj, up, down = (g.astype(jnp.float32) for g in (qkv, proj, up.T, down))
        rest = [small[first : first + count].reshape(-1) for first, count in SMALL_ROWS]
    gain_1, shift_1, qkv_b, proj_b, gain_2, shift_2, up_b, down_b = rest
    return (
        layer_out[None], input_grad[None], gain_1, shift_1, qkv, qkv_b, proj, proj_b, gain_2, shift_2, up, up_b, down, down_b,
    )


def solution(mesh):
    in_specs = (
        P("batch", "seq", None),
        P("batch", "seq", None),
        P("batch", None),
        P(),
        P(),
        P(),
        P(),
        P(),
        P(),
        P(),
        P(),
        P(),
        P(),
        P(),
        P(),
    )
    out_specs = (
        P("batch", "seq", None),
        P("batch", "seq", None),
        P(),
        P(),
        P(),
        P(),
        P(),
        P(),
        P(),
        P(),
        P(),
        P(),
        P(),
        P(),
    )
    return jax.shard_map(
        per_device, mesh=mesh, in_specs=in_specs, out_specs=out_specs, check_vma=False
    )
```

```python
import functools
import math

import jax
import jax.numpy as jnp
from jax import lax
from jax.experimental import pallas as pl
from jax.experimental.pallas import tpu as pltpu
from jax.sharding import PartitionSpec as P

HEADS = 12
HD = 64


norm_eps = 1e-05
masked_low = -1e30


MESH_ID = pl.DeviceIdType.MESH
TILE = 16
LANES = 128
FF_TILE = 768
ITEM = 256
KINDS = "13111140004435354202"
GROUPS = 5
PACE = 8
UNROLL = 2
FAR = ("down", "up")
TURNED = 2
K2_LIMIT = 45
KEPT = (0,)
WIDEN = 128 * 2304
SMALL_ROWS = ((11, 1), (12, 1), (8, 3), (3, 1), (0, 1), (1, 1), (4, 4), (2, 1))
SCHEDULE = (
    -1, 13, -2, 2, 0, 7, 13, 2, 12, 5, 3, -3, 7, 0, 10, 9, 6, 8, 0, 3, 4, 10, -4, 8, 5, 7, 6, 11, 2, 0, 3, 4, 9, 1,
    13, -5, 7, 12, 11, 10, 2, -6, 6, 0, 1, 1, 8, 11, -7, 5, 16, 9, 12, 13, 8, 3, 15, 10, 2, 14, 1, 6, 15, 9, 17, 10,
    20, 17, 13, 18, 19, 7, 15, 11, 19, 1, 13, 12, 4, 16, 20, 14, 9, 7, 1, 11, 15, 8, 19, 5, 7, 10, 9, 20, 1, 8, 0, 18,
    14, 15, 16, 9, 13, 17, 4, 10, 19, 6, 11, 7, 1, 16, 14, 5, 9, 2, 8, 19, 11, 18, 10, 15, 17, 3, 12, 1, 14, 5, 16, 4,
    19, 7, 3, 15, 6, 20, 2, 10, 18, 14, 2, 17, 18, 8, 11, 16, 12, 3, 4, 6, 2, 5, 19, 14, 8, 15, 16, 3, 7, 1, 13, 18,
    0, 19, 11, 17, 4, 3, 5, 5, 9, 20, 0, 12, 14, 13, 4, 17, 10, 12, 6, 8, 14, 0, 9, 18, 16, 13, 15, 17, 12, 4, 18, 6,
    16, 3, 18, 17, 12, 15, 16, 2, 15, 6, 0, 20, 17, 5, 19, 14, 13, 19, 18, 16, 17, 12, 4, 14, 18, 11, 19,
)


class Place:
    def __init__(self):
        self.seq = lax.axis_index("seq")
        self.batch = lax.axis_index("batch")
        self.level = self.seq // 2
        self.levels = lax.axis_size("seq") // 2

    def bit(self, axis):
        name, k = axis
        return ((self.seq if name == "seq" else self.batch) // (1 << k)) % 2

    def partner(self, axis):
        name, k = axis
        step = (1 << k) * (1 - 2 * self.bit(axis))
        if name == "seq":
            return (self.seq + step, self.batch)
        return (self.seq, self.batch + step)


CORE = ("batch", 0)
ACROSS = ("batch", 1)
LEVELS = ("seq", None)


def seq_axes(peers):
    return [("seq", k) for k in range((peers - 1).bit_length())]


def axis_orders():
    x, y, z = ("seq", 0), ACROSS, LEVELS
    return [[x, y, z], [y, z, x], [z, x, y], [y, x, z], [x, z, y], [z, y, x]]


class Sems:
    def __init__(self, send, recv):
        self.send, self.recv, self.count = send, recv, 0

    def take(self):
        k = self.count
        self.count += 1
        return self.send.at[k], self.recv.at[k]


def rows_at(start, size):
    return pl.ds(pl.multiple_of(start, TILE), size)


def add_rows(into, one, at, other, other_at, rows):
    step = 32 if rows % 32 == 0 else TILE

    def body(i, carry):
        here = rows_at(at + i * step, step)
        there = rows_at(other_at + i * step, step)
        both = one[here].astype(jnp.float32) + other[there].astype(jnp.float32)
        into[here] = both.astype(into.dtype)
        return carry

    lax.fori_loop(0, rows // step, body, 0)


def sum_item(place, sems, buf, at, rows, order, inbox, used, total, leaving, begun=False):
    z, nz = place.level, place.levels
    above, below = (place.seq + 2, place.batch), (place.seq - 2, place.batch)
    at_end = (z == 0) | (z == nz - 1)
    low, length, held, plan = at, rows, None, []

    def where(condition, act):
        if condition is None:
            act()
        else:
            pl.when(condition)(act)

    def remote(source, into, to):
        return pltpu.make_async_remote_copy(source, into, *sems.take(), device_id=to, device_id_type=MESH_ID)

    def part_of(ref, start, size):
        return ref.at[rows_at(start, size)]

    def chain(up, down, step_up, step_down):
        pl.when(z == 0)(up.start)
        pl.when(z == nz - 1)(down.start)
        yield
        for first, last in hop_groups(nz):
            for hop, copy, step in ((z, up, step_up), (nz - 1 - z, down, step_down)):
                here = (hop >= first) & (hop < last)

                @pl.when(here)
                def _(copy=copy, step=step):
                    copy.wait_recv()
                    step(False)

                @pl.when(here & (hop < nz - 1))
                def _(copy=copy):
                    copy.start()

                @pl.when(here & (hop == nz - 1))
                def _(step=step):
                    step(True)

            if last < nz:
                yield

        def sent():
            pl.when(z < nz - 1)(up.wait_send)
            pl.when(z > 0)(down.wait_send)

        leaving.append(sent)

    for k, axis in enumerate(order):
        last = k == len(order) - 1
        part = length // 2
        if axis == LEVELS:
            ups, downs = low + part, low

            def adder(start, slot, part=part, last=last):
                def step(end):
                    if not last:
                        if not end:
                            add_rows(buf, buf, start, inbox, slot, part)
                    elif end:
                        add_rows(total, buf, start, inbox, slot, part)

                return step

            def adder_last(start, slot, hop, part=part):
                def step(end):
                    if end:
                        add_rows(total, buf, start, inbox, slot, part)
                    else:
                        pl.when(hop < nz - 1)(lambda: add_rows(buf, buf, start, inbox, slot, part))

                return step

            make_up = adder_last(ups, used, z) if last else adder(ups, used)
            make_down = adder_last(downs, used + part, nz - 1 - z) if last else adder(downs, used + part)
            yield from chain(
                remote(part_of(buf, ups, part), part_of(inbox, used, part), above),
                remote(part_of(buf, downs, part), part_of(inbox, used + part, part), below),
                make_up,
                make_down,
            )
            used += 2 * part
            plan.append((axis, low, part, held))
            low = low + jnp.where(z == nz - 1, part, 0)
            held = at_end
        else:
            bit = place.bit(axis)
            keep, give = low + bit * part, low + (1 - bit) * part
            if begun and k == 0:
                plan.append((axis, keep, part, held))
                low, length = keep, part
                continue
            copy = remote(part_of(buf, give, part), part_of(inbox, used, part), place.partner(axis))
            where(held, copy.start)
            yield

            def take(copy=copy, keep=keep, used=used, part=part, last=last):
                copy.wait()
                add_rows(total if last else buf, buf, keep, inbox, used, part)

            where(held, take)
            used += part
            plan.append((axis, keep, part, held))
            low = keep
        length = part
    for axis, low, part, held in reversed(plan):
        if axis == LEVELS:
            ups, downs = part_of(total, low + part, part), part_of(total, low, part)
            nothing = lambda end: None
            yield from chain(remote(downs, downs, above), remote(ups, ups, below), nothing, nothing)
        else:
            here = part_of(total, low, part)
            copy = remote(here, here, place.partner(axis))
            where(held, copy.start)
            yield
            where(held, copy.wait)


def hop_groups(levels):
    groups = min(levels - 1, 3)
    cuts = [1 + (levels - 1) * k // groups for k in range(groups + 1)]
    return list(zip(cuts, cuts[1:]))


def inbox_rows(rows, order, begun):
    used = 0
    for k, axis in enumerate(order):
        rows //= 2
        if begun and k == 0:
            continue
        used += 2 * rows if axis == LEVELS else rows
    return used


def dot(a, b, dims=((1,), (0,))):
    return lax.dot_general(a, b, (dims, ((), ())), preferred_element_type=jnp.float32)


NT = ((1,), (1,))
TN = ((0,), (0,))


def norm_parts(rows):
    center = rows - jnp.mean(rows, axis=-1, keepdims=True)
    spread = jnp.mean(center * center, axis=-1, keepdims=True)
    inverse = lax.rsqrt(spread + norm_eps)
    return center * inverse, inverse


def norm_back(grad, unit, inverse, gain):
    scaled = grad * gain
    along = jnp.mean(scaled * unit, axis=-1, keepdims=True)
    return inverse * (scaled - jnp.mean(scaled, axis=-1, keepdims=True) - unit * along)


def doc_ids(lengths, places):
    found = jnp.zeros(places.shape, jnp.int32)
    end = 0
    for k in range(lengths.shape[1]):
        end += lengths[0, k]
        found += (end <= places).astype(jnp.int32)
    return found


def as_row(ref):
    return ref[...].reshape(1, -1)


def places_down(first, rows):
    return first + lax.broadcasted_iota(jnp.int32, (rows, 1), 0)


def places_along(first, rows):
    return first + lax.broadcasted_iota(jnp.int32, (1, rows), 1)


def mask_of(ends, q_places, k_places):
    allowed = (doc_ids(ends, q_places) == doc_ids(ends, k_places)) & (k_places <= q_places)
    return jnp.where(allowed, 0.0, masked_low)


def first_half():
    return lax.broadcasted_iota(jnp.int32, (1, LANES), 1) < HD


def both_heads(pair):
    left = first_half()
    none = jnp.zeros_like(pair)
    return jnp.concatenate([jnp.where(left, pair, none), jnp.where(left, none, pair)], axis=0)


def own_columns(stacked):
    rows = stacked.shape[0] // 2
    return jnp.where(first_half(), stacked[:rows], stacked[rows:])


def lanes(p):
    return pl.ds(p * LANES, LANES)


def forward_kernel(
    nz, x_ref, e_ref, ends, gain_one1, shift_one1, qkv_bias1, proj_bias1, gain_two1, shift_two1, up_bias1, down_bias1,
    qkv_hbm, proj_hbm, up_hbm, down_hbm,
    layer_out, n1_all, q_out, attn_out, da_out, do_out, n2_out, g_out, du_out, dx_out, stats_out, small_out,
    x_all, qkv_w, proj_w, up_w, down_w, kv, scores, mask, top, total, acc, two_q, res_acc, dh_acc,
    gain_one, shift_one, qkv_bias, proj_bias, gain_two, shift_two, up_bias, down_bias,
    up_send, up_recv, down_send, down_recv, side_send, side_recv, w_sem,
):
    rows, width = x_ref.shape
    pair = 2 * rows
    seq = lax.axis_index("seq")
    batch = lax.axis_index("batch")
    z = seq // 2
    x = seq % 2
    loads = [
        pltpu.make_async_copy(hbm, vmem, w_sem.at[k])
        for k, (hbm, vmem) in enumerate(
            [(qkv_hbm, qkv_w), (proj_hbm, proj_w), (up_hbm, up_w), (down_hbm, down_w)]
        )
    ]
    loads[0].start()
    barrier = pltpu.get_barrier_semaphore()
    has_up = z + 1 < nz
    has_down = z > 0
    above = (seq + 2, batch)
    below = (seq - 2, batch)
    beside = (seq + 1 - 2 * x, batch)

    @pl.when(has_up)
    def _():
        pl.semaphore_signal(barrier, inc=1, device_id=above, device_id_type=MESH_ID)

    @pl.when(has_down)
    def _():
        pl.semaphore_signal(barrier, inc=1, device_id=below, device_id_type=MESH_ID)

    pl.semaphore_signal(barrier, inc=1, device_id=beside, device_id_type=MESH_ID)
    pl.semaphore_wait(barrier, 1 + has_up.astype(jnp.int32) + has_down.astype(jnp.int32))
    for load in loads[1:]:
        load.start()

    half = rows // 2

    def block(level, side, h):
        return x_all.at[rows_at((2 * level + side) * rows + h * half, half)]

    def copies(level, side, to, send_sem, recv_sem, own=False):
        found = []
        for h in range(2):
            source = x_ref.at[h * half : (h + 1) * half] if own else block(level, side, h)
            found.append(
                pltpu.make_async_remote_copy(
                    source, block(level, side, h), send_sem.at[level, h], recv_sem.at[level, h],
                    device_id=to, device_id_type=MESH_ID,
                )
            )
        return found

    def up_copies(level, own=False):
        return copies(level, x, above, up_send, up_recv, own)

    def down_copies(level, own=False):
        return copies(level, x, below, down_send, down_recv, own)

    def side_copies(level, own=False):
        return copies(level, x, beside, side_send, side_recv, own)

    def wait_side(level):
        for copy in copies(level, 1 - x, beside, side_send, side_recv):
            copy.wait_recv()

    own_up, own_side, own_down = up_copies(z, True), side_copies(z, True), down_copies(z, True)
    for h in range(2):

        @pl.when(has_up)
        def _(h=h):
            own_up[h].start()

        own_side[h].start()

        @pl.when(has_down)
        def _(h=h):
            own_down[h].start()

    vectors = [gain_one, shift_one, qkv_bias, proj_bias, gain_two, shift_two, up_bias, down_bias]
    flats = [gain_one1, shift_one1, qkv_bias1, proj_bias1, gain_two1, shift_two1, up_bias1, down_bias1]
    for vector, flat in zip(vectors, flats):
        vector[...] = as_row(flat)
    x_all[rows_at(seq * rows, rows)] = x_ref[...]
    x32 = x_ref[...].astype(jnp.float32)
    unit_one, _ = norm_parts(x32)
    mine = (unit_one * gain_one[...] + shift_one[...]).astype(jnp.bfloat16)
    top[...] = jnp.full(top.shape, masked_low, jnp.float32)
    total[...] = jnp.zeros(total.shape, jnp.float32)
    acc[...] = jnp.zeros(acc.shape, jnp.float32)
    loads[0].wait()
    q = (dot(mine, qkv_w[:, :width]) + qkv_bias[:, :width]).astype(jnp.bfloat16)
    q = q * jnp.asarray(1.0 / math.sqrt(HD), jnp.bfloat16)
    q_out[...] = q
    for p in range(HEADS // 2):
        two_q[p] = both_heads(q[:, p * LANES : (p + 1) * LANES])

    def pass_on(d):
        @pl.when(z >= d)
        def _():
            level = z - d
            ups, sides = up_copies(level), side_copies(level)
            for h in range(2):
                ups[h].wait_recv()

                @pl.when(has_up)
                def _(h=h):
                    ups[h].start()

                sides[h].start()

        @pl.when(z + d < nz)
        def _():
            level = z + d
            downs, sides = down_copies(level), side_copies(level)
            for h in range(2):
                downs[h].wait_recv()

                @pl.when(has_down)
                def _(h=h):
                    downs[h].start()

                sides[h].start()

    def normalize(level):
        here = rows_at(level * pair, pair)
        unit, _ = norm_parts(x_all[here].astype(jnp.float32))
        n1 = (unit * gain_one[...] + shift_one[...]).astype(jnp.bfloat16)
        n1_all[here] = n1
        return n1

    def attend(level):
        wait_side(level)
        n1 = normalize(level)
        kv[...] = (dot(n1, qkv_w[:, width:]) + qkv_bias[:, width:]).astype(jnp.bfloat16)
        one = mask_of(ends, places_down(seq * rows, rows), places_along(level * pair, pair))
        mask[:rows] = one
        mask[rows:] = one
        keeps = []
        for p in range(HEADS // 2):
            s = dot(two_q[p], kv[:, p * LANES : (p + 1) * LANES], NT)
            scores[p] = s
            low = jnp.abs(s) + mask[...]
            before = top[p]
            most = jnp.max(jnp.maximum(low[:, :LANES], low[:, LANES:]), axis=1, keepdims=True)
            newer = jnp.maximum(before, most)
            keeps.append(jnp.exp(before - newer))
            top[p] = newer
        for p in range(HEADS // 2):
            s = scores[p]
            low = mask[...] - jnp.concatenate([top[p], top[p]], axis=1)
            plus = jnp.exp(low + s)
            minus = jnp.exp(low - s)
            both = plus + minus
            total[p] = total[p] * keeps[p] + (both[:, :LANES] + both[:, LANES:])
            v_pair = kv[:, width + p * LANES : width + (p + 1) * LANES]
            out = own_columns(dot((plus - minus).astype(jnp.bfloat16), v_pair))
            here = slice(p * LANES, (p + 1) * LANES)
            acc[:, here] = acc[:, here] * own_columns(keeps[p]) + out

    def level_step(d, carry):
        @pl.when(d + 1 < nz)
        def _():
            pass_on(d + 1)

        @pl.when(z >= d)
        def _():
            attend(z - d)

        @pl.when((d > 0) & (z + d < nz))
        def _():
            wait_side(z + d)
            normalize(z + d)

        return carry

    lax.fori_loop(0, nz, level_step, 0)

    column = lax.broadcasted_iota(jnp.int32, (1, LANES), 1)
    log_total = jnp.zeros((rows, LANES), jnp.float32)
    for p in range(HEADS // 2):
        here = slice(p * LANES, (p + 1) * LANES)
        row_total = jnp.broadcast_to(jnp.sum(total[p], axis=1, keepdims=True), (pair, LANES))
        acc[:, here] = acc[:, here] / own_columns(row_total)
        lse = top[p] + jnp.log(row_total)
        log_total = jnp.where(column == 2 * p, lse[:rows], log_total)
        log_total = jnp.where(column == 2 * p + 1, lse[rows:], log_total)
    attn = acc[...].astype(jnp.bfloat16)
    attn_out[...] = attn
    loads[1].wait()
    resid = x32 + dot(attn, proj_w[...]) + proj_bias[...]
    unit, inverse = norm_parts(resid)
    n2 = (unit * gain_two[...] + shift_two[...]).astype(jnp.bfloat16)
    n2_out[...] = n2
    res_acc[...] = resid + down_bias[...]
    dh_acc[...] = jnp.zeros(dh_acc.shape, jnp.float32)
    loads[2].wait()
    loads[3].wait()
    slope = math.sqrt(2.0 / math.pi)

    def ff_step(t, carry):
        here = pl.ds(pl.multiple_of(t * FF_TILE, FF_TILE), FF_TILE)
        u = dot(n2_out[...], up_w[:, here]) + up_bias[:, here]
        square = u * u
        bend = jnp.tanh(slope * (u + 0.044715 * (square * u)))
        half = 0.5 * (1.0 + bend)
        g = (u * half).astype(jnp.bfloat16)
        slant = half + (0.5 * u) * (1.0 - bend * bend) * (slope * (1.0 + 3.0 * 0.044715 * square))
        g_out[:, here] = g
        res_acc[...] += dot(g, down_w[here])
        du32 = dot(e_ref[...], down_w[here], NT) * slant
        du = du32.astype(jnp.bfloat16)
        du_out[:, here] = du
        small_out[pl.ds(4 + t, 1)] = jnp.sum(du.astype(jnp.float32), axis=0, keepdims=True)
        dh_acc[...] += dot(du, up_w[:, here], NT)
        return carry

    lax.fori_loop(0, up_w.shape[1] // FF_TILE, ff_step, 0)
    layer_out[...] = res_acc[...].astype(jnp.bfloat16)
    dh = dh_acc[...]
    grad_rows = e_ref[...].astype(jnp.float32)
    dx = grad_rows + norm_back(dh, unit, inverse, gain_two[...])
    dx_out[...] = dx
    da = dx.astype(jnp.bfloat16)
    da_out[...] = da
    do = dot(da, proj_w[...], NT).astype(jnp.bfloat16)
    do_out[...] = do
    product = do.astype(jnp.float32) * acc[...]
    delta = jnp.zeros((rows, LANES), jnp.float32)
    left = first_half()
    for p in range(HEADS // 2):
        here = product[:, p * LANES : (p + 1) * LANES]
        one = jnp.sum(jnp.where(left, here, 0.0), axis=1, keepdims=True)
        two = jnp.sum(jnp.where(left, 0.0, here), axis=1, keepdims=True)
        delta = jnp.where(column == 2 * p, one, delta)
        delta = jnp.where(column == 2 * p + 1, two, delta)
    stats_out[0] = log_total
    stats_out[1] = delta
    small_out[0:1] = jnp.sum(dh * unit, axis=0, keepdims=True)
    small_out[1:2] = jnp.sum(dh, axis=0, keepdims=True)
    small_out[2:3] = jnp.sum(grad_rows, axis=0, keepdims=True)
    small_out[3:4] = jnp.sum(da.astype(jnp.float32), axis=0, keepdims=True)

    def left_all(found):
        for copy in found:
            copy.wait_send()

    left_all(side_copies(z, True))

    @pl.when(has_up)
    def _():
        left_all(up_copies(z, True))

    @pl.when(has_down)
    def _():
        left_all(down_copies(z, True))

    def sent(d, carry):
        @pl.when(z >= d)
        def _():
            left_all(side_copies(z - d))

            @pl.when(has_up)
            def _():
                left_all(up_copies(z - d))

        @pl.when(z + d < nz)
        def _():
            left_all(side_copies(z + d))

            @pl.when(has_down)
            def _():
                left_all(down_copies(z + d))

        return carry

    lax.fori_loop(1, nz, sent, 0)


def run_forward(x, e, lengths, gain_one, shift_one, qkv_weight, qkv_bias, proj_weight, proj_bias, gain_two, shift_two, up_weight, up_bias, down_weight, down_bias, peers):
    rows, width = x.shape
    hidden = up_weight.shape[1]
    nz = peers // 2
    bf, f32 = jnp.bfloat16, jnp.float32
    vmem = pl.BlockSpec(memory_space=pltpu.VMEM)
    smem = pl.BlockSpec(memory_space=pltpu.SMEM)
    hbm = pl.BlockSpec(memory_space=pl.ANY)
    dma = pltpu.SemaphoreType.DMA
    outs = [
        ((rows, width), bf), ((peers * rows, width), bf), ((rows, width), bf), ((rows, width), bf), ((rows, width), bf),
        ((rows, width), bf), ((rows, width), bf), ((rows, hidden), bf), ((rows, hidden), bf), ((rows, width), f32),
        ((2, rows, LANES), f32), ((4 + hidden // width, width), f32),
    ]
    vectors = [gain_one, shift_one, qkv_bias, proj_bias, gain_two, shift_two, up_bias, down_bias]
    return pl.pallas_call(
        functools.partial(forward_kernel, nz),
        out_shape=[(pltpu.VMEM if fits(peers, rows) and k in KEPT else jax.ShapeDtypeStruct)(*o) for k, o in enumerate(outs)],
        in_specs=[vmem, vmem, smem] + [vmem] * 8 + [hbm] * 4,
        out_specs=[vmem] * len(outs),
        scratch_shapes=[
            pltpu.VMEM((peers * rows, width), bf),
            pltpu.VMEM(qkv_weight.shape, bf),
            pltpu.VMEM(proj_weight.shape, bf),
            pltpu.VMEM(up_weight.shape, bf),
            pltpu.VMEM(down_weight.shape, bf),
            pltpu.VMEM((2 * rows, 2 * width), bf),
            pltpu.VMEM((HEADS // 2, 2 * rows, 2 * rows), f32),
            pltpu.VMEM((2 * rows, 2 * rows), f32),
            pltpu.VMEM((HEADS // 2, 2 * rows, LANES), f32),
            pltpu.VMEM((HEADS // 2, 2 * rows, LANES), f32),
            pltpu.VMEM((rows, width), f32),
            pltpu.VMEM((HEADS // 2, 2 * rows, LANES), bf),
            pltpu.VMEM((rows, width), f32),
            pltpu.VMEM((rows, width), f32),
            *[pltpu.VMEM((1, v.shape[0]), f32) for v in vectors],
            *[dma((nz, 2))] * 6, dma((4,)),
        ],
        compiler_params=pltpu.CompilerParams(collective_id=0, has_side_effects=True, vmem_limit_bytes=60 * 2**20),
        cost_estimate=pl.CostEstimate(flops=10**9, bytes_accessed=2 * 10**7, transcendentals=10**6),
    )(x, e, lengths, *vectors, qkv_weight, proj_weight, up_weight, down_weight)


def backward_kernel(
    nz, items, orders, schedule,
    x_ref, e_ref, ends, gain_flat, bias_flat, n1_all, q_ref, attn_ref, da_ref, do_ref, n2_ref, g_ref, du_ref, dx_ref,
    stats_ref, first_small, qkv_hbm,
    input_grad, qkv_out, proj_out, up_out, down_out, small_out,
    qkv_w, buf, inbox, total, do_all, rows_all, g_cat, e_cat, n2_cat, du_cat, attn_cat, da_cat, n1_cat, dqkv_cat,
    two_q, two_do, two_k, two_v, lse_cols, delta_cols, kv, n1_held, mask, dq, dk, dv, small_in, gain_one, qkv_bias,
    e_far, g_far, n2_far, du_far,
    down_send, down_recv, side_send, side_recv, ssem, rsem, lsem,
):
    rows, width = x_ref.shape
    pair = 2 * rows
    place = Place()
    seq, batch = place.seq, place.batch
    z = seq // 2
    x = seq % 2
    core = place.bit(CORE)
    sems = Sems(ssem, rsem)
    local = Sems(lsem, lsem)
    load = pltpu.make_async_copy(qkv_hbm, qkv_w, local.take()[0])
    load.start()
    small_axes = [CORE, ACROSS] + seq_axes(2 * nz)
    has_up = z + 1 < nz
    has_down = z > 0
    above = (seq + 2, batch)
    below = (seq - 2, batch)
    beside = (seq + 1 - 2 * x, batch)
    barrier = pltpu.get_barrier_semaphore()
    for axis in small_axes:
        pl.semaphore_signal(barrier, inc=1, device_id=place.partner(axis), device_id_type=MESH_ID)

    @pl.when(has_up)
    def _():
        pl.semaphore_signal(barrier, inc=1, device_id=above, device_id_type=MESH_ID)

    @pl.when(has_down)
    def _():
        pl.semaphore_signal(barrier, inc=1, device_id=below, device_id_type=MESH_ID)

    gain_one[...] = as_row(gain_flat)
    qkv_bias[...] = as_row(bias_flat)
    for k in range(2):
        rows_all[seq, k * TILE : (k + 1) * TILE] = stats_ref[k].T[:TILE]
    pl.semaphore_wait(barrier, len(small_axes) + has_up.astype(jnp.int32) + has_down.astype(jnp.int32))

    def cols(half, size):
        return pl.ds(pl.multiple_of(half * size, LANES), size)

    def to_core(source, into):
        return pltpu.make_async_remote_copy(
            source, into.at[rows:], *sems.take(), device_id=place.partner(CORE), device_id_type=MESH_ID
        )

    def keep_own(source, into):
        return pltpu.make_async_copy(source, into.at[:rows], local.take()[0])

    def exchange(ref, into, halved):
        size = into.shape[1]
        give = ref.at[:, cols(1 - core, size)] if halved else ref
        keep = ref.at[:, cols(core, size)] if halved else ref
        copies = [to_core(give, into), keep_own(keep, into)]
        for copy in copies:
            copy.start()
        return copies

    def done(copies):
        for copy in copies:
            copy.wait()

    down_parts = exchange(g_ref, g_cat, True) + exchange(e_ref, e_cat, False)
    up_parts = exchange(n2_ref, n2_cat, False) + exchange(du_ref, du_cat, True)

    def do_block(level, side):
        return do_all.at[rows_at((2 * level + side) * rows, rows)]

    def do_copies(level, side, to, send_sem, recv_sem, own=False):
        source = do_ref if own else do_block(level, side)
        stat = rows_all.at[2 * level + side]
        return [
            pltpu.make_async_remote_copy(
                source, do_block(level, side), send_sem.at[level, 0], recv_sem.at[level, 0], device_id=to, device_id_type=MESH_ID
            ),
            pltpu.make_async_remote_copy(
                stat, stat, send_sem.at[level, 1], recv_sem.at[level, 1], device_id=to, device_id_type=MESH_ID
            ),
        ]

    def down_copies(level, own=False):
        return do_copies(level, x, below, down_send, down_recv, own)

    def side_copies(level, own=False):
        return do_copies(level, x, beside, side_send, side_recv, own)

    def begin(copies):
        for copy in copies:
            copy.start()

    @pl.when(has_down)
    def _():
        begin(down_copies(z, True))

    begin(side_copies(z, True))
    do_all[rows_at(seq * rows, rows)] = do_ref[...]

    spread = [1]

    def spread_until(last):
        while spread[0] <= min(last, nz - 1):
            d = spread[0]
            spread[0] += 1

            @pl.when(z + d < nz)
            def _():
                level = z + d
                for copy in down_copies(level):
                    copy.wait_recv()

                @pl.when(has_down)
                def _():
                    begin(down_copies(level))

                begin(side_copies(level))

    def spread_end():
        def sent(copies):
            for copy in copies:
                copy.wait_send()

        sent(side_copies(z, True))

        @pl.when(has_down)
        def _():
            sent(down_copies(z, True))

        def each(level, carry):
            sent(side_copies(level))

            @pl.when(has_down)
            def _():
                sent(down_copies(level))

            return carry

        lax.fori_loop(z + 1, nz, each, 0)

    slots = []
    at = used = 0
    for size, kind, (name, _) in items:
        slots.append((at, size, orders[kind], used))
        at += size
        used += inbox_rows(size, orders[kind], name in FAR)
    places = [(name, r) for _, _, (name, r) in items]

    def destination(name, r, size):
        half = width // 2
        if name == "down":
            return down_out.at[rows_at(core * down_out.shape[0] // 2 + r, size)]
        if name == "up":
            return up_out.at[rows_at(core * up_out.shape[0] // 2 + r, size)]
        if name == "proj":
            return proj_out.at[rows_at(core * half + r, size)]
        return qkv_out.at[rows_at(core * half + r, size), int(name[3:]) * width : (int(name[3:]) + 1) * width]

    ready = set()

    def item_task(k):
        at, size, order, used = slots[k]
        name, r = places[k]
        begun = name[:2] in far
        if begun:
            axis, left, right, left_far, right_far, copy, columns = far[name[:2]]
            if name[:2] not in ready:
                ready.add(name[:2])
                share(copy, right_far)
            part = size // 2
            n = r // size
            columns[n].wait()
            mine = left[:, pl.ds(pl.multiple_of(r + place.bit(axis) * part, LANES), part)]
            both = dot(mine, right[...], TN) + dot(left_far[:, n * part : (n + 1) * part], right_far[...], TN)
            buf[rows_at(at + place.bit(axis) * part, part)] = both.astype(jnp.bfloat16)
        else:
            if name[:2] not in ready:
                ready.add(name[:2])
                done(parts[name[:2]])
            left, right = operands(name)
            buf[at : at + size] = dot(left[:, r : r + size], right, TN).astype(jnp.bfloat16)
        yield from sum_item(place, sems, buf, at, size, order, inbox, used, total, ending, begun)
        there = destination(name, r, size)
        here = total.at[rows_at(at, size)]
        keep = pltpu.make_async_copy(here, there, local.take()[0])
        give = pltpu.make_async_remote_copy(here, there, *sems.take(), device_id=place.partner(CORE), device_id_type=MESH_ID)
        keep.start()
        give.start()
        leaving.extend([keep, give])

    def small_task():
        for k, axis in enumerate(small_axes):
            copy = pltpu.make_async_remote_copy(
                small_out, small_in.at[k], *sems.take(), device_id=place.partner(axis), device_id_type=MESH_ID
            )
            copy.start()
            yield
            copy.wait()
            small_out[...] += small_in[k]

    leaving, ending = [], []

    def operands(name):
        if name == "proj":
            return attn_cat, da_cat[...]
        j = int(name[-1])
        block = slice(j * width, (j + 1) * width)
        return n1_cat, dqkv_cat[:, block]

    x_axis = ("seq", 0)

    def far_start(ref, into, axis):
        copy = pltpu.make_async_remote_copy(
            ref, into.at[:rows], *sems.take(), device_id=place.partner(axis), device_id_type=MESH_ID
        )
        copy.start()
        return copy

    def far_columns(cat, into, axis):
        copies = []
        for n in range(into.shape[1] // LANES):
            columns = pl.ds(pl.multiple_of((2 * n + 1 - place.bit(axis)) * LANES, LANES), LANES)
            copy = pltpu.make_async_remote_copy(
                cat.at[:, columns], into.at[:, n * LANES : (n + 1) * LANES], *sems.take(),
                device_id=place.partner(axis), device_id_type=MESH_ID,
            )
            copy.start()
            copies.append(copy)
        return copies

    def share(copy, into):
        copy.wait()
        other = pltpu.make_async_remote_copy(
            into.at[:rows], into.at[rows:], *sems.take(), device_id=place.partner(CORE), device_id_type=MESH_ID
        )
        other.start()
        other.wait()

    e_copy = far_start(e_ref, e_far, ACROSS)
    n2_copy = far_start(n2_ref, n2_far, x_axis)
    done(down_parts)
    done(up_parts)
    far = {
        "do": (ACROSS, g_cat, e_cat, g_far, e_far, e_copy, far_columns(g_cat, g_far, ACROSS)),
        "up": (x_axis, du_cat, n2_cat, du_far, n2_far, n2_copy, far_columns(du_cat, du_far, x_axis)),
    }
    small_out[:8] = first_small[...]
    own_n1 = rows_at(seq * rows, rows)
    parts = {
        "pr": exchange(attn_ref, attn_cat, True) + exchange(da_ref, da_cat, False),
        "qk": exchange(n1_all.at[own_n1], n1_cat, True),
    }

    load.wait()
    scale = jnp.asarray(1.0 / math.sqrt(HD), jnp.bfloat16)

    chunk_sem = local.take()[0]

    def n1_chunk(level):
        copy = pltpu.make_async_copy(n1_all.at[rows_at(level * pair, pair)], n1_held, chunk_sem)
        copy.start()
        copy.wait()
        return n1_held[...]

    def prepare():
        n1_chunk(z)
        mine = n1_held[rows_at(x * rows, rows)]
        own_kv = (dot(mine, qkv_w[:, width:]) + qkv_bias[:, width:]).astype(jnp.bfloat16)
        for p in range(HEADS // 2):
            here = slice(p * LANES, (p + 1) * LANES)
            two_q[p] = both_heads(q_ref[:, here])
            two_do[p] = both_heads(do_ref[:, here])
            two_k[p] = both_heads(own_kv[:, here])
            two_v[p] = both_heads(own_kv[:, width + p * LANES : width + (p + 1) * LANES])
            for k, into in enumerate((lse_cols, delta_cols)):
                for h in range(2):
                    column = stats_ref[k, :, 2 * p + h : 2 * p + h + 1]
                    into[p, h * rows : (h + 1) * rows] = jnp.broadcast_to(column, (rows, LANES))
        dq[...] = jnp.zeros(dq.shape, jnp.float32)
        dk[...] = jnp.zeros(dk.shape, jnp.float32)
        dv[...] = jnp.zeros(dv.shape, jnp.float32)

    def columns_of(p):
        return pl.ds(pl.multiple_of(p * LANES, LANES), LANES)

    def query_step(level):
        n1 = n1_chunk(level)
        kv[...] = (dot(n1, qkv_w[:, width:]) + qkv_bias[:, width:]).astype(jnp.bfloat16)
        one = mask_of(ends, places_down(seq * rows, rows), places_along(level * pair, pair))
        mask[:rows] = one
        mask[rows:] = one

        def each(p, carry):
            k_pair = kv[:, columns_of(p)]
            v_pair = kv[:, columns_of(p + HEADS // 2)]
            s = dot(two_q[p], k_pair, NT)
            along = dot(two_do[p], v_pair, NT)
            low = mask[...] - lse_cols[p][:, :1]
            plus = jnp.exp(low + s)
            minus = jnp.exp(low - s)
            ds = ((plus + minus) * along - (plus - minus) * delta_cols[p][:, :1]).astype(jnp.bfloat16)
            dq[:, columns_of(p)] += own_columns(dot(ds, k_pair))
            return carry

        lax.fori_loop(0, HEADS // 2, each, 0, unroll=UNROLL)

    def key_step(level):
        side = 1 - x
        for copy in do_copies(level, side, beside, side_send, side_recv):
            copy.wait_recv()
        here = rows_at(level * pair, pair)
        n1 = n1_chunk(level)
        kv[:, :width] = (dot(n1, qkv_w[:, :width]) + qkv_bias[:, :width]).astype(jnp.bfloat16) * scale
        one = mask_of(ends, places_along(level * pair, pair), places_down(seq * rows, rows))
        mask[:rows] = one
        mask[rows:] = one

        def stat(row):
            both = [rows_all[2 * level + k, pl.ds(row, 1)] for k in range(2)]
            return jnp.concatenate(both, axis=1)

        def stat_rows(k, p):
            both = [jnp.broadcast_to(stat(k * TILE + 2 * p + h), (rows, pair)) for h in range(2)]
            return jnp.concatenate(both, axis=0)

        def each(p, carry):
            q_pair = kv[:, columns_of(p)]
            do_pair = do_all[here, columns_of(p)]
            s = dot(two_k[p], q_pair, NT)
            along = dot(two_v[p], do_pair, NT)
            low = mask[...] - stat_rows(0, p)
            plus = jnp.exp(low + s)
            minus = jnp.exp(low - s)
            signed = plus - minus
            ds = ((plus + minus) * along - signed * stat_rows(1, p)).astype(jnp.bfloat16)
            dk[:, columns_of(p)] += own_columns(dot(ds, q_pair))
            dv[:, columns_of(p)] += own_columns(dot(signed.astype(jnp.bfloat16), do_pair))
            return carry

        lax.fori_loop(0, HEADS // 2, each, 0, unroll=UNROLL)

    def one_step(t):
        @pl.when(t <= z)
        def _():
            query_step(z - t)

        @pl.when(t > z)
        def _():
            key_step(t - 1)

    def steps_piece(first, last):
        def piece():
            spread_until(last)
            if last - first == 1:
                one_step(first)
            else:

                def body(t, carry):
                    one_step(t)
                    return carry

                lax.fori_loop(first, last, body, 0)

        return piece

    def finish():
        dqkv = jnp.concatenate(
            [
                (dq[...] * (1.0 / math.sqrt(HD))).astype(jnp.bfloat16),
                dk[...].astype(jnp.bfloat16),
                dv[...].astype(jnp.bfloat16),
            ],
            axis=1,
        )
        dqkv_cat[:rows] = dqkv
        send = to_core(dqkv_cat.at[:rows], dqkv_cat)
        send.start()
        dh = dot(dqkv, qkv_w[...], NT)
        unit, inverse = norm_parts(x_ref[...].astype(jnp.float32))
        input_grad[...] = (dx_ref[...] + norm_back(dh, unit, inverse, gain_one[...])).astype(jnp.bfloat16)
        sums = jnp.sum(dqkv.astype(jnp.float32), axis=0, keepdims=True)
        for k in range(3):
            small_out[8 + k : 9 + k] = sums[:, k * width : (k + 1) * width]
        small_out[11:12] = jnp.sum(dh * unit, axis=0, keepdims=True)
        small_out[12:13] = jnp.sum(dh, axis=0, keepdims=True)
        small_out[13:16] = jnp.zeros((3, width), jnp.float32)
        parts["qk"].append(send)

    groups = min(nz + 1, GROUPS)
    cuts = [(nz + 1) * k // groups for k in range(groups + 1)]
    pieces = [prepare] + [steps_piece(a, b) for a, b in zip(cuts, cuts[1:])] + [finish]
    tasks = [item_task(k) for k in range(len(items))] + [small_task()]
    for token in schedule:
        if token < 0:
            pieces[-1 - token]()
        else:
            next(tasks[token], None)
    for copy in leaving:
        copy.wait()
    for sent in ending:
        sent()
    spread_end()


def in_turns(items, counts, n_pieces):
    early = [k for k, (_, _, (name, _)) in enumerate(items) if name[:3] != "qkv"]
    late = [k for k in range(len(counts)) if k not in early]
    tokens, piece = [], 0
    for waiting in (early, late):
        live = []
        while live or waiting:
            live, waiting = live + waiting[:3], waiting[3:]
            for k in live:
                tokens.append(k)
                if len(tokens) % PACE == 0 and piece < n_pieces:
                    piece += 1
                    tokens.append(-piece)
            live = [k for k in live if tokens.count(k) < counts[k]]
        while piece < n_pieces:
            piece += 1
            tokens.append(-piece)
    return tokens


def fits(peers, rows):
    return peers * rows <= 2048


def plan_items(width, hidden):
    half = width // 2

    def cut(name, size):
        return [(min(ITEM, size - r), (name, r)) for r in range(0, size, ITEM)]

    found = cut("down", hidden // 2)
    found += cut("up", hidden // 2)
    found += cut("proj", half)
    for j in range(3):
        found += cut(f"qkv{j}", half)
    return [(size, int(KINDS[k % len(KINDS)]), where) for k, (size, where) in enumerate(found)]


def run_backward(x, e, lengths, gain_one, qkv_weight, qkv_bias, kept, peers):
    n1_all, q, attn, da, do, n2, g, du, dx, stats, small = kept
    rows, width = x.shape
    hidden = g.shape[1]
    nz = peers // 2
    bf, f32 = jnp.bfloat16, jnp.float32
    orders = axis_orders()
    stages = 2 + len(seq_axes(peers))
    items = plan_items(width, hidden)
    used = sum(inbox_rows(size, orders[kind], name in FAR) for size, kind, (name, _) in items)
    height = sum(size for size, _, _ in items)
    turns = [1 + 2 * (2 + len(hop_groups(nz))) - (name in FAR) for _, _, (name, _) in items] + [1 + stages]
    n_pieces = 2 + min(nz + 1, GROUPS)
    schedule = SCHEDULE
    if sorted(schedule) != sorted([k for k, n in enumerate(turns) for _ in range(n)] + [-1 - k for k in range(n_pieces)]):
        schedule = in_turns(items, turns, n_pieces)
    copies = 9 * len(items) + stages + 8 + 4 + hidden // LANES // 2
    vmem = pl.BlockSpec(memory_space=pltpu.VMEM)
    smem = pl.BlockSpec(memory_space=pltpu.SMEM)
    hbm = pl.BlockSpec(memory_space=pl.ANY)
    dma = pltpu.SemaphoreType.DMA
    out = jax.ShapeDtypeStruct
    small_mesh = fits(peers, rows)
    grad = pltpu.VMEM if small_mesh else out
    stack = (HEADS // 2, 2 * rows, LANES)
    return pl.pallas_call(
        functools.partial(backward_kernel, nz, items, orders, schedule),
        out_shape=[
            grad((rows, width), bf), grad((width, 3 * width), bf), grad((width, width), bf), grad((hidden, width), bf),
            grad((hidden, width), bf), out((16, width), f32),
        ],
        in_specs=[vmem, hbm, smem, vmem, vmem]
        + [vmem if k in (2, 5, 9, 10, 11) or (small_mesh and k in KEPT) else hbm for k in range(1, 12)]
        + [hbm],
        out_specs=[vmem] + [vmem if small_mesh else hbm] * 4 + [vmem],
        scratch_shapes=[
            pltpu.VMEM(qkv_weight.shape, bf),
            pltpu.VMEM((height, width), bf),
            pltpu.VMEM((used, width), bf),
            pltpu.VMEM((height, width), bf),
            pltpu.VMEM((peers * rows, width), bf),
            pltpu.VMEM((peers, 2 * TILE, LANES), f32),
            pltpu.VMEM((2 * rows, hidden // 2), bf),
            pltpu.VMEM((2 * rows, width), bf),
            pltpu.VMEM((2 * rows, width), bf),
            pltpu.VMEM((2 * rows, hidden // 2), bf),
            pltpu.VMEM((2 * rows, width // 2), bf),
            pltpu.VMEM((2 * rows, width), bf),
            pltpu.VMEM((2 * rows, width // 2), bf),
            pltpu.VMEM((2 * rows, 3 * width), bf),
            pltpu.VMEM(stack, bf), pltpu.VMEM(stack, bf), pltpu.VMEM(stack, bf), pltpu.VMEM(stack, bf),
            pltpu.VMEM(stack, f32), pltpu.VMEM(stack, f32),
            pltpu.VMEM((2 * rows, 2 * width), bf),
            pltpu.VMEM((2 * rows, width), bf),
            pltpu.VMEM((2 * rows, 2 * rows), f32),
            pltpu.VMEM((rows, width), f32), pltpu.VMEM((rows, width), f32), pltpu.VMEM((rows, width), f32),
            pltpu.VMEM((stages, 16, width), f32),
            pltpu.VMEM((1, width), f32), pltpu.VMEM((1, 3 * width), f32),
            pltpu.VMEM((2 * rows, width), bf), pltpu.VMEM((2 * rows, hidden // 4), bf),
            pltpu.VMEM((2 * rows, width), bf), pltpu.VMEM((2 * rows, hidden // 4), bf),
            dma((nz, 2)), dma((nz, 2)), dma((nz, 2)), dma((nz, 2)),
            dma((copies,)), dma((copies,)), dma((len(items) + 10,)),
        ],
        compiler_params=pltpu.CompilerParams(collective_id=1, has_side_effects=True, vmem_limit_bytes=(K2_LIMIT if small_mesh else 62) * 2**20),
    )(x, e, lengths, gain_one, qkv_bias, n1_all, q, attn, da, do, n2, g, du, dx, stats, small, qkv_weight)


def widen_kernel(grads, small, passed, outs, rests, passed_outs, slots, sems, pass_sems):
    moved = [pltpu.make_async_copy(a, b, pass_sems.at[k]) for k, (a, b) in enumerate(zip(passed, passed_outs))]
    for copy in moved:
        copy.start()
    for k, (grad, out) in enumerate(zip(grads, outs)):
        slot = slots[k]
        turned = k == TURNED
        rows = slot.shape[2] if turned else slot.shape[1]
        flying = []
        for n in range(grad.shape[0] // rows):
            at = n % slot.shape[0]
            if len(flying) >= slot.shape[0]:
                flying[n - slot.shape[0]].wait()

            def body(i, carry, n=n, at=at, grad=grad, slot=slot, rows=rows):
                here = pl.ds(pl.multiple_of(i * TILE, TILE), TILE)
                there = pl.ds(pl.multiple_of(n * rows + i * TILE, TILE), TILE)
                slot[at, here] = grad[there].astype(jnp.float32)
                return carry

            def turn(i, carry, n=n, at=at, grad=grad, slot=slot, rows=rows):
                here = pl.ds(pl.multiple_of(i * LANES, LANES), LANES)
                there = pl.ds(pl.multiple_of(n * rows + i * LANES, LANES), LANES)
                for c in range(0, grad.shape[1], LANES):
                    slot[at, c : c + LANES, here] = grad[there, c : c + LANES].astype(jnp.float32).T
                return carry

            if turned:
                lax.fori_loop(0, rows // LANES, turn, 0)
            else:
                lax.fori_loop(0, rows // TILE, body, 0)
            into = out.at[:, n * rows : (n + 1) * rows] if turned else out.at[n * rows : (n + 1) * rows]
            copy = pltpu.make_async_copy(slot.at[at], into, sems.at[k, n % slot.shape[0]])
            copy.start()
            flying.append(copy)
        moved += flying[-slot.shape[0] :]
    for (first, count), rest in zip(SMALL_ROWS, rests):
        for k in range(count):
            rest[k * small.shape[1] : (k + 1) * small.shape[1]] = small[first + k : first + k + 1].reshape(small.shape[1])
    for copy in moved:
        copy.wait()


def widen(grads, small, passed):
    width = small.shape[1]
    depth = 4
    sizes = [(g.shape, max(TILE, WIDEN // g.shape[1] // TILE * TILE)) for g in grads]
    vmem = pl.BlockSpec(memory_space=pltpu.VMEM)
    hbm = pl.BlockSpec(memory_space=pl.ANY)
    n = len(grads)
    m = len(SMALL_ROWS)
    q = len(passed)

    def kernel(*refs):
        found = []
        for count in (n, 1, q, n, m, q, n):
            found.append(refs[:count])
            refs = refs[count:]
        found[1] = found[1][0]
        widen_kernel(*found, *refs)

    return pl.pallas_call(
        kernel,
        out_shape=[jax.ShapeDtypeStruct(g.shape[::-1] if k == TURNED else g.shape, jnp.float32) for k, g in enumerate(grads)]
        + [jax.ShapeDtypeStruct((count * width,), jnp.float32) for _, count in SMALL_ROWS]
        + [jax.ShapeDtypeStruct(p.shape, p.dtype) for p in passed],
        in_specs=[vmem] * (n + 1) + [vmem] * q,
        out_specs=[hbm] * n + [vmem] * m + [hbm] * q,
        scratch_shapes=[
            pltpu.VMEM((depth, shape[1], rows) if k == TURNED else (depth, rows, shape[1]), jnp.float32)
            for k, (shape, rows) in enumerate(sizes)
        ]
        + [pltpu.SemaphoreType.DMA((n, depth)), pltpu.SemaphoreType.DMA((q,))],
        compiler_params=pltpu.CompilerParams(vmem_limit_bytes=34 * 2**20),
    )(*grads, small, *passed)


def per_device(
    inputs,
    cotangent,
    doc_lengths,
    gain_one,
    shift_one,
    qkv_weight,
    qkv_bias,
    proj_weight,
    proj_bias,
    gain_two,
    shift_two,
    up_weight,
    up_bias,
    down_weight,
    down_bias,
):
    peers = lax.axis_size("seq")
    width = inputs.shape[2]
    layer_out, *kept = run_forward(
        inputs[0], cotangent[0], doc_lengths, gain_one, shift_one, qkv_weight, qkv_bias, proj_weight, proj_bias, gain_two, shift_two,
        up_weight, up_bias, down_weight, down_bias, peers,
    )
    input_grad, qkv, proj, up, down, small = run_backward(
        inputs[0], cotangent[0], doc_lengths, gain_one, qkv_weight, qkv_bias, kept, peers
    )
    large = (qkv, proj, up, down)
    if fits(peers, inputs.shape[1]):
        qkv, proj, up, down, *rest, layer_out, input_grad = widen(large, small, (layer_out, input_grad))
    else:
        qkv, proj, up, down = (g.astype(jnp.float32) for g in (qkv, proj, up.T, down))
        rest = [small[first : first + count].reshape(-1) for first, count in SMALL_ROWS]
    gain_1, shift_1, qkv_b, proj_b, gain_2, shift_2, up_b, down_b = rest
    return (
        layer_out[None], input_grad[None], gain_1, shift_1, qkv, qkv_b, proj, proj_b, gain_2, shift_2, up, up_b, down, down_b,
    )


def solution(mesh):
    in_specs = (
        P("batch", "seq", None),
        P("batch", "seq", None),
        P("batch", None),
        P(),
        P(),
        P(),
        P(),
        P(),
        P(),
        P(),
        P(),
        P(),
        P(),
        P(),
        P(),
    )
    out_specs = (
        P("batch", "seq", None),
        P("batch", "seq", None),
        P(),
        P(),
        P(),
        P(),
        P(),
        P(),
        P(),
        P(),
        P(),
        P(),
        P(),
        P(),
    )
    return jax.shard_map(
        per_device, mesh=mesh, in_specs=in_specs, out_specs=out_specs, check_vma=False
    )
```
